32 devices in a mesh: gx: 4 (over x, core), gy: 8 (over z, y).
Axes of the slice: x: 2, y: 2, z: 4, core: 2. Of those that a mesh axis runs over, the one named last changes fastest.
Arguments:
- density: float32 [64, 256, 128], P('gx', 'gy'), may hold values from 0.05 to 1
- potential: float32 [64, 256, 128], P('gx', 'gy'), may hold values from -14 to 25
- adjoint_start: float32 [64, 256, 128], P('gx', 'gy'), may hold values from -6 to 6
- adjoint_source: float32 [64, 256, 128], P('gx', 'gy'), may hold values from -6 to 6
- labels: int32 [64, 256, 128], P('gx', 'gy'), may hold values from 0 to 2
Outputs:
- sensitivity: float32 [64, 256, 128], P('gx', 'gy')
- mean_energy: float32 [], replicated
The draws below stay inside these ranges and needn't reach their ends.
All inputs are finite; a program needn't handle non-finite values.
Results may differ from the reference program's by a relative error of at most 0.0001.
Values sent between devices are 32-bit elements; how exact they have to be, the bound alone decides.
No kernel may reach another device: no remote copies, remote signals or barrier semaphores. Data moves between devices by JAX's collectives and lax.ppermute only.
A program may use at most 64 MiB of HBM per device.

```python
import jax
import jax.numpy as jnp

ADJ_SWEEPS = 2
FILTER_SWEEPS = 4
NX = 64
NY = 256
NZ = 128


def draw_potential(key, part):
    key = jax.random.fold_in(key, 7)
    places = jnp.arange(NX, dtype=jnp.float32) / NX
    rising = jnp.sqrt(1.0 + 2.0 * places)[:, None, None]
    base = jnp.clip(jax.random.normal(key, (NX, NY, NZ), jnp.float32), -6.0, 6.0)
    return (base * rising).astype(jnp.float32)


def place_ends(drawn, own_key, smallest, high):
    dims = drawn.shape
    index_at = [jax.random.randint(jax.random.fold_in(own_key, axis), (), 0, dims[axis]) for axis in range(len(dims))]
    drawn = drawn.at[tuple(index_at)].set(smallest)
    longest = dims.index(max(dims))
    index_at[longest] = (index_at[longest] + 1) % dims[longest]
    return drawn.at[tuple(index_at)].set(high)


def block_scale(key, extent, pieces, least, largest):
    loudness = 1.0
    for dim, parts in pieces:
        heights = jax.random.uniform(jax.random.fold_in(jax.random.fold_in(key, 6), dim), (parts,), jnp.float32, least / len(pieces), largest / len(pieces))
        loudness = loudness * jnp.repeat(jnp.exp(heights), extent[dim] // parts).reshape((-1,) + (1,) * (len(extent) - 1 - dim))
    return loudness


def bell_draw(stream_key, shape, scale, most, shards=(), kind=jnp.bfloat16):
    gain = block_scale(stream_key, shape, shards, -0.22, 0.18) if shards else 1.0
    drawn = jax.random.normal(stream_key, shape, jnp.float32) * scale * gain
    return jnp.minimum(jnp.maximum(drawn, -most), most).astype(kind)


def setup_inputs(seed: int = 0) -> dict:
    splits = jax.random.split(jax.random.key(seed), 6)
    density = jnp.clip(0.05 + 0.95 * jax.random.uniform(splits[0], (NX, NY, NZ), jnp.float32) ** block_scale(splits[0], (NX, NY, NZ), ((0, 4), (1, 8)), -0.2, 0.2), 0.05, 1.0)
    potential = draw_potential(jax.random.fold_in(splits[5], 71), 0)
    adjoint_start = bell_draw(splits[2], (NX, NY, NZ), 1.0, 6.0, ((0, 4), (1, 8)), jnp.float32)
    adjoint_source = bell_draw(splits[3], (NX, NY, NZ), 1.0, 6.0, ((0, 4), (1, 8)), jnp.float32)
    labels = place_ends(jax.random.randint(splits[4], (NX, NY, NZ), 0, 3), jax.random.fold_in(splits[4], 1), 0, 2).astype(jnp.int32)
    return {"density": density, "potential": potential, "adjoint_start": adjoint_start, "adjoint_source": adjoint_source, "labels": labels}


eps_void = 1.0
eps_solid = 12.0
eps_back = 4.0
eps_metal = 40.0
screen = 0.5
radius_sq = 2.0
epsilon_mean = 1e-6


def material(density, labels):
    design = eps_void + density ** 3 * (eps_solid - eps_void)
    return jnp.where(labels == 1, design, jnp.where(labels == 2, eps_metal, eps_back))


def neighbours(padded):
    return [padded[2:, 1:-1, 1:-1], padded[:-2, 1:-1, 1:-1],
            padded[1:-1, 2:, 1:-1], padded[1:-1, :-2, 1:-1],
            padded[1:-1, 1:-1, 2:], padded[1:-1, 1:-1, :-2]]


def reference(density, potential, adjoint_start, adjoint_source, labels):
    permit = material(density, labels)
    permit_nb = neighbours(jnp.pad(permit, 1))
    weights = [2.0 * permit * other / (permit + other) for other in permit_nb]
    total_weight = screen + weights[0] + weights[1] + weights[2] + weights[3] + weights[4] + weights[5]
    metal_mask = labels == 2
    adjoint = adjoint_start
    for repeat in range(ADJ_SWEEPS):
        beside = neighbours(jnp.pad(adjoint, 1))
        total = adjoint_source
        for weight, other in zip(weights, beside):
            total = total + weight * other
        adjoint = jnp.where(metal_mask, 0.0, total / total_weight)
    adjoint_nb = neighbours(jnp.pad(adjoint, 1))
    potential_nb = neighbours(jnp.pad(potential, 1))
    product = jnp.zeros_like(potential)
    squares = jnp.zeros_like(potential)
    for other_pot, other_adj in zip(potential_nb, adjoint_nb):
        diff = other_pot - potential
        product = product + diff * (other_adj - adjoint)
        squares = squares + diff * diff
    product = 0.5 * product
    energy = 0.5 * permit * squares
    raw = jnp.where(labels == 1, -3.0 * density ** 2 * (eps_solid - eps_void) * product, 0.0)
    mean_energy = jnp.sum(energy) / (NX * NY * NZ) + epsilon_mean
    count_cells = sum(neighbours(jnp.pad(jnp.ones_like(potential), 1)))
    filtered = raw
    for repeat in range(FILTER_SWEEPS):
        beside = sum(neighbours(jnp.pad(filtered, 1)))
        filtered = (raw + radius_sq * beside) / (1.0 + radius_sq * count_cells)
    sensitivity = jnp.where(labels == 1, filtered, 0.0) / mean_energy
    return sensitivity, mean_energy
```

```python
import jax
import jax.numpy as jnp
from jax import lax
from jax.sharding import PartitionSpec as P

ADJ_SWEEPS = 2
FILTER_SWEEPS = 4

eps_void = 1.0
eps_solid = 12.0
eps_back = 4.0
eps_metal = 40.0
screen = 0.5
radius_sq = 2.0
epsilon_mean = 1e-06


def shift_pairs(axis):
    count = lax.axis_size(axis)
    forward = [(i, i + 1) for i in range(count - 1)]
    return forward, [(b, a) for a, b in forward]


def exchange(fields, widths, axis, dim):
    forward, backward = shift_pairs(axis)

    def pack(low):
        parts = []
        for f, w in zip(fields, widths):
            n = f.shape[dim]
            s = lax.slice_in_dim(f, 0, w, axis=dim) if low else lax.slice_in_dim(f, n - w, n, axis=dim)
            parts.append(s.reshape(-1, 128))
        return jnp.concatenate(parts, 0) if len(parts) > 1 else parts[0]

    to_low, to_high = pack(True), pack(False)
    from_high = lax.ppermute(to_low, axis, backward)
    from_low = lax.ppermute(to_high, axis, forward)
    out, at = [], 0
    for f, w in zip(fields, widths):
        shape = list(f.shape)
        shape[dim] = w
        rows = shape[0] * shape[1]
        lo = from_low[at:at + rows].reshape(shape)
        hi = from_high[at:at + rows].reshape(shape)
        at += rows
        out.append(jnp.concatenate([lo, f, hi], axis=dim))
    return out


def material(density, labels):
    design = eps_void + density**3 * (eps_solid - eps_void)
    return jnp.where(labels == 1, design, jnp.where(labels == 2, eps_metal, eps_back))


def crop(f, have, want):
    d = have - want
    return f[d:f.shape[0] - d, d:f.shape[1] - d]


def beside(f):
    zpad = jnp.pad(f[1:-1, 1:-1], ((0, 0), (0, 0), (1, 1)))
    return [f[2:, 1:-1], f[:-2, 1:-1], f[1:-1, 2:], f[1:-1, :-2], zpad[:, :, 2:], zpad[:, :, :-2]]


def shards(density, potential, adjoint_start, adjoint_source, labels):
    size_x, size_y, size_z = potential.shape
    extent_x = lax.axis_size("gx") * size_x
    extent_y = lax.axis_size("gy") * size_y
    permit = material(density, labels)
    fields = [permit, adjoint_start, adjoint_source, potential]
    widths = [3, 3, 2, 1]
    fields = exchange(fields, widths, "gx", 0)
    permit3, adjoint3, source2, potential1 = exchange(fields, widths, "gy", 1)

    permit2 = crop(permit3, 3, 2)
    weights = [2.0 * permit2 * other / jnp.maximum(permit2 + other, 0.25) for other in beside(permit3)]
    total = screen + weights[0] + weights[1] + weights[2] + weights[3] + weights[4] + weights[5]
    inverse = jnp.where(permit2 > 20.0, 0.0, 1.0 / total)
    adjoint = adjoint3
    for sweep in range(ADJ_SWEEPS):
        have = 2 - sweep
        total = crop(source2, 2, have)
        for weight, other in zip(weights, beside(adjoint)):
            total = total + crop(weight, 2, have) * other
        adjoint = total * crop(inverse, 2, have)
    centre = crop(adjoint, 1, 0)
    product = jnp.zeros_like(potential)
    squares = jnp.zeros_like(potential)
    for other_pot, other_adj in zip(beside(potential1), beside(adjoint)):
        diff = other_pot - potential
        product = product + diff * (other_adj - centre)
        squares = squares + diff * diff
    energy = jnp.sum((permit * squares).reshape(-1, size_z), axis=0, keepdims=True)
    energies = lax.all_gather(energy, ("gx", "gy"), axis=0, tiled=True)
    raw = jnp.where(labels == 1, -1.5 * density**2 * (eps_solid - eps_void) * product, 0.0)

    (raw4,) = exchange([raw], [4], "gx", 0)
    (raw4,) = exchange([raw4], [4], "gy", 1)
    place_x = lax.axis_index("gx") * size_x - 3 + jnp.arange(size_x + 6, dtype=jnp.int32)
    place_y = lax.axis_index("gy") * size_y - 3 + jnp.arange(size_y + 6, dtype=jnp.int32)
    place_z = jnp.arange(size_z, dtype=jnp.int32)

    def edges(place, extent):
        return (place > 0).astype(jnp.float32) + (place < extent - 1).astype(jnp.float32)

    count = edges(place_x, extent_x)[:, None, None] + edges(place_y, extent_y)[None, :, None] + edges(place_z, size_z)[None, None, :]
    inside = ((place_x >= 0) & (place_x < extent_x))[:, None, None] & ((place_y >= 0) & (place_y < extent_y))[None, :, None]
    scale = jnp.where(inside, 1.0 / (1.0 + radius_sq * count), 0.0)
    filtered = raw4
    for sweep in range(FILTER_SWEEPS):
        have = 3 - sweep
        near = beside(filtered)
        filtered = (crop(raw4, 4, have) + radius_sq * (near[0] + near[1] + near[2] + near[3] + near[4] + near[5])) * crop(scale, 3, have)
    mean_energy = 0.5 * jnp.sum(energies) / (extent_x * extent_y * size_z) + epsilon_mean
    sensitivity = jnp.where(labels == 1, filtered, 0.0) / mean_energy
    return (sensitivity, mean_energy)


def solution(mesh):
    spec = P("gx", "gy", None)
    return jax.shard_map(shards, mesh=mesh, in_specs=(spec,) * 5, out_specs=(spec, P()), check_vma=False)
```

```python
import functools

import jax
import jax.numpy as jnp
from jax import lax
from jax.experimental import pallas as pl
from jax.experimental.pallas import tpu as pltpu
from jax.sharding import PartitionSpec as P

ADJ_SWEEPS = 2
FILTER_SWEEPS = 4

eps_void = 1.0
eps_solid = 12.0
eps_back = 4.0
eps_metal = 40.0
screen = 0.5
radius_sq = 2.0
epsilon_mean = 1e-06

WIDTHS = (ADJ_SWEEPS + 1, ADJ_SWEEPS + 1, ADJ_SWEEPS, 1)
RIM = 4
VMEM_LIMIT = 24 * 1024 * 1024


def segments(widths, size_x):
    found, at = [], 0
    for field, width in enumerate(widths):
        for x in range(-width, size_x + width):
            rows = width - max(0, -x, x - size_x + 1)
            if rows > 0:
                found.append((field, x, rows, at))
                at += rows
    return found, -(-at // 8) * 8


def plane_starts(widths):
    starts, at = [], 0
    for width in widths:
        starts.append(at)
        at += width
    return starts, at


def material(density, labels):
    design = eps_void + density * density * density * (eps_solid - eps_void)
    return jnp.where(labels == 1, design, jnp.where(labels == 2, eps_metal, eps_back))


def call(body, outs, scratch=(), in_specs=None, cost=10000):
    kwargs = {} if in_specs is None else {"in_specs": in_specs, "grid": (1,)}
    return pl.pallas_call(
        body,
        out_shape=outs,
        scratch_shapes=list(scratch),
        compiler_params=pltpu.CompilerParams(vmem_limit_bytes=VMEM_LIMIT),
        cost_estimate=pl.CostEstimate(flops=cost, bytes_accessed=cost, transcendentals=0),
        **kwargs,
    )


def f32(*shape):
    return jax.ShapeDtypeStruct(shape, jnp.float32)


def pack_x(density, labels, adjoint, source, potential, low_out, high_out):
    size_x = density.shape[0]
    starts, _ = plane_starts(WIDTHS)
    for out, low in ((low_out, True), (high_out, False)):
        for field, width in enumerate(WIDTHS):
            span = pl.ds(0 if low else size_x - width, width)
            if field == 0:
                face = material(density[span], labels[span])
            else:
                face = (adjoint, source, potential)[field - 1][span]
            out[pl.ds(starts[field], width)] = face


def pack_y(size_x, from_low, from_high, density_l, labels_l, adjoint_l, source_l, potential_l,
           density_h, labels_h, adjoint_h, source_h, potential_h, low_out, high_out):
    starts, _ = plane_starts(WIDTHS)
    found, _ = segments(WIDTHS, size_x)
    size_y = from_low.shape[1]
    sides = (
        (low_out, (density_l, labels_l, adjoint_l, source_l, potential_l), True),
        (high_out, (density_h, labels_h, adjoint_h, source_h, potential_h), False),
    )
    for out, (density, labels, adjoint, source, potential), low in sides:
        for field, x, rows, at in found:
            own = slice(0, rows) if low else slice(8 - rows, 8)
            rim = slice(0, rows) if low else slice(size_y - rows, size_y)
            if x < 0:
                face = from_low[starts[field] + WIDTHS[field] + x, rim]
            elif x >= size_x:
                face = from_high[starts[field] + x - size_x, rim]
            elif field == 0:
                face = material(density[x, own], labels[x, own])
            else:
                face = (adjoint, source, potential)[field - 1][x, own]
            out[at:at + rows] = face


def shift(value, by, axis):
    return pltpu.roll(value, by % value.shape[axis], axis)


def adjoint_part(xlow, xhigh, ylow, yhigh, density, labels, adjoint_start, adjoint_source, potential,
                 raw_out, low_out, high_out, energy_out,
                 permit, start, source, poten, face_x, face_y, face_z, inverse, first, second):
    size_x, size_y, size_z = density.shape
    starts, _ = plane_starts(WIDTHS)
    found, _ = segments(WIDTHS, size_x)
    fields = (permit, start, source, poten)
    body = pl.ds(RIM, size_y)

    def fill(x, carry):
        permit[x + WIDTHS[0], body] = material(density[x], labels[x])
        start[x + WIDTHS[1], body] = adjoint_start[x]
        source[x + WIDTHS[2], body] = adjoint_source[x]
        poten[x + WIDTHS[3], body] = potential[x]
        return carry

    lax.fori_loop(0, size_x, fill, 0)
    for field, width in enumerate(WIDTHS):
        for k in range(width):
            fields[field][k, body] = xlow[starts[field] + k]
            fields[field][width + size_x + k, body] = xhigh[starts[field] + k]
    for field, x, rows, at in found:
        fields[field][x + WIDTHS[field], RIM - rows:RIM] = ylow[at:at + rows]
        fields[field][x + WIDTHS[field], RIM + size_y:RIM + size_y + rows] = yhigh[at:at + rows]

    wide = size_y + 2 * RIM
    lane = lax.broadcasted_iota(jnp.int32, (wide, size_z), 1)
    is_first = lane == 0
    is_last = lane == size_z - 1

    def harmonic(a, b):
        return 2.0 * a * b / jnp.maximum(a + b, 0.25)

    def faces_x(x, carry):
        face_x[x] = harmonic(permit[x], permit[x + 1])
        return carry

    lax.fori_loop(0, size_x + 5, faces_x, 0)

    def weigh(x, carry):
        p = permit[x + 1]
        fy = harmonic(p, shift(p, -1, 0))
        fz = jnp.where(is_last, 0.0, harmonic(p, shift(p, -1, 1)))
        face_y[x] = fy
        face_z[x] = fz
        total = screen + face_x[x] + face_x[x + 1] + fy + shift(fy, 1, 0) + fz + shift(fz, 1, 1)
        inverse[x] = jnp.where(p > 20.0, 0.0, 1.0 / total)
        return carry

    lax.fori_loop(0, size_x + 4, weigh, 0)

    def relax(x, a, a_low, a_high):
        fy, fz = face_y[x], face_z[x]
        total = source[x] + face_x[x + 1] * a_high + face_x[x] * a_low
        total = total + fy * shift(a, -1, 0) + shift(fy * a, 1, 0)
        total = total + fz * shift(a, -1, 1) + shift(fz * a, 1, 1)
        return total * inverse[x]

    def sweep_one(x, carry):
        first[x] = relax(x, start[x + 1], start[x], start[x + 2])
        return carry

    lax.fori_loop(0, size_x + 4, sweep_one, 0)

    def sweep_two(x, carry):
        second[x] = relax(x + 1, first[x + 1], first[x], first[x + 2])
        return carry

    lax.fori_loop(0, size_x + 2, sweep_two, 0)

    row = lax.broadcasted_iota(jnp.int32, (wide, size_z), 0)
    own = (row >= RIM) & (row < RIM + size_y)

    def finish(x, carry):
        v, a = poten[x + 1], second[x + 1]
        product = jnp.zeros_like(v)
        squares = jnp.zeros_like(v)
        for k in (0, 2):
            dv, da = poten[x + k] - v, second[x + k] - a
            product = product + dv * da
            squares = squares + dv * dv
        dv, da = shift(v, -1, 0) - v, shift(a, -1, 0) - a
        both, square = dv * da, dv * dv
        product = product + both + shift(both, 1, 0)
        squares = squares + square + shift(square, 1, 0)
        dv = jnp.where(is_last, 0.0, shift(v, -1, 1)) - v
        da = jnp.where(is_last, 0.0, shift(a, -1, 1)) - a
        both, square = dv * da, dv * dv
        product = product + both + jnp.where(is_first, v * a, shift(both, 1, 1))
        squares = squares + square + jnp.where(is_first, v * v, shift(square, 1, 1))
        energy = jnp.where(own, permit[x + 3] * squares, 0.0)
        d = density[x]
        gain = jnp.where(labels[x] == 1, -1.5 * (eps_solid - eps_void) * d * d, 0.0)
        raw_out[x] = gain * product[RIM:RIM + size_y]
        for k in range(wide // 8):
            carry = carry + energy[8 * k:8 * k + 8]
        return carry

    energy_out[...] = lax.fori_loop(0, size_x, finish, jnp.zeros((8, size_z), jnp.float32))
    low_out[...] = raw_out[pl.ds(0, FILTER_SWEEPS)]
    high_out[...] = raw_out[pl.ds(size_x - FILTER_SWEEPS, FILTER_SWEEPS)]


def pack_raw_y(from_low, from_high, raw, low_out, high_out):
    size_x, size_y, _ = raw.shape
    found, _ = segments((FILTER_SWEEPS,), size_x)
    for out, low in ((low_out, True), (high_out, False)):
        for _, x, rows, at in found:
            rim = slice(0, rows) if low else slice(size_y - rows, size_y)
            if x < 0:
                face = from_low[FILTER_SWEEPS + x, rim]
            elif x >= size_x:
                face = from_high[x - size_x, rim]
            else:
                face = raw[x, rim]
            out[at:at + rows] = face


def filter_part(xlow, xhigh, ylow, yhigh, raw_in, labels, out, raw, even, odd):
    size_x, size_y, size_z = raw_in.shape
    width = FILTER_SWEEPS
    found, _ = segments((width,), size_x)
    body = pl.ds(RIM, size_y)

    def fill(x, carry):
        raw[x + width, body] = raw_in[x]
        return carry

    lax.fori_loop(0, size_x, fill, 0)
    for k in range(width):
        raw[k, body] = xlow[k]
        raw[width + size_x + k, body] = xhigh[k]
    for _, x, rows, at in found:
        raw[x + width, RIM - rows:RIM] = ylow[at:at + rows]
        raw[x + width, RIM + size_y:RIM + size_y + rows] = yhigh[at:at + rows]

    wide = size_y + 2 * RIM
    extent_x = lax.axis_size("gx") * size_x
    extent_y = lax.axis_size("gy") * size_y
    base_x = lax.axis_index("gx") * size_x - width
    lane = lax.broadcasted_iota(jnp.int32, (wide, size_z), 1)
    place = lax.broadcasted_iota(jnp.int32, (wide, size_z), 0) + (lax.axis_index("gy") * size_y - RIM)
    is_first, is_last = lane == 0, lane == size_z - 1

    def edges(at, extent):
        return jnp.where(at > 0, 1.0, 0.0) + jnp.where(at < extent - 1, 1.0, 0.0)

    count = edges(place, extent_y) + edges(lane, size_z)
    inside = (place >= 0) & (place < extent_y)
    scale_two = jnp.where(inside, 1.0 / (1.0 + radius_sq * (count + 2.0)), 0.0)
    scale_one = jnp.where(inside, 1.0 / (1.0 + radius_sq * (count + 1.0)), 0.0)

    def relax(src, x):
        f = src[x]
        near = src[x - 1] + src[x + 1] + shift(f, 1, 0) + shift(f, -1, 0)
        near = near + jnp.where(is_first, 0.0, shift(f, 1, 1)) + jnp.where(is_last, 0.0, shift(f, -1, 1))
        at = base_x + x
        outside = (at < 0) | (at >= extent_x)
        border = (at == 0) | (at == extent_x - 1)
        scale = jnp.where(outside, 0.0, jnp.where(border, scale_one, scale_two))
        return (raw[x] + radius_sq * near) * scale

    src = raw
    for sweep in range(FILTER_SWEEPS - 1):
        dst = (even, odd)[sweep % 2]

        def step(x, carry, src=src, dst=dst):
            dst[x] = relax(src, x)
            return carry

        lax.fori_loop(sweep + 1, size_x + 2 * width - sweep - 1, step, 0)
        src = dst

    def last(x, carry):
        f = relax(src, x + width)
        out[x] = jnp.where(labels[x] == 1, f[RIM:RIM + size_y], 0.0)
        return carry

    lax.fori_loop(0, size_x, last, 0)


def rescale(voxels, filtered, mine, other, out, mean_out):
    total = jnp.sum(mine[...] + other[...])
    mean = 0.5 * total / voxels + epsilon_mean
    mean_out[0, 0] = mean
    out[...] = filtered[...] * (1.0 / jnp.full((1, 1, out.shape[2]), mean, jnp.float32))


def both_ways(low, high, axis):
    count = lax.axis_size(axis)
    forward = [(i, i + 1) for i in range(count - 1)]
    backward = [(b, a) for a, b in forward]
    from_high = lax.ppermute(low, axis, backward)
    from_low = lax.ppermute(high, axis, forward)
    return from_low, from_high


def partner(value, axis, bit):
    return lax.ppermute(value, axis, [(i, i ^ bit) for i in range(lax.axis_size(axis))])


def shards(density, potential, adjoint_start, adjoint_source, labels):
    size_x, size_y, size_z = potential.shape
    _, planes = plane_starts(WIDTHS)
    _, rows = segments(WIDTHS, size_x)
    own = (density, labels, adjoint_start, adjoint_source, potential)

    low, high = call(pack_x, (f32(planes, size_y, size_z),) * 2)(*own)
    xlow, xhigh = both_ways(low, high, "gx")
    top, end = (0, 0, 0), (0, size_y // 8 - 1, 0)
    whole = pl.BlockSpec((planes, size_y, size_z), lambda i: (0, 0, 0))
    low_spec = pl.BlockSpec((size_x, 8, size_z), lambda i: top)
    high_spec = pl.BlockSpec((size_x, 8, size_z), lambda i: end)
    low, high = call(
        functools.partial(pack_y, size_x),
        (f32(rows, size_z),) * 2,
        in_specs=[whole] * 2 + [low_spec] * 5 + [high_spec] * 5,
    )(xlow, xhigh, *own, *own)
    ylow, yhigh = both_ways(low, high, "gy")

    wide = size_y + 2 * RIM

    def room(extra):
        return pltpu.VMEM((size_x + extra, wide, size_z), jnp.float32)

    face = f32(FILTER_SWEEPS, size_y, size_z)
    raw, low, high, energy = call(
        adjoint_part,
        (f32(size_x, size_y, size_z), face, face, f32(8, size_z)),
        [room(6), room(6), room(4), room(2), room(5), room(4), room(4), room(4), room(4), room(2)],
    )(xlow, xhigh, ylow, yhigh, *own)

    xlow, xhigh = both_ways(low, high, "gx")
    stages = [("gx", 1 << k) for k in range((lax.axis_size("gx") - 1).bit_length())]
    stages += [("gy", 1 << k) for k in range((lax.axis_size("gy") - 1).bit_length())]
    other = partner(energy, *stages[0])
    _, rows = segments((FILTER_SWEEPS,), size_x)
    low, high = call(pack_raw_y, (f32(rows, size_z),) * 2)(xlow, xhigh, raw)
    ylow, yhigh = both_ways(low, high, "gy")
    for stage in stages[1:]:
        energy = energy + other
        other = partner(energy, *stage)
    filtered = call(
        filter_part,
        f32(size_x, size_y, size_z),
        [room(2 * FILTER_SWEEPS)] * 3,
    )(xlow, xhigh, ylow, yhigh, raw, labels)
    voxels = lax.axis_size("gx") * size_x * lax.axis_size("gy") * size_y * size_z
    sensitivity, mean_energy = pl.pallas_call(
        functools.partial(rescale, float(voxels)),
        out_shape=(f32(size_x, size_y, size_z), f32(1, 1)),
        out_specs=(pl.BlockSpec(memory_space=pltpu.VMEM), pl.BlockSpec(memory_space=pltpu.SMEM)),
        compiler_params=pltpu.CompilerParams(vmem_limit_bytes=VMEM_LIMIT),
    )(filtered, energy, other)
    return (sensitivity, mean_energy[0, 0])


def solution(mesh):
    spec = P("gx", "gy", None)
    return jax.shard_map(
        shards, mesh=mesh, in_specs=(spec,) * 5, out_specs=(spec, P()), check_vma=False
    )
```

```python
import functools

import jax
import jax.numpy as jnp
from jax import lax
from jax.experimental import pallas as pl
from jax.experimental.pallas import tpu as pltpu
from jax.sharding import PartitionSpec as P

ADJ_SWEEPS = 2
FILTER_SWEEPS = 4

eps_void = 1.0
eps_solid = 12.0
eps_back = 4.0
eps_metal = 40.0
screen = 0.5
radius_sq = 2.0
epsilon_mean = 1e-06

WIDTHS = (ADJ_SWEEPS + 1, ADJ_SWEEPS + 1, ADJ_SWEEPS, 1)
RIM = 4
VMEM_LIMIT = 24 * 1024 * 1024


def segments(widths, size_x):
    found, at = [], 0
    for field, width in enumerate(widths):
        for x in range(-width, size_x + width):
            rows = width - max(0, -x, x - size_x + 1)
            if rows > 0:
                found.append((field, x, rows, at))
                at += rows
    return found, -(-at // 8) * 8


def plane_starts(widths):
    starts, at = [], 0
    for width in widths:
        starts.append(at)
        at += width
    return starts, at


def material(density, labels):
    design = eps_void + density * density * density * (eps_solid - eps_void)
    return jnp.where(labels == 1, design, jnp.where(labels == 2, eps_metal, eps_back))


def call(body, outs, scratch=(), in_specs=None, cost=10000):
    kwargs = {} if in_specs is None else {"in_specs": in_specs, "grid": (1,)}
    return pl.pallas_call(
        body,
        out_shape=outs,
        scratch_shapes=list(scratch),
        compiler_params=pltpu.CompilerParams(vmem_limit_bytes=VMEM_LIMIT),
        cost_estimate=pl.CostEstimate(flops=cost, bytes_accessed=cost, transcendentals=0),
        **kwargs,
    )


def f32(*shape):
    return jax.ShapeDtypeStruct(shape, jnp.float32)


def pack_x(density, labels, adjoint, source, potential, low_out, high_out, dense, label, sem):
    size_x = density.shape[0]
    starts, _ = plane_starts(WIDTHS)
    width = WIDTHS[0]
    copies = []
    for side, out in enumerate((low_out, high_out)):
        def face(k):
            return pl.ds(0 if side == 0 else size_x - k, k)

        copies.append((density.at[face(width)], dense.at[side]))
        copies.append((labels.at[face(width)], label.at[side]))
        for array, start, count in zip((adjoint, source, potential), starts[1:], WIDTHS[1:]):
            copies.append((array.at[face(count)], out.at[pl.ds(start, count)]))
    copies = [pltpu.make_async_copy(a, b, sem.at[k]) for k, (a, b) in enumerate(copies)]
    for copy in copies:
        copy.start()
    for copy in copies:
        copy.wait()
    low_out[pl.ds(0, width)] = material(dense[0], label[0])
    high_out[pl.ds(0, width)] = material(dense[1], label[1])


def pack_y(size_x, from_low, from_high, density_l, labels_l, adjoint_l, source_l, potential_l,
           density_h, labels_h, adjoint_h, source_h, potential_h, low_out, high_out):
    starts, _ = plane_starts(WIDTHS)
    found, _ = segments(WIDTHS, size_x)
    size_y = from_low.shape[1]
    sides = (
        (low_out, (density_l, labels_l, adjoint_l, source_l, potential_l), True),
        (high_out, (density_h, labels_h, adjoint_h, source_h, potential_h), False),
    )
    for out, (density, labels, adjoint, source, potential), low in sides:
        for field, x, rows, at in found:
            own = slice(0, rows) if low else slice(8 - rows, 8)
            rim = slice(0, rows) if low else slice(size_y - rows, size_y)
            if x < 0:
                face = from_low[starts[field] + WIDTHS[field] + x, rim]
            elif x >= size_x:
                face = from_high[starts[field] + x - size_x, rim]
            elif field == 0:
                face = material(density[x, own], labels[x, own])
            else:
                face = (adjoint, source, potential)[field - 1][x, own]
            out[at:at + rows] = face


def shift(value, by, axis):
    return pltpu.roll(value, by % value.shape[axis], axis)


def planes_loop(low, high, block, step):
    count = high - low
    block = max(k for k in range(1, block + 1) if count % k == 0)

    def body(k, carry):
        step(low + k * block, block)
        return carry

    lax.fori_loop(0, count // block, body, 0)


def unpack_rows(fields, widths, low, high, size_x, size_y):
    found, _ = segments(widths, size_x)
    wide = size_y + 2 * RIM
    for field, x, rows, at in found:
        fields[field][x + widths[field], wide - rows:wide] = low[at:at + rows]
        fields[field][x + widths[field], size_y:size_y + rows] = high[at:at + rows]


def adjoint_part(xlow, xhigh, ylow, yhigh, density, labels, adjoint_start, adjoint_source, potential,
                 raw_out, low_out, high_out, energy_out,
                 permit, start, source, poten, face_x, face_y, face_z, inverse, first, second):
    size_x, size_y, size_z = density.shape
    starts, _ = plane_starts(WIDTHS)
    fields = (permit, start, source, poten)
    tile = pl.ds(0, size_y)

    def fill(x, n):
        span = pl.ds(x, n)
        permit[pl.ds(x + WIDTHS[0], n), tile] = material(density[span], labels[span])
        start[pl.ds(x + WIDTHS[1], n), tile] = adjoint_start[span]
        source[pl.ds(x + WIDTHS[2], n), tile] = adjoint_source[span]
        poten[pl.ds(x + WIDTHS[3], n), tile] = potential[span]

    planes_loop(0, size_x, 4, fill)
    for field, width in enumerate(WIDTHS):
        fields[field][pl.ds(0, width), tile] = xlow[pl.ds(starts[field], width)]
        fields[field][pl.ds(width + size_x, width), tile] = xhigh[pl.ds(starts[field], width)]
    unpack_rows(fields, WIDTHS, ylow, yhigh, size_x, size_y)

    wide = size_y + 2 * RIM
    lane = lax.broadcasted_iota(jnp.int32, (1, wide, size_z), 2)
    is_first = lane == 0
    is_last = lane == size_z - 1

    def harmonic(a, b):
        return 2.0 * a * b / jnp.maximum(a + b, 0.25)

    def faces_x(x, n):
        face_x[pl.ds(x, n)] = harmonic(permit[pl.ds(x, n)], permit[pl.ds(x + 1, n)])

    planes_loop(0, size_x + 5, 4, faces_x)

    def weigh(x, n):
        span = pl.ds(x, n)
        p = permit[pl.ds(x + 1, n)]
        fy = harmonic(p, shift(p, -1, 1))
        fz = jnp.where(is_last, 0.0, harmonic(p, shift(p, -1, 2)))
        face_y[span] = fy
        face_z[span] = fz
        total = screen + face_x[span] + face_x[pl.ds(x + 1, n)] + fy + shift(fy, 1, 1) + fz + shift(fz, 1, 2)
        inverse[span] = jnp.where(p > 20.0, 0.0, 1.0 / total)

    planes_loop(0, size_x + 4, 4, weigh)

    def relax(x, n, a, a_low, a_high):
        span = pl.ds(x, n)
        fy, fz = face_y[span], face_z[span]
        total = source[span] + face_x[pl.ds(x + 1, n)] * a_high + face_x[span] * a_low
        total = total + fy * shift(a, -1, 1) + shift(fy * a, 1, 1)
        total = total + fz * shift(a, -1, 2) + shift(fz * a, 1, 2)
        return total * inverse[span]

    def sweep_one(x, n):
        first[pl.ds(x, n)] = relax(x, n, start[pl.ds(x + 1, n)], start[pl.ds(x, n)], start[pl.ds(x + 2, n)])

    planes_loop(0, size_x + 4, 4, sweep_one)

    def sweep_two(x, n):
        second[pl.ds(x, n)] = relax(x + 1, n, first[pl.ds(x + 1, n)], first[pl.ds(x, n)], first[pl.ds(x + 2, n)])

    planes_loop(0, size_x + 2, 4, sweep_two)
    energy_out[...] = jnp.zeros_like(energy_out)

    def finish(x, n):
        span = pl.ds(x, n)
        v, a = poten[pl.ds(x + 1, n)], second[pl.ds(x + 1, n)]
        product = jnp.zeros_like(v)
        squares = jnp.zeros_like(v)
        for k in (0, 2):
            dv, da = poten[pl.ds(x + k, n)] - v, second[pl.ds(x + k, n)] - a
            product = product + dv * da
            squares = squares + dv * dv
        dv, da = shift(v, -1, 1) - v, shift(a, -1, 1) - a
        both, square = dv * da, dv * dv
        product = product + both + shift(both, 1, 1)
        squares = squares + square + shift(square, 1, 1)
        dv = jnp.where(is_last, 0.0, shift(v, -1, 2)) - v
        da = jnp.where(is_last, 0.0, shift(a, -1, 2)) - a
        both, square = dv * da, dv * dv
        product = product + both + jnp.where(is_first, v * a, shift(both, 1, 2))
        squares = squares + square + jnp.where(is_first, v * v, shift(square, 1, 2))
        energy = (permit[pl.ds(x + 3, n)] * squares)[:, :size_y]
        d = density[span]
        gain = jnp.where(labels[span] == 1, -1.5 * (eps_solid - eps_void) * d * d, 0.0)
        raw_out[span] = gain * product[:, :size_y]
        energy_out[...] += jnp.sum(energy.reshape(-1, 8, size_z), axis=0)

    planes_loop(0, size_x, 4, finish)
    low_out[...] = raw_out[pl.ds(0, FILTER_SWEEPS)]
    high_out[...] = raw_out[pl.ds(size_x - FILTER_SWEEPS, FILTER_SWEEPS)]


def pack_raw_y(from_low, from_high, raw, low_out, high_out):
    size_x, size_y, _ = raw.shape
    found, _ = segments((FILTER_SWEEPS,), size_x)
    for out, low in ((low_out, True), (high_out, False)):
        for _, x, rows, at in found:
            rim = slice(0, rows) if low else slice(size_y - rows, size_y)
            if x < 0:
                face = from_low[FILTER_SWEEPS + x, rim]
            elif x >= size_x:
                face = from_high[x - size_x, rim]
            else:
                face = raw[x, rim]
            out[at:at + rows] = face


def filter_part(xlow, xhigh, ylow, yhigh, raw_in, labels, out, raw, even, odd):
    size_x, size_y, size_z = raw_in.shape
    width = FILTER_SWEEPS
    tile = pl.ds(0, size_y)

    def fill(x, n):
        raw[pl.ds(x + width, n), tile] = raw_in[pl.ds(x, n)]

    planes_loop(0, size_x, 4, fill)
    raw[pl.ds(0, width), tile] = xlow[...]
    raw[pl.ds(width + size_x, width), tile] = xhigh[...]
    unpack_rows((raw,), (width,), ylow, yhigh, size_x, size_y)

    wide = size_y + 2 * RIM
    extent_x = lax.axis_size("gx") * size_x
    extent_y = lax.axis_size("gy") * size_y
    base_x = lax.axis_index("gx") * size_x - width
    lane = lax.broadcasted_iota(jnp.int32, (1, wide, size_z), 2)
    row = lax.broadcasted_iota(jnp.int32, (1, wide, size_z), 1)
    place = lax.axis_index("gy") * size_y + jnp.where(row < size_y + RIM, row, row - wide)
    is_first, is_last = lane == 0, lane == size_z - 1

    def edges(at, extent):
        return jnp.where(at > 0, 1.0, 0.0) + jnp.where(at < extent - 1, 1.0, 0.0)

    count = edges(place, extent_y) + edges(lane, size_z)
    inside = (place >= 0) & (place < extent_y)
    scale_two = jnp.where(inside, 1.0 / (1.0 + radius_sq * (count + 2.0)), 0.0)
    scale_one = jnp.where(inside, 1.0 / (1.0 + radius_sq * (count + 1.0)), 0.0)

    def relax(src, x, n):
        f = src[pl.ds(x, n)]
        near = src[pl.ds(x - 1, n)] + src[pl.ds(x + 1, n)] + shift(f, 1, 1) + shift(f, -1, 1)
        near = near + jnp.where(is_first, 0.0, shift(f, 1, 2)) + jnp.where(is_last, 0.0, shift(f, -1, 2))
        total = raw[pl.ds(x, n)] + radius_sq * near
        scaled = []
        for k in range(n):
            at = base_x + x + k
            outside = (at < 0) | (at >= extent_x)
            border = (at == 0) | (at == extent_x - 1)
            scale = jnp.where(outside, 0.0, jnp.where(border, scale_one, scale_two))
            scaled.append(total[k:k + 1] * scale)
        return jnp.concatenate(scaled, axis=0)

    src = raw
    for sweep in range(FILTER_SWEEPS - 1):
        dst = (even, odd)[sweep % 2]

        def step(x, n, src=src, dst=dst):
            dst[pl.ds(x, n)] = relax(src, x, n)

        planes_loop(sweep + 1, size_x + 2 * width - sweep - 1, 4, step)
        src = dst

    def last(x, n):
        f = relax(src, x + width, n)
        out[pl.ds(x, n)] = jnp.where(labels[pl.ds(x, n)] == 1, f[:, :size_y], 0.0)

    planes_loop(0, size_x, 4, last)


def rescale(voxels, filtered, mine, other, out, mean_out):
    total = jnp.sum(mine[...] + other[...])
    mean = 0.5 * total / voxels + epsilon_mean
    mean_out[0, 0] = mean
    out[...] = filtered[...] * (1.0 / jnp.full((1, 1, out.shape[2]), mean, jnp.float32))


def both_ways(low, high, axis):
    count = lax.axis_size(axis)
    forward = [(i, i + 1) for i in range(count - 1)]
    backward = [(b, a) for a, b in forward]
    from_high = lax.ppermute(low, axis, backward)
    from_low = lax.ppermute(high, axis, forward)
    return from_low, from_high


def partner(value, axis, bit):
    return lax.ppermute(value, axis, [(i, i ^ bit) for i in range(lax.axis_size(axis))])


def shards(density, potential, adjoint_start, adjoint_source, labels):
    size_x, size_y, size_z = potential.shape
    _, planes = plane_starts(WIDTHS)
    _, rows = segments(WIDTHS, size_x)
    own = (density, labels, adjoint_start, adjoint_source, potential)

    depth = (2, WIDTHS[0], size_y, size_z)
    low, high = pl.pallas_call(
        pack_x,
        out_shape=(f32(planes, size_y, size_z),) * 2,
        in_specs=[pl.BlockSpec(memory_space=pltpu.HBM)] * 5,
        scratch_shapes=[
            pltpu.VMEM(depth, jnp.float32),
            pltpu.VMEM(depth, jnp.int32),
            pltpu.SemaphoreType.DMA((10,)),
        ],
        compiler_params=pltpu.CompilerParams(vmem_limit_bytes=VMEM_LIMIT),
    )(*own)
    xlow, xhigh = both_ways(low, high, "gx")
    top, end = (0, 0, 0), (0, size_y // 8 - 1, 0)
    whole = pl.BlockSpec((planes, size_y, size_z), lambda i: (0, 0, 0))
    low_spec = pl.BlockSpec((size_x, 8, size_z), lambda i: top)
    high_spec = pl.BlockSpec((size_x, 8, size_z), lambda i: end)
    low, high = call(
        functools.partial(pack_y, size_x),
        (f32(rows, size_z),) * 2,
        in_specs=[whole] * 2 + [low_spec] * 5 + [high_spec] * 5,
    )(xlow, xhigh, *own, *own)
    ylow, yhigh = both_ways(low, high, "gy")

    wide = size_y + 2 * RIM

    def room(extra):
        return pltpu.VMEM((size_x + extra, wide, size_z), jnp.float32)

    face = f32(FILTER_SWEEPS, size_y, size_z)
    raw, low, high, energy = call(
        adjoint_part,
        (f32(size_x, size_y, size_z), face, face, f32(8, size_z)),
        [room(6), room(6), room(4), room(2), room(5), room(4), room(4), room(4), room(4), room(2)],
    )(xlow, xhigh, ylow, yhigh, *own)

    xlow, xhigh = both_ways(low, high, "gx")
    stages = [("gx", 1 << k) for k in range((lax.axis_size("gx") - 1).bit_length())]
    stages += [("gy", 1 << k) for k in range((lax.axis_size("gy") - 1).bit_length())]
    other = partner(energy, *stages[0])
    _, rows = segments((FILTER_SWEEPS,), size_x)
    low, high = call(pack_raw_y, (f32(rows, size_z),) * 2)(xlow, xhigh, raw)
    ylow, yhigh = both_ways(low, high, "gy")
    for stage in stages[1:]:
        energy = energy + other
        other = partner(energy, *stage)
    filtered = call(
        filter_part,
        f32(size_x, size_y, size_z),
        [room(2 * FILTER_SWEEPS)] * 3,
    )(xlow, xhigh, ylow, yhigh, raw, labels)
    voxels = lax.axis_size("gx") * size_x * lax.axis_size("gy") * size_y * size_z
    sensitivity, mean_energy = pl.pallas_call(
        functools.partial(rescale, float(voxels)),
        out_shape=(f32(size_x, size_y, size_z), f32(1, 1)),
        out_specs=(pl.BlockSpec(memory_space=pltpu.VMEM), pl.BlockSpec(memory_space=pltpu.SMEM)),
        compiler_params=pltpu.CompilerParams(vmem_limit_bytes=VMEM_LIMIT),
    )(filtered, energy, other)
    return (sensitivity, mean_energy[0, 0])


def solution(mesh):
    spec = P("gx", "gy", None)
    return jax.shard_map(
        shards, mesh=mesh, in_specs=(spec,) * 5, out_specs=(spec, P()), check_vma=False
    )
```

```python
import functools

import jax
import jax.numpy as jnp
from jax import lax
from jax.experimental import pallas as pl
from jax.experimental.pallas import tpu as pltpu
from jax.sharding import PartitionSpec as P

ADJ_SWEEPS = 2
FILTER_SWEEPS = 4

eps_void = 1.0
eps_solid = 12.0
eps_back = 4.0
eps_metal = 40.0
screen = 0.5
radius_sq = 2.0
epsilon_mean = 1e-06

WIDTHS = (ADJ_SWEEPS + 1, ADJ_SWEEPS + 1, ADJ_SWEEPS, 1)
RIM = 4
VMEM_LIMIT = 24 * 1024 * 1024


def segments(widths, size_x):
    found, at = [], 0
    for field, width in enumerate(widths):
        for x in range(-width, size_x + width):
            rows = width - max(0, -x, x - size_x + 1)
            if rows > 0:
                found.append((field, x, rows, at))
                at += rows
    return found, -(-at // 8) * 8


def plane_starts(widths):
    starts, at = [], 0
    for width in widths:
        starts.append(at)
        at += width
    return starts, at


def material(density, labels):
    design = eps_void + density * density * density * (eps_solid - eps_void)
    return jnp.where(labels == 1, design, jnp.where(labels == 2, eps_metal, eps_back))


def call(body, outs, scratch=(), in_specs=None, cost=10000):
    kwargs = {} if in_specs is None else {"in_specs": in_specs, "grid": (1,)}
    return pl.pallas_call(
        body,
        out_shape=outs,
        scratch_shapes=list(scratch),
        compiler_params=pltpu.CompilerParams(vmem_limit_bytes=VMEM_LIMIT),
        cost_estimate=pl.CostEstimate(flops=cost, bytes_accessed=cost, transcendentals=0),
        **kwargs,
    )


def f32(*shape):
    return jax.ShapeDtypeStruct(shape, jnp.float32)


def odd_place(axis):
    return lax.rem(lax.axis_index(axis), 2) == 1


def pack_x(*refs):
    inputs, (even_out, odd_out), held, (sem,) = refs[:5], refs[5:7], refs[7:12], refs[12:]
    density, labels, adjoint, source, potential = held
    size_x = density.shape[0]
    starts, _ = plane_starts(WIDTHS)
    copies = [pltpu.make_async_copy(a, b, sem.at[k]) for k, (a, b) in enumerate(zip(inputs, held))]
    for copy in copies:
        copy.start()
    for copy in copies:
        copy.wait()
    low_first = odd_place("gx")
    for out, low in ((even_out, low_first), (odd_out, jnp.logical_not(low_first))):
        for field, width in enumerate(WIDTHS):
            span = pl.ds(jnp.where(low, 0, size_x - width), width)
            if field == 0:
                face = material(density[span], labels[span])
            else:
                face = (adjoint, source, potential)[field - 1][span]
            out[pl.ds(starts[field], width)] = face


def pack_y(x_even, x_odd, density, labels, adjoint, source, potential, even_out, odd_out):
    size_x, size_y, _ = density.shape
    starts, _ = plane_starts(WIDTHS)
    found, _ = segments(WIDTHS, size_x)
    x_swap, y_swap = odd_place("gx"), odd_place("gy")
    for field, x, rows, at in found:
        faces = []
        for rim in (slice(0, rows), slice(size_y - rows, size_y)):
            if x < 0:
                plane = starts[field] + WIDTHS[field] + x
                face = jnp.where(x_swap, x_even[plane, rim], x_odd[plane, rim])
            elif x >= size_x:
                plane = starts[field] + x - size_x
                face = jnp.where(x_swap, x_odd[plane, rim], x_even[plane, rim])
            elif field == 0:
                face = material(density[x, rim], labels[x, rim])
            else:
                face = (adjoint, source, potential)[field - 1][x, rim]
            faces.append(face)
        low, high = faces
        even_out[at:at + rows] = jnp.where(y_swap, low, high)
        odd_out[at:at + rows] = jnp.where(y_swap, high, low)


def shift(value, by, axis):
    return pltpu.roll(value, by % value.shape[axis], axis)


def planes_loop(low, high, block, step):
    count = high - low
    block = max(k for k in range(1, block + 1) if count % k == 0)

    def body(k, carry):
        step(low + k * block, block)
        return carry

    lax.fori_loop(0, count // block, body, 0)


def unpack_rows(fields, widths, even, odd, size_x, size_y, chosen=None):
    found, _ = segments(widths, size_x)
    wide = size_y + 2 * RIM
    swap = odd_place("gy")
    for field, x, rows, at in found:
        if chosen is not None and field not in chosen:
            continue
        a, b = even[at:at + rows], odd[at:at + rows]
        fields[field][x + widths[field], wide - rows:wide] = jnp.where(swap, a, b)
        fields[field][x + widths[field], size_y:size_y + rows] = jnp.where(swap, b, a)


def unpack_planes(field, width, even, odd, size_x, size_y):
    swap = odd_place("gx")
    tile = pl.ds(0, size_y)
    field[pl.ds(0, width), tile] = jnp.where(swap, even, odd)
    field[pl.ds(width + size_x, width), tile] = jnp.where(swap, odd, even)


def energy_part(x_even, x_odd, y_even, y_odd, density, labels, potential, energy_out, poten):
    size_x, size_y, size_z = density.shape
    starts, planes = plane_starts(WIDTHS)
    planes_loop(0, size_x, 4, lambda x, n: poten.__setitem__((pl.ds(x + 1, n), pl.ds(0, size_y)), potential[pl.ds(x, n)]))
    span = pl.ds(starts[3], 1)
    unpack_planes(poten, 1, x_even[span], x_odd[span], size_x, size_y)
    unpack_rows((None, None, None, poten), WIDTHS, y_even, y_odd, size_x, size_y, (3,))
    wide = size_y + 2 * RIM
    lane = lax.broadcasted_iota(jnp.int32, (1, wide, size_z), 2)
    is_first = lane == 0
    is_last = lane == size_z - 1
    energy_out[...] = jnp.zeros_like(energy_out)

    def step(x, n):
        span = pl.ds(x, n)
        v = poten[pl.ds(x + 1, n)]
        low, high = poten[pl.ds(x, n)] - v, poten[pl.ds(x + 2, n)] - v
        squares = low * low + high * high
        dv = shift(v, -1, 1) - v
        square = dv * dv
        squares = squares + square + shift(square, 1, 1)
        dv = jnp.where(is_last, 0.0, shift(v, -1, 2)) - v
        square = dv * dv
        squares = squares + square + jnp.where(is_first, v * v, shift(square, 1, 2))
        energy = material(density[span], labels[span]) * squares[:, :size_y]
        energy_out[...] += jnp.sum(energy.reshape(-1, 8, size_z), axis=0)

    planes_loop(0, size_x, 4, step)


def adjoint_part(x_even, x_odd, y_even, y_odd, density, labels, adjoint_start, adjoint_source, potential,
                 raw_out,
                 permit, start, source, poten, face_x, face_y, face_z, inverse, first, second):
    size_x, size_y, size_z = density.shape
    starts, _ = plane_starts(WIDTHS)
    fields = (permit, start, source, poten)
    tile = pl.ds(0, size_y)

    def fill(x, n):
        span = pl.ds(x, n)
        permit[pl.ds(x + WIDTHS[0], n), tile] = material(density[span], labels[span])
        start[pl.ds(x + WIDTHS[1], n), tile] = adjoint_start[span]
        source[pl.ds(x + WIDTHS[2], n), tile] = adjoint_source[span]
        poten[pl.ds(x + WIDTHS[3], n), tile] = potential[span]

    planes_loop(0, size_x, 4, fill)
    for field, width in enumerate(WIDTHS):
        span = pl.ds(starts[field], width)
        unpack_planes(fields[field], width, x_even[span], x_odd[span], size_x, size_y)
    unpack_rows(fields, WIDTHS, y_even, y_odd, size_x, size_y)

    wide = size_y + 2 * RIM
    lane = lax.broadcasted_iota(jnp.int32, (1, wide, size_z), 2)
    is_first = lane == 0
    is_last = lane == size_z - 1

    def harmonic(a, b):
        return 2.0 * a * b / jnp.maximum(a + b, 0.25)

    def faces_x(x, n):
        face_x[pl.ds(x, n)] = harmonic(permit[pl.ds(x, n)], permit[pl.ds(x + 1, n)])

    planes_loop(0, size_x + 5, 4, faces_x)

    def weigh(x, n):
        span = pl.ds(x, n)
        p = permit[pl.ds(x + 1, n)]
        fy = harmonic(p, shift(p, -1, 1))
        fz = jnp.where(is_last, 0.0, harmonic(p, shift(p, -1, 2)))
        face_y[span] = fy
        face_z[span] = fz
        total = screen + face_x[span] + face_x[pl.ds(x + 1, n)] + fy + shift(fy, 1, 1) + fz + shift(fz, 1, 2)
        inverse[span] = jnp.where(p > 20.0, 0.0, 1.0 / total)

    planes_loop(0, size_x + 4, 4, weigh)

    def relax(x, n, a, a_low, a_high):
        span = pl.ds(x, n)
        fy, fz = face_y[span], face_z[span]
        total = source[span] + face_x[pl.ds(x + 1, n)] * a_high + face_x[span] * a_low
        total = total + fy * shift(a, -1, 1) + shift(fy * a, 1, 1)
        total = total + fz * shift(a, -1, 2) + shift(fz * a, 1, 2)
        return total * inverse[span]

    def sweep_one(x, n):
        first[pl.ds(x, n)] = relax(x, n, start[pl.ds(x + 1, n)], start[pl.ds(x, n)], start[pl.ds(x + 2, n)])

    planes_loop(0, size_x + 4, 4, sweep_one)

    def sweep_two(x, n):
        second[pl.ds(x, n)] = relax(x + 1, n, first[pl.ds(x + 1, n)], first[pl.ds(x, n)], first[pl.ds(x + 2, n)])

    planes_loop(0, size_x + 2, 4, sweep_two)

    def finish(x, n):
        span = pl.ds(x, n)
        v, a = poten[pl.ds(x + 1, n)], second[pl.ds(x + 1, n)]
        product = (poten[pl.ds(x, n)] - v) * (second[pl.ds(x, n)] - a)
        product = product + (poten[pl.ds(x + 2, n)] - v) * (second[pl.ds(x + 2, n)] - a)
        both = (shift(v, -1, 1) - v) * (shift(a, -1, 1) - a)
        product = product + both + shift(both, 1, 1)
        both = (jnp.where(is_last, 0.0, shift(v, -1, 2)) - v) * (jnp.where(is_last, 0.0, shift(a, -1, 2)) - a)
        product = product + both + jnp.where(is_first, v * a, shift(both, 1, 2))
        d = density[span]
        gain = jnp.where(labels[span] == 1, -1.5 * (eps_solid - eps_void) * d * d, 0.0)
        raw_out[span] = gain * product[:, :size_y]

    planes_loop(0, size_x, 4, finish)


def pack_raw_x(raw, mine, other, even_out, odd_out, energy_out):
    size_x, size_y, size_z = raw.shape
    width = FILTER_SWEEPS
    low_first = odd_place("gx")
    energy = mine[...] + other[...]
    energy_out[...] = energy
    for out, low in ((even_out, low_first), (odd_out, jnp.logical_not(low_first))):
        out[pl.ds(0, width)] = raw[pl.ds(jnp.where(low, 0, size_x - width), width)]
    even_out[width, 0:8] = energy


def pack_raw_y(x_even, x_odd, raw, mine, other, even_out, odd_out, energy_out):
    size_x, size_y, _ = raw.shape
    width = FILTER_SWEEPS
    found, total = segments((width,), size_x)
    x_swap, y_swap = odd_place("gx"), odd_place("gy")
    energy = mine[...] + other[...]
    energy_out[...] = energy
    even_out[total:total + 8] = energy
    for _, x, rows, at in found:
        faces = []
        for rim in (slice(0, rows), slice(size_y - rows, size_y)):
            if x < 0:
                face = jnp.where(x_swap, x_even[width + x, rim], x_odd[width + x, rim])
            elif x >= size_x:
                face = jnp.where(x_swap, x_odd[x - size_x, rim], x_even[x - size_x, rim])
            else:
                face = raw[x, rim]
            faces.append(face)
        low, high = faces
        even_out[at:at + rows] = jnp.where(y_swap, low, high)
        odd_out[at:at + rows] = jnp.where(y_swap, high, low)


def filter_part(x_even, x_odd, y_even, y_odd, raw_in, labels, out, raw, even, odd):
    size_x, size_y, size_z = raw_in.shape
    width = FILTER_SWEEPS
    tile = pl.ds(0, size_y)

    def fill(x, n):
        raw[pl.ds(x + width, n), tile] = raw_in[pl.ds(x, n)]

    planes_loop(0, size_x, 4, fill)
    unpack_planes(raw, width, x_even[pl.ds(0, width)], x_odd[pl.ds(0, width)], size_x, size_y)
    unpack_rows((raw,), (width,), y_even, y_odd, size_x, size_y)

    wide = size_y + 2 * RIM
    extent_x = lax.axis_size("gx") * size_x
    extent_y = lax.axis_size("gy") * size_y
    base_x = lax.axis_index("gx") * size_x - width
    lane = lax.broadcasted_iota(jnp.int32, (1, wide, size_z), 2)
    row = lax.broadcasted_iota(jnp.int32, (1, wide, size_z), 1)
    place = lax.axis_index("gy") * size_y + jnp.where(row < size_y + RIM, row, row - wide)
    is_first, is_last = lane == 0, lane == size_z - 1

    def edges(at, extent):
        return jnp.where(at > 0, 1.0, 0.0) + jnp.where(at < extent - 1, 1.0, 0.0)

    count = edges(place, extent_y) + edges(lane, size_z)
    inside = (place >= 0) & (place < extent_y)
    scale_two = jnp.where(inside, 1.0 / (1.0 + radius_sq * (count + 2.0)), 0.0)
    scale_one = jnp.where(inside, 1.0 / (1.0 + radius_sq * (count + 1.0)), 0.0)

    def relax(src, x, n):
        f = src[pl.ds(x, n)]
        near = src[pl.ds(x - 1, n)] + src[pl.ds(x + 1, n)] + shift(f, 1, 1) + shift(f, -1, 1)
        near = near + jnp.where(is_first, 0.0, shift(f, 1, 2)) + jnp.where(is_last, 0.0, shift(f, -1, 2))
        total = raw[pl.ds(x, n)] + radius_sq * near
        scaled = []
        for k in range(n):
            at = base_x + x + k
            outside = (at < 0) | (at >= extent_x)
            border = (at == 0) | (at == extent_x - 1)
            scale = jnp.where(outside, 0.0, jnp.where(border, scale_one, scale_two))
            scaled.append(total[k:k + 1] * scale)
        return jnp.concatenate(scaled, axis=0)

    src = raw
    for sweep in range(FILTER_SWEEPS - 1):
        dst = (even, odd)[sweep % 2]

        def step(x, n, src=src, dst=dst):
            dst[pl.ds(x, n)] = relax(src, x, n)

        planes_loop(sweep + 1, size_x + 2 * width - sweep - 1, 4, step)
        src = dst

    def last(x, n):
        f = relax(src, x + width, n)
        out[pl.ds(x, n)] = jnp.where(labels[pl.ds(x, n)] == 1, f[:, :size_y], 0.0)

    planes_loop(0, size_x, 4, last)


def rescale(voxels, filtered, mine, other, out, mean_out):
    total = jnp.sum(mine[...] + other[...])
    mean = 0.5 * total / voxels + epsilon_mean
    mean_out[0, 0] = mean
    out[...] = filtered[...] * (1.0 / jnp.full((1, 1, out.shape[2]), mean, jnp.float32))


def swap_even(value, axis):
    return lax.ppermute(value, axis, [(i, i ^ 1) for i in range(lax.axis_size(axis))])


def swap_odd(value, axis):
    count = lax.axis_size(axis)
    up = [(i, i + 1) for i in range(1, count - 1, 2)]
    return lax.ppermute(value, axis, up + [(b, a) for a, b in up])


def partner(value, axis, bit):
    return lax.ppermute(value, axis, [(i, i ^ bit) for i in range(lax.axis_size(axis))])


def doubling(energy, stages):
    other = partner(energy, *stages[0])
    for stage in stages[1:]:
        energy = energy + other
        other = partner(energy, *stage)
    return energy, other


def shards(density, potential, adjoint_start, adjoint_source, labels):
    size_x, size_y, size_z = potential.shape
    _, planes = plane_starts(WIDTHS)
    _, rows = segments(WIDTHS, size_x)
    own = [
        pltpu.with_memory_space_constraint(array, pltpu.HBM)
        for array in (density, labels, adjoint_start, adjoint_source, potential)
    ]
    x_bits = [("gx", 1 << k) for k in range(1, (lax.axis_size("gx") - 1).bit_length())]
    y_bits = [("gy", 1 << k) for k in range(1, (lax.axis_size("gy") - 1).bit_length())]

    shape = (size_x, size_y, size_z)
    even, odd, *own = pl.pallas_call(
        pack_x,
        out_shape=(f32(planes, size_y, size_z),) * 2
        + (f32(*shape), jax.ShapeDtypeStruct(shape, jnp.int32)) + (f32(*shape),) * 3,
        in_specs=[pl.BlockSpec(memory_space=pltpu.HBM)] * 5,
        scratch_shapes=[pltpu.SemaphoreType.DMA((5,))],
        compiler_params=pltpu.CompilerParams(vmem_limit_bytes=VMEM_LIMIT),
    )(*own)
    x_odd = swap_odd(odd, "gx")
    x_even = swap_even(even, "gx")
    even, odd = call(pack_y, (f32(rows, size_z),) * 2)(x_even, x_odd, *own)
    y_odd = swap_odd(odd, "gy")
    y_even = swap_even(even, "gy")

    wide = size_y + 2 * RIM

    def room(extra):
        return pltpu.VMEM((size_x + extra, wide, size_z), jnp.float32)

    energy = call(energy_part, f32(8, size_z), [room(2)])(x_even, x_odd, y_even, y_odd, own[0], own[1], own[4])
    mine, other = doubling(energy, y_bits[1:])
    raw = call(
        adjoint_part,
        f32(*shape),
        [room(6), room(6), room(4), room(2), room(5), room(4), room(4), room(4), room(4), room(2)],
        cost=10000000,
    )(x_even, x_odd, y_even, y_odd, *own)

    face = f32(FILTER_SWEEPS, size_y, size_z)
    tall = f32(FILTER_SWEEPS + 1, size_y, size_z)
    even, odd, energy = call(pack_raw_x, (tall, face, f32(8, size_z)))(raw, mine, other)
    x_odd = swap_odd(odd, "gx")
    x_even = swap_even(even, "gx")
    energy = energy + x_even[FILTER_SWEEPS, 0:8]
    mine, other = doubling(energy, x_bits)
    _, rows = segments((FILTER_SWEEPS,), size_x)
    even, odd, energy = call(pack_raw_y, (f32(rows + 8, size_z), f32(rows, size_z), f32(8, size_z)))(
        x_even, x_odd, raw, mine, other)
    y_odd = swap_odd(odd, "gy")
    y_even = swap_even(even, "gy")
    energy = energy + y_even[rows:rows + 8]
    mine, other = doubling(energy, y_bits[:1])
    filtered = call(
        filter_part,
        f32(*shape),
        [room(2 * FILTER_SWEEPS)] * 3,
        cost=10000000,
    )(x_even, x_odd, y_even, y_odd, raw, own[1])
    voxels = lax.axis_size("gx") * size_x * lax.axis_size("gy") * size_y * size_z
    sensitivity, mean_energy = pl.pallas_call(
        functools.partial(rescale, float(voxels)),
        out_shape=(f32(*shape), f32(1, 1)),
        out_specs=(pl.BlockSpec(memory_space=pltpu.VMEM), pl.BlockSpec(memory_space=pltpu.SMEM)),
        compiler_params=pltpu.CompilerParams(vmem_limit_bytes=VMEM_LIMIT),
    )(filtered, mine, other)
    return (sensitivity, mean_energy[0, 0])


def solution(mesh):
    spec = P("gx", "gy", None)
    return jax.shard_map(
        shards, mesh=mesh, in_specs=(spec,) * 5, out_specs=(spec, P()), check_vma=False
    )
```

```python
import jax
import jax.numpy as jnp
from jax import lax
from jax.experimental import pallas as pl
from jax.experimental.pallas import tpu as pltpu
from jax.sharding import PartitionSpec as P

ADJ_SWEEPS = 2
FILTER_SWEEPS = 4

eps_void = 1.0
eps_solid = 12.0
eps_back = 4.0
eps_metal = 40.0
screen = 0.5
radius_sq = 2.0
epsilon_mean = 1e-06

WIDTHS = (ADJ_SWEEPS + 1, ADJ_SWEEPS + 1, ADJ_SWEEPS, 1)
RIM = 4
VMEM_LIMIT = 24 * 1024 * 1024


def segments(widths, size_x):
    found, at = [], 0
    for field, width in enumerate(widths):
        for x in range(-width, size_x + width):
            rows = width - max(0, -x, x - size_x + 1)
            if rows > 0:
                found.append((field, x, rows, at))
                at += rows
    return found, -(-at // 8) * 8


def plane_starts(widths):
    starts, at = [], 0
    for width in widths:
        starts.append(at)
        at += width
    return starts, at


def material(density, labels):
    design = eps_void + density * density * density * (eps_solid - eps_void)
    return jnp.where(labels == 1, design, jnp.where(labels == 2, eps_metal, eps_back))


def call(body, outs, scratch=(), in_specs=None, cost=10000):
    kwargs = {} if in_specs is None else {"in_specs": in_specs, "grid": (1,)}
    return pl.pallas_call(
        body,
        out_shape=outs,
        scratch_shapes=list(scratch),
        compiler_params=pltpu.CompilerParams(vmem_limit_bytes=VMEM_LIMIT),
        cost_estimate=pl.CostEstimate(flops=cost, bytes_accessed=cost, transcendentals=0),
        **kwargs,
    )


def f32(*shape):
    return jax.ShapeDtypeStruct(shape, jnp.float32)


def odd_place(axis):
    return lax.rem(lax.axis_index(axis), 2) == 1


def pack_x(*refs):
    inputs, (even_out, odd_out), held, (sem,) = refs[:5], refs[5:7], refs[7:12], refs[12:]
    density, labels, adjoint, source, potential = held
    size_x = density.shape[0]
    starts, _ = plane_starts(WIDTHS)
    copies = [pltpu.make_async_copy(a, b, sem.at[k]) for k, (a, b) in enumerate(zip(inputs, held))]
    for copy in copies:
        copy.start()
    for copy in copies:
        copy.wait()
    low_first = odd_place("gx")
    for out, low in ((even_out, low_first), (odd_out, jnp.logical_not(low_first))):
        for field, width in enumerate(WIDTHS):
            span = pl.ds(jnp.where(low, 0, size_x - width), width)
            if field == 0:
                face = material(density[span], labels[span])
            else:
                face = (adjoint, source, potential)[field - 1][span]
            out[pl.ds(starts[field], width)] = face


def pack_y(x_odd, x_even, density, labels, adjoint, source, potential, even_out, odd_out):
    size_x, size_y, _ = density.shape
    starts, _ = plane_starts(WIDTHS)
    found, _ = segments(WIDTHS, size_x)
    x_swap, y_swap = odd_place("gx"), odd_place("gy")
    for field, x, rows, at in found:
        faces = []
        for rim in (slice(0, rows), slice(size_y - rows, size_y)):
            if x < 0:
                plane = starts[field] + WIDTHS[field] + x
                face = jnp.where(x_swap, x_even[plane, rim], x_odd[plane, rim])
            elif x >= size_x:
                plane = starts[field] + x - size_x
                face = jnp.where(x_swap, x_odd[plane, rim], x_even[plane, rim])
            elif field == 0:
                face = material(density[x, rim], labels[x, rim])
            else:
                face = (adjoint, source, potential)[field - 1][x, rim]
            faces.append(face)
        low, high = faces
        even_out[at:at + rows] = jnp.where(y_swap, low, high)
        odd_out[at:at + rows] = jnp.where(y_swap, high, low)


def shift(value, by, axis):
    return pltpu.roll(value, by % value.shape[axis], axis)


def planes_loop(low, high, block, step):
    count = high - low
    block = max(k for k in range(1, block + 1) if count % k == 0)

    def body(k, carry):
        step(low + k * block, block)
        return carry

    lax.fori_loop(0, count // block, body, 0)


def unpack_rows(fields, widths, even, odd, size_x, size_y, chosen=None):
    found, _ = segments(widths, size_x)
    wide = size_y + 2 * RIM
    swap = odd_place("gy")
    for field, x, rows, at in found:
        if chosen is not None and field not in chosen:
            continue
        a, b = even[at:at + rows], odd[at:at + rows]
        fields[field][x + widths[field], wide - rows:wide] = jnp.where(swap, a, b)
        fields[field][x + widths[field], size_y:size_y + rows] = jnp.where(swap, b, a)


def unpack_planes(field, width, even, odd, size_x, size_y):
    swap = odd_place("gx")
    tile = pl.ds(0, size_y)
    field[pl.ds(0, width), tile] = jnp.where(swap, even, odd)
    field[pl.ds(width + size_x, width), tile] = jnp.where(swap, odd, even)


def energy_part(x_odd, x_even, y_odd, y_even, density, labels, potential, energy_out, poten):
    size_x, size_y, size_z = density.shape
    starts, planes = plane_starts(WIDTHS)
    planes_loop(0, size_x, 4, lambda x, n: poten.__setitem__((pl.ds(x + 1, n), pl.ds(0, size_y)), potential[pl.ds(x, n)]))
    span = pl.ds(starts[3], 1)
    unpack_planes(poten, 1, x_even[span], x_odd[span], size_x, size_y)
    unpack_rows((None, None, None, poten), WIDTHS, y_even, y_odd, size_x, size_y, (3,))
    wide = size_y + 2 * RIM
    lane = lax.broadcasted_iota(jnp.int32, (1, wide, size_z), 2)
    is_first = lane == 0
    is_last = lane == size_z - 1
    energy_out[...] = jnp.zeros_like(energy_out)

    def step(x, n):
        span = pl.ds(x, n)
        v = poten[pl.ds(x + 1, n)]
        low, high = poten[pl.ds(x, n)] - v, poten[pl.ds(x + 2, n)] - v
        squares = low * low + high * high
        dv = shift(v, -1, 1) - v
        square = dv * dv
        squares = squares + square + shift(square, 1, 1)
        dv = jnp.where(is_last, 0.0, shift(v, -1, 2)) - v
        square = dv * dv
        squares = squares + square + jnp.where(is_first, v * v, shift(square, 1, 2))
        energy = material(density[span], labels[span]) * squares[:, :size_y]
        energy_out[...] += jnp.sum(energy.reshape(-1, 8, size_z), axis=0)

    planes_loop(0, size_x, 4, step)


def adjoint_part(x_odd, x_even, y_odd, y_even, density, labels, adjoint_start, adjoint_source, potential,
                 raw_out,
                 permit, start, source, poten, face_x, face_y, face_z, inverse, first, second):
    size_x, size_y, size_z = density.shape
    starts, _ = plane_starts(WIDTHS)
    fields = (permit, start, source, poten)
    tile = pl.ds(0, size_y)

    def fill(x, n):
        span = pl.ds(x, n)
        permit[pl.ds(x + WIDTHS[0], n), tile] = material(density[span], labels[span])
        start[pl.ds(x + WIDTHS[1], n), tile] = adjoint_start[span]
        source[pl.ds(x + WIDTHS[2], n), tile] = adjoint_source[span]
        poten[pl.ds(x + WIDTHS[3], n), tile] = potential[span]

    planes_loop(0, size_x, 4, fill)
    for field, width in enumerate(WIDTHS):
        span = pl.ds(starts[field], width)
        unpack_planes(fields[field], width, x_even[span], x_odd[span], size_x, size_y)
    unpack_rows(fields, WIDTHS, y_even, y_odd, size_x, size_y)

    wide = size_y + 2 * RIM
    lane = lax.broadcasted_iota(jnp.int32, (1, wide, size_z), 2)
    is_first = lane == 0
    is_last = lane == size_z - 1

    def harmonic(a, b):
        return 2.0 * a * b / jnp.maximum(a + b, 0.25)

    def faces_x(x, n):
        face_x[pl.ds(x, n)] = harmonic(permit[pl.ds(x, n)], permit[pl.ds(x + 1, n)])

    planes_loop(0, size_x + 5, 7, faces_x)

    def weigh(x, n):
        span = pl.ds(x, n)
        p = permit[pl.ds(x + 1, n)]
        fy = harmonic(p, shift(p, -1, 1))
        fz = jnp.where(is_last, 0.0, harmonic(p, shift(p, -1, 2)))
        face_y[span] = fy
        face_z[span] = fz
        total = screen + face_x[span] + face_x[pl.ds(x + 1, n)] + fy + shift(fy, 1, 1) + fz + shift(fz, 1, 2)
        inverse[span] = jnp.where(p > 20.0, 0.0, 1.0 / total)

    planes_loop(0, size_x + 4, 5, weigh)

    def relax(x, n, a, a_low, a_high):
        span = pl.ds(x, n)
        fy, fz = face_y[span], face_z[span]
        total = source[span] + face_x[pl.ds(x + 1, n)] * a_high + face_x[span] * a_low
        total = total + fy * shift(a, -1, 1) + shift(fy * a, 1, 1)
        total = total + fz * shift(a, -1, 2) + shift(fz * a, 1, 2)
        return total * inverse[span]

    def sweep_one(x, n):
        first[pl.ds(x, n)] = relax(x, n, start[pl.ds(x + 1, n)], start[pl.ds(x, n)], start[pl.ds(x + 2, n)])

    planes_loop(0, size_x + 4, 10, sweep_one)

    def sweep_two(x, n):
        second[pl.ds(x, n)] = relax(x + 1, n, first[pl.ds(x + 1, n)], first[pl.ds(x, n)], first[pl.ds(x + 2, n)])

    planes_loop(0, size_x + 2, 9, sweep_two)

    def finish(x, n):
        span = pl.ds(x, n)
        v, a = poten[pl.ds(x + 1, n)], second[pl.ds(x + 1, n)]
        product = (poten[pl.ds(x, n)] - v) * (second[pl.ds(x, n)] - a)
        product = product + (poten[pl.ds(x + 2, n)] - v) * (second[pl.ds(x + 2, n)] - a)
        both = (shift(v, -1, 1) - v) * (shift(a, -1, 1) - a)
        product = product + both + shift(both, 1, 1)
        both = (jnp.where(is_last, 0.0, shift(v, -1, 2)) - v) * (jnp.where(is_last, 0.0, shift(a, -1, 2)) - a)
        product = product + both + jnp.where(is_first, v * a, shift(both, 1, 2))
        d = density[span]
        gain = jnp.where(labels[span] == 1, -1.5 * (eps_solid - eps_void) * d * d, 0.0)
        raw_out[span] = gain * product[:, :size_y]

    planes_loop(0, size_x, 8, finish)


def pack_raw_x(raw, mine, other, even_out, odd_out, energy_out):
    size_x, size_y, size_z = raw.shape
    width = FILTER_SWEEPS
    low_first = odd_place("gx")
    energy = mine[...] + other[...]
    energy_out[...] = energy
    for out, low in ((even_out, low_first), (odd_out, jnp.logical_not(low_first))):
        out[pl.ds(0, width)] = raw[pl.ds(jnp.where(low, 0, size_x - width), width)]
    even_out[width, 0:8] = energy


def pack_raw_y(x_odd, x_even, raw, mine, other, even_out, odd_out, energy_out):
    size_x, size_y, _ = raw.shape
    width = FILTER_SWEEPS
    found, total = segments((width,), size_x)
    x_swap, y_swap = odd_place("gx"), odd_place("gy")
    energy = mine[...] + other[...]
    energy_out[...] = energy
    even_out[total:total + 8] = energy
    for _, x, rows, at in found:
        faces = []
        for rim in (slice(0, rows), slice(size_y - rows, size_y)):
            if x < 0:
                face = jnp.where(x_swap, x_even[width + x, rim], x_odd[width + x, rim])
            elif x >= size_x:
                face = jnp.where(x_swap, x_odd[x - size_x, rim], x_even[x - size_x, rim])
            else:
                face = raw[x, rim]
            faces.append(face)
        low, high = faces
        even_out[at:at + rows] = jnp.where(y_swap, low, high)
        odd_out[at:at + rows] = jnp.where(y_swap, high, low)


def filter_part(x_odd, x_even, y_odd, y_even, raw_in, labels, mine, other, out, mean_out, raw, even, odd, held, sem):
    size_x, size_y, size_z = raw_in.shape
    width = FILTER_SWEEPS
    tile = pl.ds(0, size_y)

    def fill(x, n):
        raw[pl.ds(x + width, n), tile] = raw_in[pl.ds(x, n)]

    planes_loop(0, size_x, 4, fill)
    unpack_planes(raw, width, x_even[pl.ds(0, width)], x_odd[pl.ds(0, width)], size_x, size_y)
    unpack_rows((raw,), (width,), y_even, y_odd, size_x, size_y)

    wide = size_y + 2 * RIM
    extent_x = lax.axis_size("gx") * size_x
    extent_y = lax.axis_size("gy") * size_y
    base_x = lax.axis_index("gx") * size_x - width
    lane = lax.broadcasted_iota(jnp.int32, (1, wide, size_z), 2)
    row = lax.broadcasted_iota(jnp.int32, (1, wide, size_z), 1)
    place = lax.axis_index("gy") * size_y + jnp.where(row < size_y + RIM, row, row - wide)
    is_first, is_last = lane == 0, lane == size_z - 1

    def edges(at, extent):
        return jnp.where(at > 0, 1.0, 0.0) + jnp.where(at < extent - 1, 1.0, 0.0)

    count = edges(place, extent_y) + edges(lane, size_z)
    inside = (place >= 0) & (place < extent_y)
    scale_two = jnp.where(inside, 1.0 / (1.0 + radius_sq * (count + 2.0)), 0.0)
    scale_one = jnp.where(inside, 1.0 / (1.0 + radius_sq * (count + 1.0)), 0.0)

    def relax(src, x, n):
        f = src[pl.ds(x, n)]
        near = src[pl.ds(x - 1, n)] + src[pl.ds(x + 1, n)] + shift(f, 1, 1) + shift(f, -1, 1)
        near = near + jnp.where(is_first, 0.0, shift(f, 1, 2)) + jnp.where(is_last, 0.0, shift(f, -1, 2))
        total = raw[pl.ds(x, n)] + radius_sq * near
        scaled = []
        for k in range(n):
            at = base_x + x + k
            outside = (at < 0) | (at >= extent_x)
            border = (at == 0) | (at == extent_x - 1)
            scale = jnp.where(outside, 0.0, jnp.where(border, scale_one, scale_two))
            scaled.append(total[k:k + 1] * scale)
        return jnp.concatenate(scaled, axis=0)

    src = raw
    for sweep in range(FILTER_SWEEPS - 1):
        dst = (even, odd)[sweep % 2]

        def step(x, n, src=src, dst=dst):
            dst[pl.ds(x, n)] = relax(src, x, n)

        planes_loop(sweep + 1, size_x + 2 * width - sweep - 1, 11, step)
        src = dst

    total = jnp.sum(mine[...] + other[...])
    mean = 0.5 * total / (extent_x * extent_y * size_z) + epsilon_mean
    mean_out[0, 0] = mean
    inverse = 1.0 / jnp.full((1, 1, size_z), mean, jnp.float32)
    block = size_x // 2
    copies = []
    for k in range(2):
        span = pl.ds(k * block, block)
        f = relax(src, k * block + width, block)[:, :size_y]
        held[span] = jnp.where(labels[span] == 1, f * inverse, 0.0)
        copies.append(pltpu.make_async_copy(held.at[span], out.at[span], sem.at[k]))
        copies[k].start()
    for copy in copies:
        copy.wait()


def swap_even(value, axis):
    return lax.ppermute(value, axis, [(i, i ^ 1) for i in range(lax.axis_size(axis))])


def swap_odd(value, axis):
    count = lax.axis_size(axis)
    up = [(i, i + 1) for i in range(1, count - 1, 2)]
    return lax.ppermute(value, axis, up + [(b, a) for a, b in up])


def partner(value, axis, bit):
    return lax.ppermute(value, axis, [(i, i ^ bit) for i in range(lax.axis_size(axis))])


def doubling(energy, stages):
    other = partner(energy, *stages[0])
    for stage in stages[1:]:
        energy = energy + other
        other = partner(energy, *stage)
    return energy, other


def shards(density, potential, adjoint_start, adjoint_source, labels):
    size_x, size_y, size_z = potential.shape
    _, planes = plane_starts(WIDTHS)
    _, rows = segments(WIDTHS, size_x)
    own = [
        pltpu.with_memory_space_constraint(array, pltpu.HBM)
        for array in (density, labels, adjoint_start, adjoint_source, potential)
    ]
    x_bits = [("gx", 1 << k) for k in range(1, (lax.axis_size("gx") - 1).bit_length())]
    y_bits = [("gy", 1 << k) for k in range(1, (lax.axis_size("gy") - 1).bit_length())]

    shape = (size_x, size_y, size_z)
    even, odd, *own = pl.pallas_call(
        pack_x,
        out_shape=(f32(planes, size_y, size_z),) * 2
        + (f32(*shape), jax.ShapeDtypeStruct(shape, jnp.int32)) + (f32(*shape),) * 3,
        in_specs=[pl.BlockSpec(memory_space=pltpu.HBM)] * 5,
        scratch_shapes=[pltpu.SemaphoreType.DMA((5,))],
        compiler_params=pltpu.CompilerParams(vmem_limit_bytes=VMEM_LIMIT),
    )(*own)
    x_even = swap_even(even, "gx")
    x_odd = swap_odd(odd, "gx")
    even, odd = call(pack_y, (f32(rows, size_z),) * 2)(x_odd, x_even, *own)
    y_even = swap_even(even, "gy")
    y_odd = swap_odd(odd, "gy")

    wide = size_y + 2 * RIM

    def room(extra):
        return pltpu.VMEM((size_x + extra, wide, size_z), jnp.float32)

    energy = call(energy_part, f32(8, size_z), [room(2)])(x_odd, x_even, y_odd, y_even, own[0], own[1], own[4])
    mine, other = doubling(energy, y_bits[1:])
    raw = call(
        adjoint_part,
        f32(*shape),
        [room(6), room(6), room(4), room(2), room(5), room(4), room(4), room(4), room(4), room(2)],
        cost=10000000,
    )(x_odd, x_even, y_odd, y_even, *own)

    face = f32(FILTER_SWEEPS, size_y, size_z)
    tall = f32(FILTER_SWEEPS + 1, size_y, size_z)
    even, odd, energy = call(pack_raw_x, (tall, face, f32(8, size_z)))(raw, mine, other)
    x_even = swap_even(even, "gx")
    x_odd = swap_odd(odd, "gx")
    energy = energy + x_even[FILTER_SWEEPS, 0:8]
    mine, other = doubling(energy, x_bits)
    _, rows = segments((FILTER_SWEEPS,), size_x)
    even, odd, energy = call(pack_raw_y, (f32(rows + 8, size_z), f32(rows, size_z), f32(8, size_z)))(
        x_odd, x_even, raw, mine, other)
    y_even = swap_even(even, "gy")
    y_odd = swap_odd(odd, "gy")
    energy = energy + y_even[rows:rows + 8]
    mine, other = doubling(energy, y_bits[:1])
    sensitivity, mean_energy = pl.pallas_call(
        filter_part,
        out_shape=(f32(*shape), f32(1, 1)),
        out_specs=(pl.BlockSpec(memory_space=pl.ANY), pl.BlockSpec(memory_space=pltpu.SMEM)),
        scratch_shapes=[room(2 * FILTER_SWEEPS)] * 3 + [pltpu.VMEM(shape, jnp.float32), pltpu.SemaphoreType.DMA((2,))],
        compiler_params=pltpu.CompilerParams(vmem_limit_bytes=VMEM_LIMIT),
    )(x_odd, x_even, y_odd, y_even, raw, own[1], mine, other)
    return (sensitivity, mean_energy[0, 0])


def solution(mesh):
    spec = P("gx", "gy", None)
    return jax.shard_map(
        shards, mesh=mesh, in_specs=(spec,) * 5, out_specs=(spec, P()), check_vma=False
    )
```

```python
import functools

import jax
import jax.numpy as jnp
from jax import lax
from jax.experimental import pallas as pl
from jax.experimental.pallas import tpu as pltpu
from jax.sharding import PartitionSpec as P

ADJ_SWEEPS = 2
FILTER_SWEEPS = 4

eps_void = 1.0
eps_solid = 12.0
eps_back = 4.0
eps_metal = 40.0
screen = 0.5
radius_sq = 2.0
epsilon_mean = 1e-06

WIDTHS = (ADJ_SWEEPS + 1, ADJ_SWEEPS + 1, ADJ_SWEEPS, 1)
RIM = 4
VMEM_LIMIT = 24 * 1024 * 1024


def segments(widths, size_x, beside=True, beyond=True):
    found, at = [], 0
    for field, width in enumerate(widths):
        for x in range(-width, size_x + width):
            rows = width - max(0, -x, x - size_x + 1)
            if rows > 0 and (beside if 0 <= x < size_x else beyond):
                found.append((field, x, rows, at))
                at += rows
    return found, -(-at // 8) * 8


def plane_starts(widths):
    starts, at = [], 0
    for width in widths:
        starts.append(at)
        at += width
    return starts, at


def material(density, labels):
    design = eps_void + density * density * density * (eps_solid - eps_void)
    return jnp.where(labels == 1, design, jnp.where(labels == 2, eps_metal, eps_back))


def call(body, outs, scratch=(), in_specs=None, cost=10000):
    kwargs = {} if in_specs is None else {"in_specs": in_specs, "grid": (1,)}
    return pl.pallas_call(
        body,
        out_shape=outs,
        scratch_shapes=list(scratch),
        compiler_params=pltpu.CompilerParams(vmem_limit_bytes=VMEM_LIMIT),
        cost_estimate=pl.CostEstimate(flops=cost, bytes_accessed=cost, transcendentals=0),
        **kwargs,
    )


def f32(*shape):
    return jax.ShapeDtypeStruct(shape, jnp.float32)


def odd_place(axis):
    return lax.rem(lax.axis_index(axis), 2) == 1


def pack_own(*refs):
    inputs, (x_odd_out, x_even_out, y_even_out, y_odd_out), held, sem = refs[:5], refs[5:9], refs[9:14], refs[14]
    density, labels, adjoint, source, potential = held
    size_x, size_y, _ = density.shape
    starts, _ = plane_starts(WIDTHS)
    copies = [pltpu.make_async_copy(a, b, sem.at[k]) for k, (a, b) in enumerate(zip(inputs, held))]
    for copy in copies:
        copy.start()
    for copy in copies:
        copy.wait()
    low_first = odd_place("gx")
    for out, low in ((x_even_out, low_first), (x_odd_out, jnp.logical_not(low_first))):
        for field, width in enumerate(WIDTHS):
            span = pl.ds(jnp.where(low, 0, size_x - width), width)
            if field == 0:
                face = material(density[span], labels[span])
            else:
                face = (adjoint, source, potential)[field - 1][span]
            out[pl.ds(starts[field], width)] = face
    y_swap = odd_place("gy")
    for field, x, rows, at in segments(WIDTHS, size_x, beyond=False)[0]:
        faces = []
        for rim in (slice(0, rows), slice(size_y - rows, size_y)):
            if field == 0:
                faces.append(material(density[x, rim], labels[x, rim]))
            else:
                faces.append((adjoint, source, potential)[field - 1][x, rim])
        low, high = faces
        y_even_out[at:at + rows] = jnp.where(y_swap, low, high)
        y_odd_out[at:at + rows] = jnp.where(y_swap, high, low)


def pack_corners(size_x, x_odd, x_even, even_out, odd_out):
    size_y = x_odd.shape[1]
    starts, _ = plane_starts(WIDTHS)
    x_swap, y_swap = odd_place("gx"), odd_place("gy")
    for field, x, rows, at in segments(WIDTHS, size_x, beside=False)[0]:
        faces = []
        for rim in (slice(0, rows), slice(size_y - rows, size_y)):
            if x < 0:
                plane = starts[field] + WIDTHS[field] + x
                face = jnp.where(x_swap, x_even[plane, rim], x_odd[plane, rim])
            else:
                plane = starts[field] + x - size_x
                face = jnp.where(x_swap, x_odd[plane, rim], x_even[plane, rim])
            faces.append(face)
        low, high = faces
        even_out[at:at + rows] = jnp.where(y_swap, low, high)
        odd_out[at:at + rows] = jnp.where(y_swap, high, low)


def shift(value, by, axis):
    return pltpu.roll(value, by % value.shape[axis], axis)


def planes_loop(low, high, block, step):
    count = high - low
    block = max(k for k in range(1, block + 1) if count % k == 0)

    def body(k, carry):
        step(low + k * block, block)
        return carry

    lax.fori_loop(0, count // block, body, 0)


def unpack_rows(fields, widths, found, even, odd, size_y):
    wide = size_y + 2 * RIM
    swap = odd_place("gy")
    for field, x, rows, at in found:
        if fields[field] is None:
            continue
        a, b = even[at:at + rows], odd[at:at + rows]
        fields[field][x + widths[field], wide - rows:wide] = jnp.where(swap, a, b)
        fields[field][x + widths[field], size_y:size_y + rows] = jnp.where(swap, b, a)


def unpack_planes(field, width, even, odd, size_x, size_y):
    swap = odd_place("gx")
    tile = pl.ds(0, size_y)
    field[pl.ds(0, width), tile] = jnp.where(swap, even, odd)
    field[pl.ds(width + size_x, width), tile] = jnp.where(swap, odd, even)


def energy_part(x_odd, x_even, y_even, y_odd, density, labels, potential, energy_out, poten):
    size_x, size_y, size_z = density.shape
    starts, planes = plane_starts(WIDTHS)
    planes_loop(0, size_x, 4, lambda x, n: poten.__setitem__((pl.ds(x + 1, n), pl.ds(0, size_y)), potential[pl.ds(x, n)]))
    span = pl.ds(starts[3], 1)
    unpack_planes(poten, 1, x_even[span], x_odd[span], size_x, size_y)
    found, _ = segments(WIDTHS, size_x, beyond=False)
    unpack_rows((None, None, None, poten), WIDTHS, found, y_even, y_odd, size_y)
    wide = size_y + 2 * RIM
    lane = lax.broadcasted_iota(jnp.int32, (1, wide, size_z), 2)
    is_first = lane == 0
    is_last = lane == size_z - 1
    energy_out[...] = jnp.zeros_like(energy_out)

    def step(x, n):
        span = pl.ds(x, n)
        v = poten[pl.ds(x + 1, n)]
        low, high = poten[pl.ds(x, n)] - v, poten[pl.ds(x + 2, n)] - v
        squares = low * low + high * high
        dv = shift(v, -1, 1) - v
        square = dv * dv
        squares = squares + square + shift(square, 1, 1)
        dv = jnp.where(is_last, 0.0, shift(v, -1, 2)) - v
        square = dv * dv
        squares = squares + square + jnp.where(is_first, v * v, shift(square, 1, 2))
        energy = material(density[span], labels[span]) * squares[:, :size_y]
        energy_out[...] += jnp.sum(energy.reshape(-1, 8, size_z), axis=0)

    planes_loop(0, size_x, 4, step)


def adjoint_part(x_odd, x_even, y_even, y_odd, corner_even, corner_odd, density, labels, adjoint_start, adjoint_source, potential,
                 raw_out,
                 permit, start, source, poten, face_x, face_y, face_z, inverse, first, second):
    size_x, size_y, size_z = density.shape
    starts, _ = plane_starts(WIDTHS)
    fields = (permit, start, source, poten)
    tile = pl.ds(0, size_y)

    def fill(x, n):
        span = pl.ds(x, n)
        permit[pl.ds(x + WIDTHS[0], n), tile] = material(density[span], labels[span])
        start[pl.ds(x + WIDTHS[1], n), tile] = adjoint_start[span]
        source[pl.ds(x + WIDTHS[2], n), tile] = adjoint_source[span]
        poten[pl.ds(x + WIDTHS[3], n), tile] = potential[span]

    planes_loop(0, size_x, 4, fill)
    for field, width in enumerate(WIDTHS):
        span = pl.ds(starts[field], width)
        unpack_planes(fields[field], width, x_even[span], x_odd[span], size_x, size_y)
    unpack_rows(fields, WIDTHS, segments(WIDTHS, size_x, beyond=False)[0], y_even, y_odd, size_y)
    unpack_rows(fields, WIDTHS, segments(WIDTHS, size_x, beside=False)[0], corner_even, corner_odd, size_y)

    wide = size_y + 2 * RIM
    lane = lax.broadcasted_iota(jnp.int32, (1, wide, size_z), 2)
    is_first = lane == 0
    is_last = lane == size_z - 1

    def harmonic(a, b):
        return 2.0 * a * b / jnp.maximum(a + b, 0.25)

    def faces_x(x, n):
        face_x[pl.ds(x, n)] = harmonic(permit[pl.ds(x, n)], permit[pl.ds(x + 1, n)])

    planes_loop(0, size_x + 5, 7, faces_x)

    def weigh(x, n):
        span = pl.ds(x, n)
        p = permit[pl.ds(x + 1, n)]
        fy = harmonic(p, shift(p, -1, 1))
        fz = jnp.where(is_last, 0.0, harmonic(p, shift(p, -1, 2)))
        face_y[span] = fy
        face_z[span] = fz
        total = screen + face_x[span] + face_x[pl.ds(x + 1, n)] + fy + shift(fy, 1, 1) + fz + shift(fz, 1, 2)
        inverse[span] = jnp.where(p > 20.0, 0.0, 1.0 / total)

    planes_loop(0, size_x + 4, 5, weigh)

    def relax(x, n, a, a_low, a_high):
        span = pl.ds(x, n)
        fy, fz = face_y[span], face_z[span]
        total = source[span] + face_x[pl.ds(x + 1, n)] * a_high + face_x[span] * a_low
        total = total + fy * shift(a, -1, 1) + shift(fy * a, 1, 1)
        total = total + fz * shift(a, -1, 2) + shift(fz * a, 1, 2)
        return total * inverse[span]

    def sweep_one(x, n):
        first[pl.ds(x, n)] = relax(x, n, start[pl.ds(x + 1, n)], start[pl.ds(x, n)], start[pl.ds(x + 2, n)])

    planes_loop(0, size_x + 4, 10, sweep_one)

    def sweep_two(x, n):
        second[pl.ds(x, n)] = relax(x + 1, n, first[pl.ds(x + 1, n)], first[pl.ds(x, n)], first[pl.ds(x + 2, n)])

    planes_loop(0, size_x + 2, 9, sweep_two)

    def finish(x, n):
        span = pl.ds(x, n)
        v, a = poten[pl.ds(x + 1, n)], second[pl.ds(x + 1, n)]
        product = (poten[pl.ds(x, n)] - v) * (second[pl.ds(x, n)] - a)
        product = product + (poten[pl.ds(x + 2, n)] - v) * (second[pl.ds(x + 2, n)] - a)
        both = (shift(v, -1, 1) - v) * (shift(a, -1, 1) - a)
        product = product + both + shift(both, 1, 1)
        both = (jnp.where(is_last, 0.0, shift(v, -1, 2)) - v) * (jnp.where(is_last, 0.0, shift(a, -1, 2)) - a)
        product = product + both + jnp.where(is_first, v * a, shift(both, 1, 2))
        d = density[span]
        gain = jnp.where(labels[span] == 1, -1.5 * (eps_solid - eps_void) * d * d, 0.0)
        raw_out[span] = gain * product[:, :size_y]

    planes_loop(0, size_x, 8, finish)


def pack_raw_x(raw, mine, other, even_out, odd_out, energy_out):
    size_x, size_y, size_z = raw.shape
    width = FILTER_SWEEPS
    low_first = odd_place("gx")
    energy = mine[...] + other[...]
    energy_out[...] = energy
    for out, low in ((even_out, low_first), (odd_out, jnp.logical_not(low_first))):
        out[pl.ds(0, width)] = raw[pl.ds(jnp.where(low, 0, size_x - width), width)]
    even_out[width, 0:8] = energy


def pack_raw_y(x_odd, x_even, raw, mine, other, even_out, odd_out, energy_out):
    size_x, size_y, _ = raw.shape
    width = FILTER_SWEEPS
    found, total = segments((width,), size_x)
    x_swap, y_swap = odd_place("gx"), odd_place("gy")
    energy = mine[...] + other[...]
    energy_out[...] = energy
    even_out[total:total + 8] = energy
    for _, x, rows, at in found:
        faces = []
        for rim in (slice(0, rows), slice(size_y - rows, size_y)):
            if x < 0:
                face = jnp.where(x_swap, x_even[width + x, rim], x_odd[width + x, rim])
            elif x >= size_x:
                face = jnp.where(x_swap, x_odd[x - size_x, rim], x_even[x - size_x, rim])
            else:
                face = raw[x, rim]
            faces.append(face)
        low, high = faces
        even_out[at:at + rows] = jnp.where(y_swap, low, high)
        odd_out[at:at + rows] = jnp.where(y_swap, high, low)


def filter_part(x_odd, x_even, y_odd, y_even, raw_in, labels, mine, other, out, mean_out, raw, even, odd, held, sem):
    size_x, size_y, size_z = raw_in.shape
    width = FILTER_SWEEPS
    tile = pl.ds(0, size_y)

    def fill(x, n):
        raw[pl.ds(x + width, n), tile] = raw_in[pl.ds(x, n)]

    planes_loop(0, size_x, 4, fill)
    unpack_planes(raw, width, x_even[pl.ds(0, width)], x_odd[pl.ds(0, width)], size_x, size_y)
    unpack_rows((raw,), (width,), segments((width,), size_x)[0], y_even, y_odd, size_y)

    wide = size_y + 2 * RIM
    extent_x = lax.axis_size("gx") * size_x
    extent_y = lax.axis_size("gy") * size_y
    base_x = lax.axis_index("gx") * size_x - width
    lane = lax.broadcasted_iota(jnp.int32, (1, wide, size_z), 2)
    row = lax.broadcasted_iota(jnp.int32, (1, wide, size_z), 1)
    place = lax.axis_index("gy") * size_y + jnp.where(row < size_y + RIM, row, row - wide)
    is_first, is_last = lane == 0, lane == size_z - 1

    def edges(at, extent):
        return jnp.where(at > 0, 1.0, 0.0) + jnp.where(at < extent - 1, 1.0, 0.0)

    count = edges(place, extent_y) + edges(lane, size_z)
    inside = (place >= 0) & (place < extent_y)
    scale_two = jnp.where(inside, 1.0 / (1.0 + radius_sq * (count + 2.0)), 0.0)
    scale_one = jnp.where(inside, 1.0 / (1.0 + radius_sq * (count + 1.0)), 0.0)

    def relax(src, x, n):
        f = src[pl.ds(x, n)]
        near = src[pl.ds(x - 1, n)] + src[pl.ds(x + 1, n)] + shift(f, 1, 1) + shift(f, -1, 1)
        near = near + jnp.where(is_first, 0.0, shift(f, 1, 2)) + jnp.where(is_last, 0.0, shift(f, -1, 2))
        total = raw[pl.ds(x, n)] + radius_sq * near
        scaled = []
        for k in range(n):
            at = base_x + x + k
            outside = (at < 0) | (at >= extent_x)
            border = (at == 0) | (at == extent_x - 1)
            scale = jnp.where(outside, 0.0, jnp.where(border, scale_one, scale_two))
            scaled.append(total[k:k + 1] * scale)
        return jnp.concatenate(scaled, axis=0)

    src = raw
    for sweep in range(FILTER_SWEEPS - 1):
        dst = (even, odd)[sweep % 2]

        def step(x, n, src=src, dst=dst):
            dst[pl.ds(x, n)] = relax(src, x, n)

        planes_loop(sweep + 1, size_x + 2 * width - sweep - 1, 11, step)
        src = dst

    total = jnp.sum(mine[...] + other[...])
    mean = 0.5 * total / (extent_x * extent_y * size_z) + epsilon_mean
    mean_out[0, 0] = mean
    inverse = 1.0 / jnp.full((1, 1, size_z), mean, jnp.float32)
    block = size_x // 2
    copies = []
    for k in range(2):
        span = pl.ds(k * block, block)
        f = relax(src, k * block + width, block)[:, :size_y]
        held[span] = jnp.where(labels[span] == 1, f * inverse, 0.0)
        copies.append(pltpu.make_async_copy(held.at[span], out.at[span], sem.at[k]))
        copies[k].start()
    for copy in copies:
        copy.wait()


def swap_even(value, axis):
    return lax.ppermute(value, axis, [(i, i ^ 1) for i in range(lax.axis_size(axis))])


def swap_odd(value, axis):
    count = lax.axis_size(axis)
    up = [(i, i + 1) for i in range(1, count - 1, 2)]
    return lax.ppermute(value, axis, up + [(b, a) for a, b in up])


def partner(value, axis, bit):
    return lax.ppermute(value, axis, [(i, i ^ bit) for i in range(lax.axis_size(axis))])


def doubling(energy, stages):
    other = partner(energy, *stages[0])
    for stage in stages[1:]:
        energy = energy + other
        other = partner(energy, *stage)
    return energy, other


def shards(density, potential, adjoint_start, adjoint_source, labels):
    size_x, size_y, size_z = potential.shape
    _, planes = plane_starts(WIDTHS)
    _, rows = segments(WIDTHS, size_x, beyond=False)
    _, corners = segments(WIDTHS, size_x, beside=False)
    own = [
        pltpu.with_memory_space_constraint(array, pltpu.HBM)
        for array in (density, labels, adjoint_start, adjoint_source, potential)
    ]
    x_bits = [("gx", 1 << k) for k in range(1, (lax.axis_size("gx") - 1).bit_length())]
    y_bits = [("gy", 1 << k) for k in range(1, (lax.axis_size("gy") - 1).bit_length())]

    shape = (size_x, size_y, size_z)
    odd, even, tile_even, tile_odd, *own = pl.pallas_call(
        pack_own,
        out_shape=(f32(planes, size_y, size_z),) * 2 + (f32(rows, size_z),) * 2
        + (f32(*shape), jax.ShapeDtypeStruct(shape, jnp.int32)) + (f32(*shape),) * 3,
        in_specs=[pl.BlockSpec(memory_space=pltpu.HBM)] * 5,
        scratch_shapes=[pltpu.SemaphoreType.DMA((5,))],
        compiler_params=pltpu.CompilerParams(vmem_limit_bytes=VMEM_LIMIT),
    )(*own)
    x_even = swap_even(even, "gx")
    x_odd = swap_odd(odd, "gx")
    y_even = swap_even(tile_even, "gy")
    y_odd = swap_odd(tile_odd, "gy")
    even, odd = call(functools.partial(pack_corners, size_x), (f32(corners, size_z),) * 2)(x_odd, x_even)
    corner_even = swap_even(even, "gy")
    corner_odd = swap_odd(odd, "gy")

    wide = size_y + 2 * RIM

    def room(extra):
        return pltpu.VMEM((size_x + extra, wide, size_z), jnp.float32)

    energy = call(energy_part, f32(8, size_z), [room(2)])(x_odd, x_even, y_even, y_odd, own[0], own[1], own[4])
    mine, other = doubling(energy, y_bits[1:])
    raw = call(
        adjoint_part,
        f32(*shape),
        [room(6), room(6), room(4), room(2), room(5), room(4), room(4), room(4), room(4), room(2)],
        cost=10000000,
    )(x_odd, x_even, y_even, y_odd, corner_even, corner_odd, *own)

    face = f32(FILTER_SWEEPS, size_y, size_z)
    tall = f32(FILTER_SWEEPS + 1, size_y, size_z)
    even, odd, energy = call(pack_raw_x, (tall, face, f32(8, size_z)))(raw, mine, other)
    x_even = swap_even(even, "gx")
    x_odd = swap_odd(odd, "gx")
    energy = energy + x_even[FILTER_SWEEPS, 0:8]
    mine, other = doubling(energy, x_bits)
    _, rows = segments((FILTER_SWEEPS,), size_x)
    even, odd, energy = call(pack_raw_y, (f32(rows + 8, size_z), f32(rows, size_z), f32(8, size_z)))(
        x_odd, x_even, raw, mine, other)
    y_even = swap_even(even, "gy")
    y_odd = swap_odd(odd, "gy")
    energy = energy + y_even[rows:rows + 8]
    mine, other = doubling(energy, y_bits[:1])
    sensitivity, mean_energy = pl.pallas_call(
        filter_part,
        out_shape=(f32(*shape), f32(1, 1)),
        out_specs=(pl.BlockSpec(memory_space=pl.ANY), pl.BlockSpec(memory_space=pltpu.SMEM)),
        scratch_shapes=[room(2 * FILTER_SWEEPS)] * 3 + [pltpu.VMEM(shape, jnp.float32), pltpu.SemaphoreType.DMA((2,))],
        compiler_params=pltpu.CompilerParams(vmem_limit_bytes=VMEM_LIMIT),
    )(x_odd, x_even, y_odd, y_even, raw, own[1], mine, other)
    return (sensitivity, mean_energy[0, 0])


def solution(mesh):
    spec = P("gx", "gy", None)
    return jax.shard_map(
        shards, mesh=mesh, in_specs=(spec,) * 5, out_specs=(spec, P()), check_vma=False
    )
```

```python
import functools

import jax
import jax.numpy as jnp
from jax import lax
from jax.experimental import pallas as pl
from jax.experimental.pallas import tpu as pltpu
from jax.sharding import PartitionSpec as P

ADJ_SWEEPS = 2
FILTER_SWEEPS = 4

eps_void = 1.0
eps_solid = 12.0
eps_back = 4.0
eps_metal = 40.0
screen = 0.5
radius_sq = 2.0
epsilon_mean = 1e-06

WIDTHS = (ADJ_SWEEPS + 1, ADJ_SWEEPS + 1, ADJ_SWEEPS, 1)
RIM = 4
VMEM_LIMIT = 24 * 1024 * 1024


def segments(widths, size_x, beside=True, beyond=True):
    found, at = [], 0
    for field, width in enumerate(widths):
        for x in range(-width, size_x + width):
            rows = width - max(0, -x, x - size_x + 1)
            if rows > 0 and (beside if 0 <= x < size_x else beyond):
                found.append((field, x, rows, at))
                at += rows
    return found, -(-at // 8) * 8


def plane_starts(widths):
    starts, at = [], 0
    for width in widths:
        starts.append(at)
        at += width
    return starts, at


def material(density, labels):
    design = eps_void + density * density * density * (eps_solid - eps_void)
    return jnp.where(labels == 1, design, jnp.where(labels == 2, eps_metal, eps_back))


def call(body, outs, scratch=(), in_specs=None, cost=10000):
    kwargs = {} if in_specs is None else {"in_specs": in_specs, "grid": (1,)}
    return pl.pallas_call(
        body,
        out_shape=outs,
        scratch_shapes=list(scratch),
        compiler_params=pltpu.CompilerParams(vmem_limit_bytes=VMEM_LIMIT),
        cost_estimate=pl.CostEstimate(flops=cost, bytes_accessed=cost, transcendentals=0),
        **kwargs,
    )


def f32(*shape):
    return jax.ShapeDtypeStruct(shape, jnp.float32)


def odd_place(axis):
    return lax.rem(lax.axis_index(axis), 2) == 1


def pack_own(*refs):
    inputs, (x_odd_out, x_even_out, y_even_out, y_odd_out), held, sem = refs[:5], refs[5:9], refs[9:14], refs[14]
    density, labels, adjoint, source, potential = held
    size_x, size_y, _ = density.shape
    starts, _ = plane_starts(WIDTHS)
    copies = [pltpu.make_async_copy(a, b, sem.at[k]) for k, (a, b) in enumerate(zip(inputs, held))]
    for copy in copies:
        copy.start()
    for copy in copies:
        copy.wait()
    low_first = odd_place("gx")
    for out, low in ((x_even_out, low_first), (x_odd_out, jnp.logical_not(low_first))):
        for field, width in enumerate(WIDTHS):
            span = pl.ds(jnp.where(low, 0, size_x - width), width)
            if field == 0:
                face = material(density[span], labels[span])
            else:
                face = (adjoint, source, potential)[field - 1][span]
            out[pl.ds(starts[field], width)] = face
    y_swap = odd_place("gy")
    for field, x, rows, at in segments(WIDTHS, size_x, beyond=False)[0]:
        faces = []
        for rim in (slice(0, rows), slice(size_y - rows, size_y)):
            if field == 0:
                faces.append(material(density[x, rim], labels[x, rim]))
            else:
                faces.append((adjoint, source, potential)[field - 1][x, rim])
        low, high = faces
        y_even_out[at:at + rows] = jnp.where(y_swap, low, high)
        y_odd_out[at:at + rows] = jnp.where(y_swap, high, low)


def pack_corners(size_x, x_odd, x_even, even_out, odd_out):
    size_y = x_odd.shape[1]
    starts, _ = plane_starts(WIDTHS)
    x_swap, y_swap = odd_place("gx"), odd_place("gy")
    for field, x, rows, at in segments(WIDTHS, size_x, beside=False)[0]:
        faces = []
        for rim in (slice(0, rows), slice(size_y - rows, size_y)):
            if x < 0:
                plane = starts[field] + WIDTHS[field] + x
                face = jnp.where(x_swap, x_even[plane, rim], x_odd[plane, rim])
            else:
                plane = starts[field] + x - size_x
                face = jnp.where(x_swap, x_odd[plane, rim], x_even[plane, rim])
            faces.append(face)
        low, high = faces
        even_out[at:at + rows] = jnp.where(y_swap, low, high)
        odd_out[at:at + rows] = jnp.where(y_swap, high, low)


def shift(value, by, axis):
    return pltpu.roll(value, by % value.shape[axis], axis)


def planes_loop(low, high, block, step):
    count = high - low
    block = max(k for k in range(1, block + 1) if count % k == 0)

    def body(k, carry):
        step(low + k * block, block)
        return carry

    lax.fori_loop(0, count // block, body, 0)


def unpack_rows(fields, widths, found, even, odd, size_y):
    wide = size_y + 2 * RIM
    swap = odd_place("gy")
    for field, x, rows, at in found:
        if fields[field] is None:
            continue
        a, b = even[at:at + rows], odd[at:at + rows]
        fields[field][x + widths[field], wide - rows:wide] = jnp.where(swap, a, b)
        fields[field][x + widths[field], size_y:size_y + rows] = jnp.where(swap, b, a)


def unpack_planes(field, width, even, odd, size_x, size_y):
    swap = odd_place("gx")
    tile = pl.ds(0, size_y)
    field[pl.ds(0, width), tile] = jnp.where(swap, even, odd)
    field[pl.ds(width + size_x, width), tile] = jnp.where(swap, odd, even)


def energy_part(x_odd, x_even, y_even, y_odd, density, labels, potential, energy_out, poten):
    size_x, size_y, size_z = density.shape
    starts, planes = plane_starts(WIDTHS)
    planes_loop(0, size_x, 4, lambda x, n: poten.__setitem__((pl.ds(x + 1, n), pl.ds(0, size_y)), potential[pl.ds(x, n)]))
    span = pl.ds(starts[3], 1)
    unpack_planes(poten, 1, x_even[span], x_odd[span], size_x, size_y)
    found, _ = segments(WIDTHS, size_x, beyond=False)
    unpack_rows((None, None, None, poten), WIDTHS, found, y_even, y_odd, size_y)
    wide = size_y + 2 * RIM
    lane = lax.broadcasted_iota(jnp.int32, (1, wide, size_z), 2)
    is_first = lane == 0
    is_last = lane == size_z - 1
    energy_out[...] = jnp.zeros_like(energy_out)

    def step(x, n):
        span = pl.ds(x, n)
        v = poten[pl.ds(x + 1, n)]
        low, high = poten[pl.ds(x, n)] - v, poten[pl.ds(x + 2, n)] - v
        squares = low * low + high * high
        dv = shift(v, -1, 1) - v
        square = dv * dv
        squares = squares + square + shift(square, 1, 1)
        dv = jnp.where(is_last, 0.0, shift(v, -1, 2)) - v
        square = dv * dv
        squares = squares + square + jnp.where(is_first, v * v, shift(square, 1, 2))
        energy = material(density[span], labels[span]) * squares[:, :size_y]
        energy_out[...] += jnp.sum(energy.reshape(-1, 8, size_z), axis=0)

    planes_loop(0, size_x, 4, step)


def adjoint_part(x_odd, x_even, y_even, y_odd, corner_even, corner_odd, density, labels, adjoint_start, adjoint_source, potential,
                 raw_out,
                 permit, start, source, poten, face_x, face_y, face_z, inverse, first, second):
    size_x, size_y, size_z = density.shape
    starts, _ = plane_starts(WIDTHS)
    fields = (permit, start, source, poten)
    tile = pl.ds(0, size_y)

    def fill(x, n):
        span = pl.ds(x, n)
        permit[pl.ds(x + WIDTHS[0], n), tile] = material(density[span], labels[span])
        start[pl.ds(x + WIDTHS[1], n), tile] = adjoint_start[span]
        source[pl.ds(x + WIDTHS[2], n), tile] = adjoint_source[span]
        poten[pl.ds(x + WIDTHS[3], n), tile] = potential[span]

    planes_loop(0, size_x, 4, fill)
    for field, width in enumerate(WIDTHS):
        span = pl.ds(starts[field], width)
        unpack_planes(fields[field], width, x_even[span], x_odd[span], size_x, size_y)
    unpack_rows(fields, WIDTHS, segments(WIDTHS, size_x, beyond=False)[0], y_even, y_odd, size_y)
    unpack_rows(fields, WIDTHS, segments(WIDTHS, size_x, beside=False)[0], corner_even, corner_odd, size_y)

    wide = size_y + 2 * RIM
    lane = lax.broadcasted_iota(jnp.int32, (1, wide, size_z), 2)
    is_first = lane == 0
    is_last = lane == size_z - 1

    def harmonic(a, b):
        return 2.0 * a * b / jnp.maximum(a + b, 0.25)

    def faces_x(x, n):
        face_x[pl.ds(x, n)] = harmonic(permit[pl.ds(x, n)], permit[pl.ds(x + 1, n)])

    planes_loop(0, size_x + 5, 7, faces_x)

    def weigh(x, n):
        span = pl.ds(x, n)
        p = permit[pl.ds(x + 1, n)]
        fy = harmonic(p, shift(p, -1, 1))
        fz = jnp.where(is_last, 0.0, harmonic(p, shift(p, -1, 2)))
        face_y[span] = fy
        face_z[span] = fz
        total = screen + face_x[span] + face_x[pl.ds(x + 1, n)] + fy + shift(fy, 1, 1) + fz + shift(fz, 1, 2)
        inverse[span] = jnp.where(p > 20.0, 0.0, 1.0 / total)

    planes_loop(0, size_x + 4, 5, weigh)

    def relax(x, n, a, a_low, a_high):
        span = pl.ds(x, n)
        fy, fz = face_y[span], face_z[span]
        total = source[span] + face_x[pl.ds(x + 1, n)] * a_high + face_x[span] * a_low
        total = total + fy * shift(a, -1, 1) + shift(fy * a, 1, 1)
        total = total + fz * shift(a, -1, 2) + shift(fz * a, 1, 2)
        return total * inverse[span]

    def sweep_one(x, n):
        first[pl.ds(x, n)] = relax(x, n, start[pl.ds(x + 1, n)], start[pl.ds(x, n)], start[pl.ds(x + 2, n)])

    planes_loop(0, size_x + 4, 10, sweep_one)

    def sweep_two(x, n):
        second[pl.ds(x, n)] = relax(x + 1, n, first[pl.ds(x + 1, n)], first[pl.ds(x, n)], first[pl.ds(x + 2, n)])

    planes_loop(0, size_x + 2, 9, sweep_two)

    def finish(x, n):
        span = pl.ds(x, n)
        v, a = poten[pl.ds(x + 1, n)], second[pl.ds(x + 1, n)]
        product = (poten[pl.ds(x, n)] - v) * (second[pl.ds(x, n)] - a)
        product = product + (poten[pl.ds(x + 2, n)] - v) * (second[pl.ds(x + 2, n)] - a)
        both = (shift(v, -1, 1) - v) * (shift(a, -1, 1) - a)
        product = product + both + shift(both, 1, 1)
        both = (jnp.where(is_last, 0.0, shift(v, -1, 2)) - v) * (jnp.where(is_last, 0.0, shift(a, -1, 2)) - a)
        product = product + both + jnp.where(is_first, v * a, shift(both, 1, 2))
        d = density[span]
        gain = jnp.where(labels[span] == 1, -1.5 * (eps_solid - eps_void) * d * d, 0.0)
        raw_out[span] = gain * product[:, :size_y]

    planes_loop(0, size_x, 8, finish)


def pack_raw_x(raw, mine, other, even_out, odd_out, energy_out):
    size_x = raw.shape[0]
    energy_out[...] = mine[...] + other[...]
    low_first = odd_place("gx")
    for out, low in ((even_out, low_first), (odd_out, jnp.logical_not(low_first))):
        out[...] = raw[pl.ds(jnp.where(low, 0, size_x - FILTER_SWEEPS), FILTER_SWEEPS)]


def pack_raw_y(x_odd, x_even, raw, mine, other, even_out, odd_out, energy_out):
    size_x, size_y, _ = raw.shape
    width = FILTER_SWEEPS
    found, total = segments((width,), size_x)
    x_swap, y_swap = odd_place("gx"), odd_place("gy")
    energy = mine[...] + other[...]
    energy_out[...] = energy
    even_out[total:total + 8] = energy
    for _, x, rows, at in found:
        faces = []
        for rim in (slice(0, rows), slice(size_y - rows, size_y)):
            if x < 0:
                face = jnp.where(x_swap, x_even[width + x, rim], x_odd[width + x, rim])
            elif x >= size_x:
                face = jnp.where(x_swap, x_odd[x - size_x, rim], x_even[x - size_x, rim])
            else:
                face = raw[x, rim]
            faces.append(face)
        low, high = faces
        even_out[at:at + rows] = jnp.where(y_swap, low, high)
        odd_out[at:at + rows] = jnp.where(y_swap, high, low)


def relaxation(raw, size_x, size_y, size_z):
    width = FILTER_SWEEPS
    wide = size_y + 2 * RIM
    extent_x = lax.axis_size("gx") * size_x
    extent_y = lax.axis_size("gy") * size_y
    base_x = lax.axis_index("gx") * size_x - width
    lane = lax.broadcasted_iota(jnp.int32, (1, wide, size_z), 2)
    row = lax.broadcasted_iota(jnp.int32, (1, wide, size_z), 1)
    place = lax.axis_index("gy") * size_y + jnp.where(row < size_y + RIM, row, row - wide)
    is_first, is_last = lane == 0, lane == size_z - 1

    def edges(at, extent):
        return jnp.where(at > 0, 1.0, 0.0) + jnp.where(at < extent - 1, 1.0, 0.0)

    count = edges(place, extent_y) + edges(lane, size_z)
    inside = (place >= 0) & (place < extent_y)
    scale_two = jnp.where(inside, 1.0 / (1.0 + radius_sq * (count + 2.0)), 0.0)
    scale_one = jnp.where(inside, 1.0 / (1.0 + radius_sq * (count + 1.0)), 0.0)

    def relax(src, x, n):
        f = src[pl.ds(x, n)]
        near = src[pl.ds(x - 1, n)] + src[pl.ds(x + 1, n)] + shift(f, 1, 1) + shift(f, -1, 1)
        near = near + jnp.where(is_first, 0.0, shift(f, 1, 2)) + jnp.where(is_last, 0.0, shift(f, -1, 2))
        total = raw[pl.ds(x, n)] + radius_sq * near
        scaled = []
        for k in range(n):
            at = base_x + x + k
            outside = (at < 0) | (at >= extent_x)
            border = (at == 0) | (at == extent_x - 1)
            scale = jnp.where(outside, 0.0, jnp.where(border, scale_one, scale_two))
            scaled.append(total[k:k + 1] * scale)
        return jnp.concatenate(scaled, axis=0)

    return relax


def filter_first(x_odd, x_even, y_odd, y_even, raw_in, raw, odd, even):
    size_x, size_y, size_z = raw_in.shape
    width = FILTER_SWEEPS
    tile = pl.ds(0, size_y)

    def fill(x, n):
        raw[pl.ds(x + width, n), tile] = raw_in[pl.ds(x, n)]

    planes_loop(0, size_x, 4, fill)
    unpack_planes(raw, width, x_even[...], x_odd[...], size_x, size_y)
    unpack_rows((raw,), (width,), segments((width,), size_x)[0], y_even, y_odd, size_y)
    relax = relaxation(raw, size_x, size_y, size_z)
    src = raw
    for sweep in range(FILTER_SWEEPS - 1):
        dst = (odd, even)[(FILTER_SWEEPS - sweep) % 2]

        def step(x, n, src=src, dst=dst):
            dst[pl.ds(x, n)] = relax(src, x, n)

        planes_loop(sweep + 1, size_x + 2 * width - sweep - 1, 11, step)
        src = dst


def filter_last(raw, src, labels, mine, other, out, mean_out, held, sem):
    size_x, size_y, size_z = labels.shape
    relax = relaxation(raw, size_x, size_y, size_z)
    voxels = lax.axis_size("gx") * size_x * lax.axis_size("gy") * size_y * size_z
    mean = 0.5 * jnp.sum(mine[...] + other[...]) / voxels + epsilon_mean
    mean_out[0, 0] = mean
    inverse = 1.0 / jnp.full((1, 1, size_z), mean, jnp.float32)
    block = size_x // 2
    copies = []
    for k in range(2):
        span = pl.ds(k * block, block)
        f = relax(src, k * block + FILTER_SWEEPS, block)[:, :size_y]
        held[span] = jnp.where(labels[span] == 1, f * inverse, 0.0)
        copies.append(pltpu.make_async_copy(held.at[span], out.at[span], sem.at[k]))
        copies[k].start()
    for copy in copies:
        copy.wait()


def swap_even(value, axis):
    return lax.ppermute(value, axis, [(i, i ^ 1) for i in range(lax.axis_size(axis))])


def swap_odd(value, axis):
    count = lax.axis_size(axis)
    up = [(i, i + 1) for i in range(1, count - 1, 2)]
    return lax.ppermute(value, axis, up + [(b, a) for a, b in up])


def partner(value, axis, bit):
    return lax.ppermute(value, axis, [(i, i ^ bit) for i in range(lax.axis_size(axis))])


def doubling(energy, stages):
    other = partner(energy, *stages[0])
    for stage in stages[1:]:
        energy = energy + other
        other = partner(energy, *stage)
    return energy, other


def shards(density, potential, adjoint_start, adjoint_source, labels):
    size_x, size_y, size_z = potential.shape
    _, planes = plane_starts(WIDTHS)
    _, rows = segments(WIDTHS, size_x, beyond=False)
    _, corners = segments(WIDTHS, size_x, beside=False)
    own = [
        pltpu.with_memory_space_constraint(array, pltpu.HBM)
        for array in (density, labels, adjoint_start, adjoint_source, potential)
    ]
    x_bits = [("gx", 1 << k) for k in range(1, (lax.axis_size("gx") - 1).bit_length())]
    y_bits = [("gy", 1 << k) for k in range(1, (lax.axis_size("gy") - 1).bit_length())]

    shape = (size_x, size_y, size_z)
    odd, even, tile_even, tile_odd, *own = pl.pallas_call(
        pack_own,
        out_shape=(f32(planes, size_y, size_z),) * 2 + (f32(rows, size_z),) * 2
        + (f32(*shape), jax.ShapeDtypeStruct(shape, jnp.int32)) + (f32(*shape),) * 3,
        in_specs=[pl.BlockSpec(memory_space=pltpu.HBM)] * 5,
        scratch_shapes=[pltpu.SemaphoreType.DMA((5,))],
        compiler_params=pltpu.CompilerParams(vmem_limit_bytes=VMEM_LIMIT),
    )(*own)
    x_even = swap_even(even, "gx")
    x_odd = swap_odd(odd, "gx")
    y_even = swap_even(tile_even, "gy")
    y_odd = swap_odd(tile_odd, "gy")
    even, odd = call(functools.partial(pack_corners, size_x), (f32(corners, size_z),) * 2)(x_odd, x_even)
    corner_even = swap_even(even, "gy")
    corner_odd = swap_odd(odd, "gy")

    wide = size_y + 2 * RIM

    def room(extra):
        return pltpu.VMEM((size_x + extra, wide, size_z), jnp.float32)

    energy = call(energy_part, f32(8, size_z), [room(2)])(x_odd, x_even, y_even, y_odd, own[0], own[1], own[4])
    mine, other = doubling(energy, y_bits[1:])
    raw = call(
        adjoint_part,
        f32(*shape),
        [room(6), room(6), room(4), room(2), room(5), room(4), room(4), room(4), room(4), room(2)],
        cost=10000000,
    )(x_odd, x_even, y_even, y_odd, corner_even, corner_odd, *own)

    face = f32(FILTER_SWEEPS, size_y, size_z)
    raw = call(
        adjoint_part,
        f32(*shape),
        [room(6), room(6), room(4), room(2), room(5), room(4), room(4), room(4), room(4), room(2)],
        cost=10000000,
    )(x_odd, x_even, y_even, y_odd, corner_even, corner_odd, *own)

    even, odd, energy = call(pack_raw_x, (face, face, f32(8, size_z)))(raw, mine, other)
    x_even = swap_even(even, "gx")
    x_odd = swap_odd(odd, "gx")
    mine, other = doubling(energy, x_bits)
    _, rows = segments((FILTER_SWEEPS,), size_x)
    even, odd, energy = call(pack_raw_y, (f32(rows + 8, size_z), f32(rows, size_z), f32(8, size_z)))(
        x_odd, x_even, raw, mine, other)
    y_even = swap_even(even, "gy")
    y_odd = swap_odd(odd, "gy")
    energy = energy + y_even[rows:rows + 8]
    mine, other = doubling(energy, y_bits[:1] + [("gx", 1)])
    padded = f32(size_x + 2 * FILTER_SWEEPS, wide, size_z)
    raw, filtered = call(
        filter_first,
        (padded, padded),
        [pltpu.VMEM(padded.shape, jnp.float32)],
        cost=10000000,
    )(x_odd, x_even, y_odd, y_even, raw)
    sensitivity, mean_energy = pl.pallas_call(
        filter_last,
        out_shape=(f32(*shape), f32(1, 1)),
        out_specs=(pl.BlockSpec(memory_space=pl.ANY), pl.BlockSpec(memory_space=pltpu.SMEM)),
        scratch_shapes=[pltpu.VMEM(shape, jnp.float32), pltpu.SemaphoreType.DMA((2,))],
        compiler_params=pltpu.CompilerParams(vmem_limit_bytes=VMEM_LIMIT),
    )(raw, filtered, own[1], mine, other)
    return (sensitivity, mean_energy[0, 0])


def solution(mesh):
    spec = P("gx", "gy", None)
    return jax.shard_map(
        shards, mesh=mesh, in_specs=(spec,) * 5, out_specs=(spec, P()), check_vma=False
    )
```

```python
import functools

import jax
import jax.numpy as jnp
from jax import lax
from jax.experimental import pallas as pl
from jax.experimental.pallas import tpu as pltpu
from jax.sharding import PartitionSpec as P

ADJ_SWEEPS = 2
FILTER_SWEEPS = 4

eps_void = 1.0
eps_solid = 12.0
eps_back = 4.0
eps_metal = 40.0
screen = 0.5
radius_sq = 2.0
epsilon_mean = 1e-06

WIDTHS = (ADJ_SWEEPS + 1, ADJ_SWEEPS + 1, ADJ_SWEEPS, 1)
RIM = 4
VMEM_LIMIT = 24 * 1024 * 1024


def segments(widths, size_x, beside=True, beyond=True):
    found, at = [], 0
    for field, width in enumerate(widths):
        for x in range(-width, size_x + width):
            rows = width - max(0, -x, x - size_x + 1)
            if rows > 0 and (beside if 0 <= x < size_x else beyond):
                found.append((field, x, rows, at))
                at += rows
    return found, -(-at // 8) * 8


def plane_starts(widths):
    starts, at = [], 0
    for width in widths:
        starts.append(at)
        at += width
    return starts, at


def material(density, labels):
    design = eps_void + density * density * density * (eps_solid - eps_void)
    return jnp.where(labels == 1, design, jnp.where(labels == 2, eps_metal, eps_back))


def call(body, outs, scratch=(), in_specs=None, cost=10000):
    kwargs = {} if in_specs is None else {"in_specs": in_specs, "grid": (1,)}
    return pl.pallas_call(
        body,
        out_shape=outs,
        scratch_shapes=list(scratch),
        compiler_params=pltpu.CompilerParams(vmem_limit_bytes=VMEM_LIMIT),
        cost_estimate=pl.CostEstimate(flops=cost, bytes_accessed=cost, transcendentals=0),
        **kwargs,
    )


def f32(*shape):
    return jax.ShapeDtypeStruct(shape, jnp.float32)


def odd_place(axis):
    return lax.rem(lax.axis_index(axis), 2) == 1


def pack_own(*refs):
    inputs, (x_odd_out, x_even_out, y_even_out, y_odd_out), held, sem = refs[:5], refs[5:9], refs[9:14], refs[14]
    density, labels, adjoint, source, potential = held
    size_x, size_y, _ = density.shape
    starts, _ = plane_starts(WIDTHS)
    copies = [pltpu.make_async_copy(a, b, sem.at[k]) for k, (a, b) in enumerate(zip(inputs, held))]
    for copy in copies:
        copy.start()
    for copy in copies:
        copy.wait()
    low_first = odd_place("gx")
    for out, low in ((x_even_out, low_first), (x_odd_out, jnp.logical_not(low_first))):
        for field, width in enumerate(WIDTHS):
            span = pl.ds(jnp.where(low, 0, size_x - width), width)
            if field == 0:
                face = material(density[span], labels[span])
            else:
                face = (adjoint, source, potential)[field - 1][span]
            out[pl.ds(starts[field], width)] = face
    y_swap = odd_place("gy")
    for field, x, rows, at in segments(WIDTHS, size_x, beyond=False)[0]:
        faces = []
        for rim in (slice(0, rows), slice(size_y - rows, size_y)):
            if field == 0:
                faces.append(material(density[x, rim], labels[x, rim]))
            else:
                faces.append((adjoint, source, potential)[field - 1][x, rim])
        low, high = faces
        y_even_out[at:at + rows] = jnp.where(y_swap, low, high)
        y_odd_out[at:at + rows] = jnp.where(y_swap, high, low)


def pack_corners(size_x, x_odd, x_even, even_out, odd_out):
    size_y = x_odd.shape[1]
    starts, _ = plane_starts(WIDTHS)
    x_swap, y_swap = odd_place("gx"), odd_place("gy")
    for field, x, rows, at in segments(WIDTHS, size_x, beside=False)[0]:
        faces = []
        for rim in (slice(0, rows), slice(size_y - rows, size_y)):
            if x < 0:
                plane = starts[field] + WIDTHS[field] + x
                face = jnp.where(x_swap, x_even[plane, rim], x_odd[plane, rim])
            else:
                plane = starts[field] + x - size_x
                face = jnp.where(x_swap, x_odd[plane, rim], x_even[plane, rim])
            faces.append(face)
        low, high = faces
        even_out[at:at + rows] = jnp.where(y_swap, low, high)
        odd_out[at:at + rows] = jnp.where(y_swap, high, low)


def shift(value, by, axis):
    return pltpu.roll(value, by % value.shape[axis], axis)


def planes_loop(low, high, block, step):
    count = high - low
    block = max(k for k in range(1, block + 1) if count % k == 0)

    def body(k, carry):
        step(low + k * block, block)
        return carry

    lax.fori_loop(0, count // block, body, 0)


def unpack_rows(fields, widths, found, even, odd, size_y):
    wide = size_y + 2 * RIM
    swap = odd_place("gy")
    for field, x, rows, at in found:
        if fields[field] is None:
            continue
        a, b = even[at:at + rows], odd[at:at + rows]
        fields[field][x + widths[field], wide - rows:wide] = jnp.where(swap, a, b)
        fields[field][x + widths[field], size_y:size_y + rows] = jnp.where(swap, b, a)


def unpack_planes(field, width, even, odd, size_x, size_y):
    swap = odd_place("gx")
    tile = pl.ds(0, size_y)
    field[pl.ds(0, width), tile] = jnp.where(swap, even, odd)
    field[pl.ds(width + size_x, width), tile] = jnp.where(swap, odd, even)


def energy_part(x_odd, x_even, y_odd, y_even, density, labels, potential, energy_out, poten):
    size_x, size_y, size_z = density.shape
    starts, planes = plane_starts(WIDTHS)
    planes_loop(0, size_x, 4, lambda x, n: poten.__setitem__((pl.ds(x + 1, n), pl.ds(0, size_y)), potential[pl.ds(x, n)]))
    span = pl.ds(starts[3], 1)
    unpack_planes(poten, 1, x_even[span], x_odd[span], size_x, size_y)
    found, _ = segments(WIDTHS, size_x, beyond=False)
    unpack_rows((None, None, None, poten), WIDTHS, found, y_even, y_odd, size_y)
    wide = size_y + 2 * RIM
    lane = lax.broadcasted_iota(jnp.int32, (1, wide, size_z), 2)
    is_first = lane == 0
    is_last = lane == size_z - 1
    energy_out[...] = jnp.zeros_like(energy_out)

    def step(x, n):
        span = pl.ds(x, n)
        v = poten[pl.ds(x + 1, n)]
        low, high = poten[pl.ds(x, n)] - v, poten[pl.ds(x + 2, n)] - v
        squares = low * low + high * high
        dv = shift(v, -1, 1) - v
        square = dv * dv
        squares = squares + square + shift(square, 1, 1)
        dv = jnp.where(is_last, 0.0, shift(v, -1, 2)) - v
        square = dv * dv
        squares = squares + square + jnp.where(is_first, v * v, shift(square, 1, 2))
        energy = material(density[span], labels[span]) * squares[:, :size_y]
        energy_out[...] += jnp.sum(energy.reshape(-1, 8, size_z), axis=0)

    planes_loop(0, size_x, 4, step)


def adjoint_part(x_odd, x_even, y_odd, y_even, corner_odd, corner_even, density, labels, adjoint_start, adjoint_source, potential,
                 raw_out,
                 permit, start, source, poten, face_x, face_y, face_z, inverse, first, second):
    size_x, size_y, size_z = density.shape
    starts, _ = plane_starts(WIDTHS)
    fields = (permit, start, source, poten)
    tile = pl.ds(0, size_y)

    def fill(x, n):
        span = pl.ds(x, n)
        permit[pl.ds(x + WIDTHS[0], n), tile] = material(density[span], labels[span])
        start[pl.ds(x + WIDTHS[1], n), tile] = adjoint_start[span]
        source[pl.ds(x + WIDTHS[2], n), tile] = adjoint_source[span]
        poten[pl.ds(x + WIDTHS[3], n), tile] = potential[span]

    planes_loop(0, size_x, 4, fill)
    for field, width in enumerate(WIDTHS):
        span = pl.ds(starts[field], width)
        unpack_planes(fields[field], width, x_even[span], x_odd[span], size_x, size_y)
    unpack_rows(fields, WIDTHS, segments(WIDTHS, size_x, beyond=False)[0], y_even, y_odd, size_y)
    unpack_rows(fields, WIDTHS, segments(WIDTHS, size_x, beside=False)[0], corner_even, corner_odd, size_y)

    wide = size_y + 2 * RIM
    lane = lax.broadcasted_iota(jnp.int32, (1, wide, size_z), 2)
    is_first = lane == 0
    is_last = lane == size_z - 1

    def harmonic(a, b):
        return 2.0 * a * b / jnp.maximum(a + b, 0.25)

    def faces_x(x, n):
        face_x[pl.ds(x, n)] = harmonic(permit[pl.ds(x, n)], permit[pl.ds(x + 1, n)])

    planes_loop(0, size_x + 5, 7, faces_x)

    def weigh(x, n):
        span = pl.ds(x, n)
        p = permit[pl.ds(x + 1, n)]
        fy = harmonic(p, shift(p, -1, 1))
        fz = jnp.where(is_last, 0.0, harmonic(p, shift(p, -1, 2)))
        face_y[span] = fy
        face_z[span] = fz
        total = screen + face_x[span] + face_x[pl.ds(x + 1, n)] + fy + shift(fy, 1, 1) + fz + shift(fz, 1, 2)
        inverse[span] = jnp.where(p > 20.0, 0.0, 1.0 / total)

    planes_loop(0, size_x + 4, 5, weigh)

    def relax(x, n, a, a_low, a_high):
        span = pl.ds(x, n)
        fy, fz = face_y[span], face_z[span]
        total = source[span] + face_x[pl.ds(x + 1, n)] * a_high + face_x[span] * a_low
        total = total + fy * shift(a, -1, 1) + shift(fy * a, 1, 1)
        total = total + fz * shift(a, -1, 2) + shift(fz * a, 1, 2)
        return total * inverse[span]

    def sweep_one(x, n):
        first[pl.ds(x, n)] = relax(x, n, start[pl.ds(x + 1, n)], start[pl.ds(x, n)], start[pl.ds(x + 2, n)])

    planes_loop(0, size_x + 4, 10, sweep_one)

    def sweep_two(x, n):
        second[pl.ds(x, n)] = relax(x + 1, n, first[pl.ds(x + 1, n)], first[pl.ds(x, n)], first[pl.ds(x + 2, n)])

    planes_loop(0, size_x + 2, 9, sweep_two)

    def finish(x, n):
        span = pl.ds(x, n)
        v, a = poten[pl.ds(x + 1, n)], second[pl.ds(x + 1, n)]
        product = (poten[pl.ds(x, n)] - v) * (second[pl.ds(x, n)] - a)
        product = product + (poten[pl.ds(x + 2, n)] - v) * (second[pl.ds(x + 2, n)] - a)
        both = (shift(v, -1, 1) - v) * (shift(a, -1, 1) - a)
        product = product + both + shift(both, 1, 1)
        both = (jnp.where(is_last, 0.0, shift(v, -1, 2)) - v) * (jnp.where(is_last, 0.0, shift(a, -1, 2)) - a)
        product = product + both + jnp.where(is_first, v * a, shift(both, 1, 2))
        d = density[span]
        gain = jnp.where(labels[span] == 1, -1.5 * (eps_solid - eps_void) * d * d, 0.0)
        raw_out[span] = gain * product[:, :size_y]

    planes_loop(0, size_x, 8, finish)


def pack_raw_x(raw, mine, other, even_out, odd_out, energy_out):
    size_x = raw.shape[0]
    energy_out[...] = mine[...] + other[...]
    low_first = odd_place("gx")
    for out, low in ((even_out, low_first), (odd_out, jnp.logical_not(low_first))):
        out[...] = raw[pl.ds(jnp.where(low, 0, size_x - FILTER_SWEEPS), FILTER_SWEEPS)]


def pack_raw_y(x_odd, x_even, raw, mine, other, even_out, odd_out, energy_out):
    size_x, size_y, _ = raw.shape
    width = FILTER_SWEEPS
    found, total = segments((width,), size_x)
    x_swap, y_swap = odd_place("gx"), odd_place("gy")
    energy = mine[...] + other[...]
    energy_out[...] = energy
    even_out[total:total + 8] = energy
    for _, x, rows, at in found:
        faces = []
        for rim in (slice(0, rows), slice(size_y - rows, size_y)):
            if x < 0:
                face = jnp.where(x_swap, x_even[width + x, rim], x_odd[width + x, rim])
            elif x >= size_x:
                face = jnp.where(x_swap, x_odd[x - size_x, rim], x_even[x - size_x, rim])
            else:
                face = raw[x, rim]
            faces.append(face)
        low, high = faces
        even_out[at:at + rows] = jnp.where(y_swap, low, high)
        odd_out[at:at + rows] = jnp.where(y_swap, high, low)


def relaxation(raw, size_x, size_y, size_z):
    width = FILTER_SWEEPS
    wide = size_y + 2 * RIM
    extent_x = lax.axis_size("gx") * size_x
    extent_y = lax.axis_size("gy") * size_y
    base_x = lax.axis_index("gx") * size_x - width
    lane = lax.broadcasted_iota(jnp.int32, (1, wide, size_z), 2)
    row = lax.broadcasted_iota(jnp.int32, (1, wide, size_z), 1)
    place = lax.axis_index("gy") * size_y + jnp.where(row < size_y + RIM, row, row - wide)
    is_first, is_last = lane == 0, lane == size_z - 1

    def edges(at, extent):
        return jnp.where(at > 0, 1.0, 0.0) + jnp.where(at < extent - 1, 1.0, 0.0)

    count = edges(place, extent_y) + edges(lane, size_z)
    inside = (place >= 0) & (place < extent_y)
    scale_two = jnp.where(inside, 1.0 / (1.0 + radius_sq * (count + 2.0)), 0.0)
    scale_one = jnp.where(inside, 1.0 / (1.0 + radius_sq * (count + 1.0)), 0.0)

    def relax(src, x, n):
        f = src[pl.ds(x, n)]
        near = src[pl.ds(x - 1, n)] + src[pl.ds(x + 1, n)] + shift(f, 1, 1) + shift(f, -1, 1)
        near = near + jnp.where(is_first, 0.0, shift(f, 1, 2)) + jnp.where(is_last, 0.0, shift(f, -1, 2))
        total = raw[pl.ds(x, n)] + radius_sq * near
        scaled = []
        for k in range(n):
            at = base_x + x + k
            outside = (at < 0) | (at >= extent_x)
            border = (at == 0) | (at == extent_x - 1)
            scale = jnp.where(outside, 0.0, jnp.where(border, scale_one, scale_two))
            scaled.append(total[k:k + 1] * scale)
        return jnp.concatenate(scaled, axis=0)

    return relax


def filter_first(x_odd, x_even, y_odd, y_even, raw_in, raw, odd, even):
    size_x, size_y, size_z = raw_in.shape
    width = FILTER_SWEEPS
    tile = pl.ds(0, size_y)

    def fill(x, n):
        raw[pl.ds(x + width, n), tile] = raw_in[pl.ds(x, n)]

    planes_loop(0, size_x, 4, fill)
    unpack_planes(raw, width, x_even[...], x_odd[...], size_x, size_y)
    unpack_rows((raw,), (width,), segments((width,), size_x)[0], y_even, y_odd, size_y)
    relax = relaxation(raw, size_x, size_y, size_z)
    src = raw
    for sweep in range(FILTER_SWEEPS - 1):
        dst = (odd, even)[(FILTER_SWEEPS - sweep) % 2]

        def step(x, n, src=src, dst=dst):
            dst[pl.ds(x, n)] = relax(src, x, n)

        planes_loop(sweep + 1, size_x + 2 * width - sweep - 1, 11, step)
        src = dst


def filter_last(raw, src, labels, mine, other, out, mean_out, held, sem):
    size_x, size_y, size_z = labels.shape
    relax = relaxation(raw, size_x, size_y, size_z)
    voxels = lax.axis_size("gx") * size_x * lax.axis_size("gy") * size_y * size_z
    mean = 0.5 * jnp.sum(mine[...] + other[...]) / voxels + epsilon_mean
    mean_out[0, 0] = mean
    inverse = 1.0 / jnp.full((1, 1, size_z), mean, jnp.float32)
    block = size_x // 2
    copies = []
    for k in range(2):
        span = pl.ds(k * block, block)
        f = relax(src, k * block + FILTER_SWEEPS, block)[:, :size_y]
        held[span] = jnp.where(labels[span] == 1, f * inverse, 0.0)
        copies.append(pltpu.make_async_copy(held.at[span], out.at[span], sem.at[k]))
        copies[k].start()
    for copy in copies:
        copy.wait()


def swap_even(value, axis):
    return lax.ppermute(value, axis, [(i, i ^ 1) for i in range(lax.axis_size(axis))])


def swap_odd(value, axis):
    count = lax.axis_size(axis)
    up = [(i, i + 1) for i in range(1, count - 1, 2)]
    return lax.ppermute(value, axis, up + [(b, a) for a, b in up])


def partner(value, axis, bit):
    return lax.ppermute(value, axis, [(i, i ^ bit) for i in range(lax.axis_size(axis))])


def doubling(energy, stages):
    other = partner(energy, *stages[0])
    for stage in stages[1:]:
        energy = energy + other
        other = partner(energy, *stage)
    return energy, other


def shards(density, potential, adjoint_start, adjoint_source, labels):
    size_x, size_y, size_z = potential.shape
    _, planes = plane_starts(WIDTHS)
    _, rows = segments(WIDTHS, size_x, beyond=False)
    _, corners = segments(WIDTHS, size_x, beside=False)
    own = [
        pltpu.with_memory_space_constraint(array, pltpu.HBM)
        for array in (density, labels, adjoint_start, adjoint_source, potential)
    ]
    x_bits = [("gx", 1 << k) for k in range(1, (lax.axis_size("gx") - 1).bit_length())]
    y_bits = [("gy", 1 << k) for k in range(1, (lax.axis_size("gy") - 1).bit_length())]

    shape = (size_x, size_y, size_z)
    odd, even, tile_even, tile_odd, *own = pl.pallas_call(
        pack_own,
        out_shape=(f32(planes, size_y, size_z),) * 2 + (f32(rows, size_z),) * 2
        + (f32(*shape), jax.ShapeDtypeStruct(shape, jnp.int32)) + (f32(*shape),) * 3,
        in_specs=[pl.BlockSpec(memory_space=pltpu.HBM)] * 5,
        scratch_shapes=[pltpu.SemaphoreType.DMA((5,))],
        compiler_params=pltpu.CompilerParams(vmem_limit_bytes=VMEM_LIMIT),
    )(*own)
    x_even = swap_even(even, "gx")
    x_odd = swap_odd(odd, "gx")
    y_even = swap_even(tile_even, "gy")
    y_odd = swap_odd(tile_odd, "gy")
    even, odd = call(functools.partial(pack_corners, size_x), (f32(corners, size_z),) * 2)(x_odd, x_even)
    corner_even = swap_even(even, "gy")
    corner_odd = swap_odd(odd, "gy")

    wide = size_y + 2 * RIM

    def room(extra):
        return pltpu.VMEM((size_x + extra, wide, size_z), jnp.float32)

    energy = call(energy_part, f32(8, size_z), [room(2)])(x_odd, x_even, y_odd, y_even, own[0], own[1], own[4])
    mine, other = doubling(energy, y_bits[1:])
    face = f32(FILTER_SWEEPS, size_y, size_z)
    raw = call(
        adjoint_part,
        f32(*shape),
        [room(6), room(6), room(4), room(2), room(5), room(4), room(4), room(4), room(4), room(2)],
        cost=10000000,
    )(x_odd, x_even, y_odd, y_even, corner_odd, corner_even, *own)

    even, odd, energy = call(pack_raw_x, (face, face, f32(8, size_z)))(raw, mine, other)
    x_even = swap_even(even, "gx")
    x_odd = swap_odd(odd, "gx")
    mine, other = doubling(energy, x_bits)
    _, rows = segments((FILTER_SWEEPS,), size_x)
    even, odd, energy = call(pack_raw_y, (f32(rows + 8, size_z), f32(rows, size_z), f32(8, size_z)))(
        x_odd, x_even, raw, mine, other)
    y_even = swap_even(even, "gy")
    y_odd = swap_odd(odd, "gy")
    energy = energy + y_even[rows:rows + 8]
    mine, other = doubling(energy, y_bits[:1] + [("gx", 1)])
    padded = f32(size_x + 2 * FILTER_SWEEPS, wide, size_z)
    raw, filtered = call(
        filter_first,
        (padded, padded),
        [pltpu.VMEM(padded.shape, jnp.float32)],
        cost=10000000,
    )(x_odd, x_even, y_odd, y_even, raw)
    sensitivity, mean_energy = pl.pallas_call(
        filter_last,
        out_shape=(f32(*shape), f32(1, 1)),
        out_specs=(pl.BlockSpec(memory_space=pl.ANY), pl.BlockSpec(memory_space=pltpu.SMEM)),
        scratch_shapes=[pltpu.VMEM(shape, jnp.float32), pltpu.SemaphoreType.DMA((2,))],
        compiler_params=pltpu.CompilerParams(vmem_limit_bytes=VMEM_LIMIT),
    )(raw, filtered, own[1], mine, other)
    return (sensitivity, mean_energy[0, 0])


def solution(mesh):
    spec = P("gx", "gy", None)
    return jax.shard_map(
        shards, mesh=mesh, in_specs=(spec,) * 5, out_specs=(spec, P()), check_vma=False
    )
```

```python
import functools

import jax
import jax.numpy as jnp
from jax import lax
from jax.experimental import pallas as pl
from jax.experimental.pallas import tpu as pltpu
from jax.sharding import PartitionSpec as P

ADJ_SWEEPS = 2
FILTER_SWEEPS = 4

eps_void = 1.0
eps_solid = 12.0
eps_back = 4.0
eps_metal = 40.0
screen = 0.5
radius_sq = 2.0
epsilon_mean = 1e-06

WIDTHS = (ADJ_SWEEPS + 1, ADJ_SWEEPS + 1, ADJ_SWEEPS, 1)
RIM = 4
VMEM_LIMIT = 24 * 1024 * 1024


def segments(widths, size_x, beside=True, beyond=True):
    found, at = [], 0
    for field, width in enumerate(widths):
        for x in range(-width, size_x + width):
            rows = width - max(0, -x, x - size_x + 1)
            if rows > 0 and (beside if 0 <= x < size_x else beyond):
                found.append((field, x, rows, at))
                at += rows
    return found, -(-at // 8) * 8


def plane_starts(widths):
    starts, at = [], 0
    for width in widths:
        starts.append(at)
        at += width
    return starts, at


def material(density, labels):
    design = eps_void + density * density * density * (eps_solid - eps_void)
    return jnp.where(labels == 1, design, jnp.where(labels == 2, eps_metal, eps_back))


def call(body, outs, scratch=(), in_specs=None, cost=10000):
    kwargs = {} if in_specs is None else {"in_specs": in_specs, "grid": (1,)}
    return pl.pallas_call(
        body,
        out_shape=outs,
        scratch_shapes=list(scratch),
        compiler_params=pltpu.CompilerParams(vmem_limit_bytes=VMEM_LIMIT),
        cost_estimate=pl.CostEstimate(flops=cost, bytes_accessed=cost, transcendentals=0),
        **kwargs,
    )


def f32(*shape):
    return jax.ShapeDtypeStruct(shape, jnp.float32)


def odd_place(axis):
    return lax.rem(lax.axis_index(axis), 2) == 1


def pack_own(*refs):
    inputs, (x_odd_out, x_even_out, y_even_out, y_odd_out), held, sem = refs[:5], refs[5:9], refs[9:14], refs[14]
    density, labels, adjoint, source, potential = held
    size_x, size_y, _ = density.shape
    starts, _ = plane_starts(WIDTHS)
    copies = [pltpu.make_async_copy(a, b, sem.at[k]) for k, (a, b) in enumerate(zip(inputs, held))]
    for copy in copies:
        copy.start()
    for copy in copies:
        copy.wait()
    low_first = odd_place("gx")
    for out, low in ((x_even_out, low_first), (x_odd_out, jnp.logical_not(low_first))):
        for field, width in enumerate(WIDTHS):
            span = pl.ds(jnp.where(low, 0, size_x - width), width)
            if field == 0:
                face = material(density[span], labels[span])
            else:
                face = (adjoint, source, potential)[field - 1][span]
            out[pl.ds(starts[field], width)] = face
    y_swap = odd_place("gy")
    for field, x, rows, at in segments(WIDTHS, size_x, beyond=False)[0]:
        faces = []
        for rim in (slice(0, rows), slice(size_y - rows, size_y)):
            if field == 0:
                faces.append(material(density[x, rim], labels[x, rim]))
            else:
                faces.append((adjoint, source, potential)[field - 1][x, rim])
        low, high = faces
        y_even_out[at:at + rows] = jnp.where(y_swap, low, high)
        y_odd_out[at:at + rows] = jnp.where(y_swap, high, low)


def pack_corners(size_x, x_odd, x_even, even_out, odd_out):
    size_y = x_odd.shape[1]
    starts, _ = plane_starts(WIDTHS)
    x_swap, y_swap = odd_place("gx"), odd_place("gy")
    for field, x, rows, at in segments(WIDTHS, size_x, beside=False)[0]:
        faces = []
        for rim in (slice(0, rows), slice(size_y - rows, size_y)):
            if x < 0:
                plane = starts[field] + WIDTHS[field] + x
                face = jnp.where(x_swap, x_even[plane, rim], x_odd[plane, rim])
            else:
                plane = starts[field] + x - size_x
                face = jnp.where(x_swap, x_odd[plane, rim], x_even[plane, rim])
            faces.append(face)
        low, high = faces
        even_out[at:at + rows] = jnp.where(y_swap, low, high)
        odd_out[at:at + rows] = jnp.where(y_swap, high, low)


def shift(value, by, axis):
    return pltpu.roll(value, by % value.shape[axis], axis)


def planes_loop(low, high, block, step):
    count = high - low
    block = max(k for k in range(1, block + 1) if count % k == 0)

    def body(k, carry):
        step(low + k * block, block)
        return carry

    lax.fori_loop(0, count // block, body, 0)


def unpack_rows(fields, widths, found, even, odd, size_y):
    wide = size_y + 2 * RIM
    swap = odd_place("gy")
    for field, x, rows, at in found:
        if fields[field] is None:
            continue
        a, b = even[at:at + rows], odd[at:at + rows]
        fields[field][x + widths[field], wide - rows:wide] = jnp.where(swap, a, b)
        fields[field][x + widths[field], size_y:size_y + rows] = jnp.where(swap, b, a)


def unpack_planes(field, width, even, odd, size_x, size_y):
    swap = odd_place("gx")
    tile = pl.ds(0, size_y)
    field[pl.ds(0, width), tile] = jnp.where(swap, even, odd)
    field[pl.ds(width + size_x, width), tile] = jnp.where(swap, odd, even)


def energy_part(x_odd, x_even, y_odd, y_even, density, labels, potential, energy_out, poten):
    size_x, size_y, size_z = density.shape
    starts, planes = plane_starts(WIDTHS)
    planes_loop(0, size_x, 4, lambda x, n: poten.__setitem__((pl.ds(x + 1, n), pl.ds(0, size_y)), potential[pl.ds(x, n)]))
    span = pl.ds(starts[3], 1)
    unpack_planes(poten, 1, x_even[span], x_odd[span], size_x, size_y)
    found, _ = segments(WIDTHS, size_x, beyond=False)
    unpack_rows((None, None, None, poten), WIDTHS, found, y_even, y_odd, size_y)
    wide = size_y + 2 * RIM
    lane = lax.broadcasted_iota(jnp.int32, (1, wide, size_z), 2)
    is_first = lane == 0
    is_last = lane == size_z - 1
    energy_out[...] = jnp.zeros_like(energy_out)

    def step(x, n):
        span = pl.ds(x, n)
        v = poten[pl.ds(x + 1, n)]
        low, high = poten[pl.ds(x, n)] - v, poten[pl.ds(x + 2, n)] - v
        squares = low * low + high * high
        dv = shift(v, -1, 1) - v
        square = dv * dv
        squares = squares + square + shift(square, 1, 1)
        dv = jnp.where(is_last, 0.0, shift(v, -1, 2)) - v
        square = dv * dv
        squares = squares + square + jnp.where(is_first, v * v, shift(square, 1, 2))
        energy = material(density[span], labels[span]) * squares[:, :size_y]
        energy_out[...] += jnp.sum(energy.reshape(-1, 8, size_z), axis=0)

    planes_loop(0, size_x, 4, step)


def adjoint_part(x_odd, x_even, y_odd, y_even, corner_odd, corner_even, density, labels, adjoint_start, adjoint_source, potential,
                 raw_out,
                 permit, start, source, poten, face_x, face_y, face_z, inverse, first, second):
    size_x, size_y, size_z = density.shape
    starts, _ = plane_starts(WIDTHS)
    fields = (permit, start, source, poten)
    tile = pl.ds(0, size_y)

    def fill(x, n):
        span = pl.ds(x, n)
        permit[pl.ds(x + WIDTHS[0], n), tile] = material(density[span], labels[span])
        start[pl.ds(x + WIDTHS[1], n), tile] = adjoint_start[span]
        source[pl.ds(x + WIDTHS[2], n), tile] = adjoint_source[span]
        poten[pl.ds(x + WIDTHS[3], n), tile] = potential[span]

    planes_loop(0, size_x, 4, fill)
    for field, width in enumerate(WIDTHS):
        span = pl.ds(starts[field], width)
        unpack_planes(fields[field], width, x_even[span], x_odd[span], size_x, size_y)
    unpack_rows(fields, WIDTHS, segments(WIDTHS, size_x, beyond=False)[0], y_even, y_odd, size_y)
    unpack_rows(fields, WIDTHS, segments(WIDTHS, size_x, beside=False)[0], corner_even, corner_odd, size_y)

    wide = size_y + 2 * RIM
    lane = lax.broadcasted_iota(jnp.int32, (1, wide, size_z), 2)
    is_first = lane == 0
    is_last = lane == size_z - 1

    def harmonic(a, b):
        return 2.0 * a * b / jnp.maximum(a + b, 0.25)

    def faces_x(x, n):
        face_x[pl.ds(x, n)] = harmonic(permit[pl.ds(x, n)], permit[pl.ds(x + 1, n)])

    planes_loop(0, size_x + 5, 7, faces_x)

    def weigh(x, n):
        span = pl.ds(x, n)
        p = permit[pl.ds(x + 1, n)]
        fy = harmonic(p, shift(p, -1, 1))
        fz = jnp.where(is_last, 0.0, harmonic(p, shift(p, -1, 2)))
        face_y[span] = fy
        face_z[span] = fz
        total = screen + face_x[span] + face_x[pl.ds(x + 1, n)] + fy + shift(fy, 1, 1) + fz + shift(fz, 1, 2)
        inverse[span] = jnp.where(p > 20.0, 0.0, 1.0 / total)

    planes_loop(0, size_x + 4, 5, weigh)

    def relax(x, n, a, a_low, a_high):
        span = pl.ds(x, n)
        fy, fz = face_y[span], face_z[span]
        total = source[span] + face_x[pl.ds(x + 1, n)] * a_high + face_x[span] * a_low
        total = total + fy * shift(a, -1, 1) + shift(fy * a, 1, 1)
        total = total + fz * shift(a, -1, 2) + shift(fz * a, 1, 2)
        return total * inverse[span]

    def sweep_one(x, n):
        first[pl.ds(x, n)] = relax(x, n, start[pl.ds(x + 1, n)], start[pl.ds(x, n)], start[pl.ds(x + 2, n)])

    planes_loop(0, size_x + 4, 10, sweep_one)

    def sweep_two(x, n):
        second[pl.ds(x, n)] = relax(x + 1, n, first[pl.ds(x + 1, n)], first[pl.ds(x, n)], first[pl.ds(x + 2, n)])

    planes_loop(0, size_x + 2, 9, sweep_two)

    def finish(x, n):
        span = pl.ds(x, n)
        v, a = poten[pl.ds(x + 1, n)], second[pl.ds(x + 1, n)]
        product = (poten[pl.ds(x, n)] - v) * (second[pl.ds(x, n)] - a)
        product = product + (poten[pl.ds(x + 2, n)] - v) * (second[pl.ds(x + 2, n)] - a)
        both = (shift(v, -1, 1) - v) * (shift(a, -1, 1) - a)
        product = product + both + shift(both, 1, 1)
        both = (jnp.where(is_last, 0.0, shift(v, -1, 2)) - v) * (jnp.where(is_last, 0.0, shift(a, -1, 2)) - a)
        product = product + both + jnp.where(is_first, v * a, shift(both, 1, 2))
        d = density[span]
        gain = jnp.where(labels[span] == 1, -1.5 * (eps_solid - eps_void) * d * d, 0.0)
        raw_out[span] = gain * product[:, :size_y]

    planes_loop(0, size_x, 8, finish)


def pack_raw_x(raw, even_out, odd_out):
    size_x = raw.shape[0]
    low_first = odd_place("gx")
    for out, low in ((even_out, low_first), (odd_out, jnp.logical_not(low_first))):
        out[...] = raw[pl.ds(jnp.where(low, 0, size_x - FILTER_SWEEPS), FILTER_SWEEPS)]


def pack_raw_y(x_odd, x_even, raw, even_out, odd_out):
    size_x, size_y, _ = raw.shape
    width = FILTER_SWEEPS
    found, _ = segments((width,), size_x)
    x_swap, y_swap = odd_place("gx"), odd_place("gy")
    for _, x, rows, at in found:
        faces = []
        for rim in (slice(0, rows), slice(size_y - rows, size_y)):
            if x < 0:
                face = jnp.where(x_swap, x_even[width + x, rim], x_odd[width + x, rim])
            elif x >= size_x:
                face = jnp.where(x_swap, x_odd[x - size_x, rim], x_even[x - size_x, rim])
            else:
                face = raw[x, rim]
            faces.append(face)
        low, high = faces
        even_out[at:at + rows] = jnp.where(y_swap, low, high)
        odd_out[at:at + rows] = jnp.where(y_swap, high, low)


def relaxation(raw, size_x, size_y, size_z):
    width = FILTER_SWEEPS
    wide = size_y + 2 * RIM
    extent_x = lax.axis_size("gx") * size_x
    extent_y = lax.axis_size("gy") * size_y
    base_x = lax.axis_index("gx") * size_x - width
    lane = lax.broadcasted_iota(jnp.int32, (1, wide, size_z), 2)
    row = lax.broadcasted_iota(jnp.int32, (1, wide, size_z), 1)
    place = lax.axis_index("gy") * size_y + jnp.where(row < size_y + RIM, row, row - wide)
    is_first, is_last = lane == 0, lane == size_z - 1

    def edges(at, extent):
        return jnp.where(at > 0, 1.0, 0.0) + jnp.where(at < extent - 1, 1.0, 0.0)

    count = edges(place, extent_y) + edges(lane, size_z)
    inside = (place >= 0) & (place < extent_y)
    scale_two = jnp.where(inside, 1.0 / (1.0 + radius_sq * (count + 2.0)), 0.0)
    scale_one = jnp.where(inside, 1.0 / (1.0 + radius_sq * (count + 1.0)), 0.0)

    def relax(src, x, n):
        f = src[pl.ds(x, n)]
        near = src[pl.ds(x - 1, n)] + src[pl.ds(x + 1, n)] + shift(f, 1, 1) + shift(f, -1, 1)
        near = near + jnp.where(is_first, 0.0, shift(f, 1, 2)) + jnp.where(is_last, 0.0, shift(f, -1, 2))
        total = raw[pl.ds(x, n)] + radius_sq * near
        scaled = []
        for k in range(n):
            at = base_x + x + k
            outside = (at < 0) | (at >= extent_x)
            border = (at == 0) | (at == extent_x - 1)
            scale = jnp.where(outside, 0.0, jnp.where(border, scale_one, scale_two))
            scaled.append(total[k:k + 1] * scale)
        return jnp.concatenate(scaled, axis=0)

    return relax


def filter_first(x_odd, x_even, y_odd, y_even, raw_in, raw, odd, even):
    size_x, size_y, size_z = raw_in.shape
    width = FILTER_SWEEPS
    tile = pl.ds(0, size_y)

    def fill(x, n):
        raw[pl.ds(x + width, n), tile] = raw_in[pl.ds(x, n)]

    planes_loop(0, size_x, 4, fill)
    unpack_planes(raw, width, x_even[...], x_odd[...], size_x, size_y)
    unpack_rows((raw,), (width,), segments((width,), size_x)[0], y_even, y_odd, size_y)
    relax = relaxation(raw, size_x, size_y, size_z)
    src = raw
    for sweep in range(FILTER_SWEEPS - 1):
        dst = (odd, even)[(FILTER_SWEEPS - sweep) % 2]

        def step(x, n, src=src, dst=dst):
            dst[pl.ds(x, n)] = relax(src, x, n)

        planes_loop(sweep + 1, size_x + 2 * width - sweep - 1, 11, step)
        src = dst


def filter_last(raw, src, labels, energies, out, mean_out, held, sem):
    size_x, size_y, size_z = labels.shape
    relax = relaxation(raw, size_x, size_y, size_z)
    voxels = lax.axis_size("gx") * size_x * lax.axis_size("gy") * size_y * size_z
    mean = 0.5 * jnp.sum(jnp.sum(energies[...], axis=0)) / voxels + epsilon_mean
    mean_out[0, 0] = mean
    inverse = 1.0 / jnp.full((1, 1, size_z), mean, jnp.float32)
    block = size_x // 2
    copies = []
    for k in range(2):
        span = pl.ds(k * block, block)
        f = relax(src, k * block + FILTER_SWEEPS, block)[:, :size_y]
        held[span] = jnp.where(labels[span] == 1, f * inverse, 0.0)
        copies.append(pltpu.make_async_copy(held.at[span], out.at[span], sem.at[k]))
        copies[k].start()
    for copy in copies:
        copy.wait()


def swap_even(value, axis):
    return lax.ppermute(value, axis, [(i, i ^ 1) for i in range(lax.axis_size(axis))])


def swap_odd(value, axis):
    count = lax.axis_size(axis)
    up = [(i, i + 1) for i in range(1, count - 1, 2)]
    return lax.ppermute(value, axis, up + [(b, a) for a, b in up])


def shards(density, potential, adjoint_start, adjoint_source, labels):
    size_x, size_y, size_z = potential.shape
    _, planes = plane_starts(WIDTHS)
    _, rows = segments(WIDTHS, size_x, beyond=False)
    _, corners = segments(WIDTHS, size_x, beside=False)
    own = [
        pltpu.with_memory_space_constraint(array, pltpu.HBM)
        for array in (density, labels, adjoint_start, adjoint_source, potential)
    ]

    shape = (size_x, size_y, size_z)
    odd, even, tile_even, tile_odd, *own = pl.pallas_call(
        pack_own,
        out_shape=(f32(planes, size_y, size_z),) * 2 + (f32(rows, size_z),) * 2
        + (f32(*shape), jax.ShapeDtypeStruct(shape, jnp.int32)) + (f32(*shape),) * 3,
        in_specs=[pl.BlockSpec(memory_space=pltpu.HBM)] * 5,
        scratch_shapes=[pltpu.SemaphoreType.DMA((5,))],
        compiler_params=pltpu.CompilerParams(vmem_limit_bytes=VMEM_LIMIT),
    )(*own)
    x_even = swap_even(even, "gx")
    x_odd = swap_odd(odd, "gx")
    y_even = swap_even(tile_even, "gy")
    y_odd = swap_odd(tile_odd, "gy")
    even, odd = call(functools.partial(pack_corners, size_x), (f32(corners, size_z),) * 2)(x_odd, x_even)
    corner_even = swap_even(even, "gy")
    corner_odd = swap_odd(odd, "gy")

    wide = size_y + 2 * RIM

    def room(extra):
        return pltpu.VMEM((size_x + extra, wide, size_z), jnp.float32)

    energy = call(energy_part, f32(8, size_z), [room(2)])(x_odd, x_even, y_odd, y_even, own[0], own[1], own[4])
    devices = lax.axis_size("gx") * lax.axis_size("gy")
    spread = jnp.broadcast_to(energy[None], (devices, 8, size_z))
    energies = lax.all_to_all(spread, ("gx", "gy"), 0, 0)
    face = f32(FILTER_SWEEPS, size_y, size_z)
    raw = call(
        adjoint_part,
        f32(*shape),
        [room(6), room(6), room(4), room(2), room(5), room(4), room(4), room(4), room(4), room(2)],
        cost=10000000,
    )(x_odd, x_even, y_odd, y_even, corner_odd, corner_even, *own)

    even, odd = call(pack_raw_x, (face, face))(raw)
    x_even = swap_even(even, "gx")
    x_odd = swap_odd(odd, "gx")
    _, rows = segments((FILTER_SWEEPS,), size_x)
    even, odd = call(pack_raw_y, (f32(rows, size_z), f32(rows, size_z)))(x_odd, x_even, raw)
    y_even = swap_even(even, "gy")
    y_odd = swap_odd(odd, "gy")
    padded = f32(size_x + 2 * FILTER_SWEEPS, wide, size_z)
    raw, filtered = call(
        filter_first,
        (padded, padded),
        [pltpu.VMEM(padded.shape, jnp.float32)],
        cost=10000000,
    )(x_odd, x_even, y_odd, y_even, raw)
    sensitivity, mean_energy = pl.pallas_call(
        filter_last,
        out_shape=(f32(*shape), f32(1, 1)),
        out_specs=(pl.BlockSpec(memory_space=pl.ANY), pl.BlockSpec(memory_space=pltpu.SMEM)),
        scratch_shapes=[pltpu.VMEM(shape, jnp.float32), pltpu.SemaphoreType.DMA((2,))],
        compiler_params=pltpu.CompilerParams(vmem_limit_bytes=VMEM_LIMIT),
    )(raw, filtered, own[1], energies)
    return (sensitivity, mean_energy[0, 0])


def solution(mesh):
    spec = P("gx", "gy", None)
    return jax.shard_map(
        shards, mesh=mesh, in_specs=(spec,) * 5, out_specs=(spec, P()), check_vma=False
    )
```

```python
import functools

import jax
import jax.numpy as jnp
from jax import lax
from jax.experimental import pallas as pl
from jax.experimental.pallas import tpu as pltpu
from jax.sharding import PartitionSpec as P

ADJ_SWEEPS = 2
FILTER_SWEEPS = 4

eps_void = 1.0
eps_solid = 12.0
eps_back = 4.0
eps_metal = 40.0
screen = 0.5
radius_sq = 2.0
epsilon_mean = 1e-06

WIDTHS = (ADJ_SWEEPS + 1, ADJ_SWEEPS + 1, ADJ_SWEEPS, 1)
RIM = 4
VMEM_LIMIT = 24 * 1024 * 1024


def segments(widths, size_x, beside=True, beyond=True):
    found, at = [], 0
    for field, width in enumerate(widths):
        for x in range(-width, size_x + width):
            rows = width - max(0, -x, x - size_x + 1)
            if rows > 0 and (beside if 0 <= x < size_x else beyond):
                found.append((field, x, rows, at))
                at += rows
    return found, -(-at // 8) * 8


def plane_starts(widths):
    starts, at = [], 0
    for width in widths:
        starts.append(at)
        at += width
    return starts, at


def material(density, labels):
    design = eps_void + density * density * density * (eps_solid - eps_void)
    return jnp.where(labels == 1, design, jnp.where(labels == 2, eps_metal, eps_back))


def call(body, outs, scratch=(), in_specs=None, cost=10000):
    kwargs = {} if in_specs is None else {"in_specs": in_specs, "grid": (1,)}
    return pl.pallas_call(
        body,
        out_shape=outs,
        scratch_shapes=list(scratch),
        compiler_params=pltpu.CompilerParams(vmem_limit_bytes=VMEM_LIMIT),
        cost_estimate=pl.CostEstimate(flops=cost, bytes_accessed=cost, transcendentals=0),
        **kwargs,
    )


def f32(*shape):
    return jax.ShapeDtypeStruct(shape, jnp.float32)


def odd_place(axis):
    return lax.rem(lax.axis_index(axis), 2) == 1


def pack_own(*refs):
    inputs, (x_odd_out, x_even_out, y_even_out, y_odd_out), held, sem = refs[:5], refs[5:9], refs[9:14], refs[14]
    density, labels, adjoint, source, potential = held
    size_x, size_y, _ = density.shape
    starts, _ = plane_starts(WIDTHS)
    copies = [pltpu.make_async_copy(a, b, sem.at[k]) for k, (a, b) in enumerate(zip(inputs, held))]
    for copy in copies:
        copy.start()
    copies[0].wait()
    low_first, y_swap = odd_place("gx"), odd_place("gy")
    found, _ = segments(WIDTHS, size_x, beyond=False)
    for field, width in enumerate(WIDTHS):
        copies[field + 1].wait()
        for out, low in ((x_even_out, low_first), (x_odd_out, jnp.logical_not(low_first))):
            span = pl.ds(jnp.where(low, 0, size_x - width), width)
            if field == 0:
                face = material(density[span], labels[span])
            else:
                face = (adjoint, source, potential)[field - 1][span]
            out[pl.ds(starts[field], width)] = face
        for _, x, rows, at in (part for part in found if part[0] == field):
            faces = []
            for rim in (slice(0, rows), slice(size_y - rows, size_y)):
                if field == 0:
                    faces.append(material(density[x, rim], labels[x, rim]))
                else:
                    faces.append((adjoint, source, potential)[field - 1][x, rim])
            low, high = faces
            y_even_out[at:at + rows] = jnp.where(y_swap, low, high)
            y_odd_out[at:at + rows] = jnp.where(y_swap, high, low)


def pack_corners(size_x, x_odd, x_even, even_out, odd_out):
    size_y = x_odd.shape[1]
    starts, _ = plane_starts(WIDTHS)
    x_swap, y_swap = odd_place("gx"), odd_place("gy")
    for field, x, rows, at in segments(WIDTHS, size_x, beside=False)[0]:
        faces = []
        for rim in (slice(0, rows), slice(size_y - rows, size_y)):
            if x < 0:
                plane = starts[field] + WIDTHS[field] + x
                face = jnp.where(x_swap, x_even[plane, rim], x_odd[plane, rim])
            else:
                plane = starts[field] + x - size_x
                face = jnp.where(x_swap, x_odd[plane, rim], x_even[plane, rim])
            faces.append(face)
        low, high = faces
        even_out[at:at + rows] = jnp.where(y_swap, low, high)
        odd_out[at:at + rows] = jnp.where(y_swap, high, low)


def shift(value, by, axis):
    return pltpu.roll(value, by % value.shape[axis], axis)


def planes_loop(low, high, block, step):
    count = high - low
    block = max(k for k in range(1, block + 1) if count % k == 0)

    def body(k, carry):
        step(low + k * block, block)
        return carry

    lax.fori_loop(0, count // block, body, 0)


def unpack_rows(fields, widths, found, even, odd, size_y):
    wide = size_y + 2 * RIM
    swap = odd_place("gy")
    for field, x, rows, at in found:
        if fields[field] is None:
            continue
        a, b = even[at:at + rows], odd[at:at + rows]
        fields[field][x + widths[field], wide - rows:wide] = jnp.where(swap, a, b)
        fields[field][x + widths[field], size_y:size_y + rows] = jnp.where(swap, b, a)


def unpack_planes(field, width, even, odd, size_x, size_y):
    swap = odd_place("gx")
    tile = pl.ds(0, size_y)
    field[pl.ds(0, width), tile] = jnp.where(swap, even, odd)
    field[pl.ds(width + size_x, width), tile] = jnp.where(swap, odd, even)


def energy_part(x_odd, x_even, y_odd, y_even, density, labels, potential, energy_out, poten):
    size_x, size_y, size_z = density.shape
    starts, planes = plane_starts(WIDTHS)
    planes_loop(0, size_x, 4, lambda x, n: poten.__setitem__((pl.ds(x + 1, n), pl.ds(0, size_y)), potential[pl.ds(x, n)]))
    span = pl.ds(starts[3], 1)
    unpack_planes(poten, 1, x_even[span], x_odd[span], size_x, size_y)
    found, _ = segments(WIDTHS, size_x, beyond=False)
    unpack_rows((None, None, None, poten), WIDTHS, found, y_even, y_odd, size_y)
    wide = size_y + 2 * RIM
    lane = lax.broadcasted_iota(jnp.int32, (1, wide, size_z), 2)
    is_first = lane == 0
    is_last = lane == size_z - 1
    energy_out[...] = jnp.zeros_like(energy_out)

    def step(x, n):
        span = pl.ds(x, n)
        v = poten[pl.ds(x + 1, n)]
        low, high = poten[pl.ds(x, n)] - v, poten[pl.ds(x + 2, n)] - v
        squares = low * low + high * high
        dv = shift(v, -1, 1) - v
        square = dv * dv
        squares = squares + square + shift(square, 1, 1)
        dv = jnp.where(is_last, 0.0, shift(v, -1, 2)) - v
        square = dv * dv
        squares = squares + square + jnp.where(is_first, v * v, shift(square, 1, 2))
        energy = material(density[span], labels[span]) * squares[:, :size_y]
        energy_out[...] += jnp.sum(energy.reshape(-1, 8, size_z), axis=0)

    planes_loop(0, size_x, 4, step)


def adjoint_part(x_odd, x_even, y_odd, y_even, corner_odd, corner_even, density, labels, adjoint_start, adjoint_source, potential,
                 raw_out,
                 permit, start, source, poten, face_x, face_y, face_z, inverse, first, second):
    size_x, size_y, size_z = density.shape
    starts, _ = plane_starts(WIDTHS)
    fields = (permit, start, source, poten)
    tile = pl.ds(0, size_y)

    def fill(x, n):
        span = pl.ds(x, n)
        permit[pl.ds(x + WIDTHS[0], n), tile] = material(density[span], labels[span])
        start[pl.ds(x + WIDTHS[1], n), tile] = adjoint_start[span]
        source[pl.ds(x + WIDTHS[2], n), tile] = adjoint_source[span]
        poten[pl.ds(x + WIDTHS[3], n), tile] = potential[span]

    planes_loop(0, size_x, 4, fill)
    for field, width in enumerate(WIDTHS):
        span = pl.ds(starts[field], width)
        unpack_planes(fields[field], width, x_even[span], x_odd[span], size_x, size_y)
    unpack_rows(fields, WIDTHS, segments(WIDTHS, size_x, beyond=False)[0], y_even, y_odd, size_y)
    unpack_rows(fields, WIDTHS, segments(WIDTHS, size_x, beside=False)[0], corner_even, corner_odd, size_y)

    wide = size_y + 2 * RIM
    lane = lax.broadcasted_iota(jnp.int32, (1, wide, size_z), 2)
    is_first = lane == 0
    is_last = lane == size_z - 1

    def harmonic(a, b):
        return 2.0 * a * b / jnp.maximum(a + b, 0.25)

    def faces_x(x, n):
        face_x[pl.ds(x, n)] = harmonic(permit[pl.ds(x, n)], permit[pl.ds(x + 1, n)])

    planes_loop(0, size_x + 5, 7, faces_x)

    def weigh(x, n):
        span = pl.ds(x, n)
        p = permit[pl.ds(x + 1, n)]
        fy = harmonic(p, shift(p, -1, 1))
        fz = jnp.where(is_last, 0.0, harmonic(p, shift(p, -1, 2)))
        face_y[span] = fy
        face_z[span] = fz
        total = screen + face_x[span] + face_x[pl.ds(x + 1, n)] + fy + shift(fy, 1, 1) + fz + shift(fz, 1, 2)
        inverse[span] = jnp.where(p > 20.0, 0.0, 1.0 / total)

    planes_loop(0, size_x + 4, 5, weigh)

    def relax(x, n, a, a_low, a_high):
        span = pl.ds(x, n)
        fy, fz = face_y[span], face_z[span]
        total = source[span] + face_x[pl.ds(x + 1, n)] * a_high + face_x[span] * a_low
        total = total + fy * shift(a, -1, 1) + shift(fy * a, 1, 1)
        total = total + fz * shift(a, -1, 2) + shift(fz * a, 1, 2)
        return total * inverse[span]

    def sweep_one(x, n):
        first[pl.ds(x, n)] = relax(x, n, start[pl.ds(x + 1, n)], start[pl.ds(x, n)], start[pl.ds(x + 2, n)])

    planes_loop(0, size_x + 4, 10, sweep_one)

    def sweep_two(x, n):
        second[pl.ds(x, n)] = relax(x + 1, n, first[pl.ds(x + 1, n)], first[pl.ds(x, n)], first[pl.ds(x + 2, n)])

    planes_loop(0, size_x + 2, 9, sweep_two)

    def finish(x, n):
        span = pl.ds(x, n)
        v, a = poten[pl.ds(x + 1, n)], second[pl.ds(x + 1, n)]
        product = (poten[pl.ds(x, n)] - v) * (second[pl.ds(x, n)] - a)
        product = product + (poten[pl.ds(x + 2, n)] - v) * (second[pl.ds(x + 2, n)] - a)
        both = (shift(v, -1, 1) - v) * (shift(a, -1, 1) - a)
        product = product + both + shift(both, 1, 1)
        both = (jnp.where(is_last, 0.0, shift(v, -1, 2)) - v) * (jnp.where(is_last, 0.0, shift(a, -1, 2)) - a)
        product = product + both + jnp.where(is_first, v * a, shift(both, 1, 2))
        d = density[span]
        gain = jnp.where(labels[span] == 1, -1.5 * (eps_solid - eps_void) * d * d, 0.0)
        raw_out[span] = gain * product[:, :size_y]

    planes_loop(0, size_x, 8, finish)


def pack_raw_x(raw, out, low):
    out[...] = raw[pl.ds(jnp.where(low, 0, raw.shape[0] - FILTER_SWEEPS), FILTER_SWEEPS)]


def pack_raw_x_odd(raw, out):
    pack_raw_x(raw, out, jnp.logical_not(odd_place("gx")))


def pack_raw_x_even(raw, mine, other, out, energy_out):
    energy_out[...] = mine[...] + other[...]
    pack_raw_x(raw, out, odd_place("gx"))


def pack_raw_y(x_odd, x_even, raw, mine, other, even_out, odd_out, energy_out):
    size_x, size_y, _ = raw.shape
    width = FILTER_SWEEPS
    found, total = segments((width,), size_x)
    x_swap, y_swap = odd_place("gx"), odd_place("gy")
    energy = mine[...] + other[...]
    energy_out[...] = energy
    even_out[total:total + 8] = energy
    for _, x, rows, at in found:
        faces = []
        for rim in (slice(0, rows), slice(size_y - rows, size_y)):
            if x < 0:
                face = jnp.where(x_swap, x_even[width + x, rim], x_odd[width + x, rim])
            elif x >= size_x:
                face = jnp.where(x_swap, x_odd[x - size_x, rim], x_even[x - size_x, rim])
            else:
                face = raw[x, rim]
            faces.append(face)
        low, high = faces
        even_out[at:at + rows] = jnp.where(y_swap, low, high)
        odd_out[at:at + rows] = jnp.where(y_swap, high, low)


def relaxation(raw, size_x, size_y, size_z):
    width = FILTER_SWEEPS
    wide = size_y + 2 * RIM
    extent_x = lax.axis_size("gx") * size_x
    extent_y = lax.axis_size("gy") * size_y
    base_x = lax.axis_index("gx") * size_x - width
    lane = lax.broadcasted_iota(jnp.int32, (1, wide, size_z), 2)
    row = lax.broadcasted_iota(jnp.int32, (1, wide, size_z), 1)
    place = lax.axis_index("gy") * size_y + jnp.where(row < size_y + RIM, row, row - wide)
    is_first, is_last = lane == 0, lane == size_z - 1

    def edges(at, extent):
        return jnp.where(at > 0, 1.0, 0.0) + jnp.where(at < extent - 1, 1.0, 0.0)

    count = edges(place, extent_y) + edges(lane, size_z)
    inside = (place >= 0) & (place < extent_y)
    scale_two = jnp.where(inside, 1.0 / (1.0 + radius_sq * (count + 2.0)), 0.0)
    scale_one = jnp.where(inside, 1.0 / (1.0 + radius_sq * (count + 1.0)), 0.0)

    def relax(src, x, n):
        f = src[pl.ds(x, n)]
        near = src[pl.ds(x - 1, n)] + src[pl.ds(x + 1, n)] + shift(f, 1, 1) + shift(f, -1, 1)
        near = near + jnp.where(is_first, 0.0, shift(f, 1, 2)) + jnp.where(is_last, 0.0, shift(f, -1, 2))
        total = raw[pl.ds(x, n)] + radius_sq * near
        scaled = []
        for k in range(n):
            at = base_x + x + k
            outside = (at < 0) | (at >= extent_x)
            border = (at == 0) | (at == extent_x - 1)
            scale = jnp.where(outside, 0.0, jnp.where(border, scale_one, scale_two))
            scaled.append(total[k:k + 1] * scale)
        return jnp.concatenate(scaled, axis=0)

    return relax


def filter_first(x_odd, x_even, y_odd, y_even, raw_in, raw, odd, even):
    size_x, size_y, size_z = raw_in.shape
    width = FILTER_SWEEPS
    tile = pl.ds(0, size_y)

    def fill(x, n):
        raw[pl.ds(x + width, n), tile] = raw_in[pl.ds(x, n)]

    planes_loop(0, size_x, 4, fill)
    unpack_planes(raw, width, x_even[...], x_odd[...], size_x, size_y)
    unpack_rows((raw,), (width,), segments((width,), size_x)[0], y_even, y_odd, size_y)
    relax = relaxation(raw, size_x, size_y, size_z)
    src = raw
    for sweep in range(FILTER_SWEEPS - 1):
        dst = (odd, even)[(FILTER_SWEEPS - sweep) % 2]

        def step(x, n, src=src, dst=dst):
            dst[pl.ds(x, n)] = relax(src, x, n)

        planes_loop(sweep + 1, size_x + 2 * width - sweep - 1, 11, step)
        src = dst


def filter_last(raw, src, labels, mine, other, out, mean_out, held, sem):
    size_x, size_y, size_z = labels.shape
    relax = relaxation(raw, size_x, size_y, size_z)
    voxels = lax.axis_size("gx") * size_x * lax.axis_size("gy") * size_y * size_z
    mean = 0.5 * jnp.sum(mine[...] + other[...]) / voxels + epsilon_mean
    mean_out[0, 0] = mean
    inverse = 1.0 / jnp.full((1, 1, size_z), mean, jnp.float32)
    block = size_x // 2
    copies = []
    for k in range(2):
        span = pl.ds(k * block, block)
        f = relax(src, k * block + FILTER_SWEEPS, block)[:, :size_y]
        held[span] = jnp.where(labels[span] == 1, f * inverse, 0.0)
        copies.append(pltpu.make_async_copy(held.at[span], out.at[span], sem.at[k]))
        copies[k].start()
    for copy in copies:
        copy.wait()


def swap_even(value, axis):
    return lax.ppermute(value, axis, [(i, i ^ 1) for i in range(lax.axis_size(axis))])


def swap_odd(value, axis):
    count = lax.axis_size(axis)
    up = [(i, i + 1) for i in range(1, count - 1, 2)]
    return lax.ppermute(value, axis, up + [(b, a) for a, b in up])


def partner(value, axis, bit):
    return lax.ppermute(value, axis, [(i, i ^ bit) for i in range(lax.axis_size(axis))])


def doubling(energy, stages):
    other = partner(energy, *stages[0])
    for stage in stages[1:]:
        energy = energy + other
        other = partner(energy, *stage)
    return energy, other


def shards(density, potential, adjoint_start, adjoint_source, labels):
    size_x, size_y, size_z = potential.shape
    _, planes = plane_starts(WIDTHS)
    _, rows = segments(WIDTHS, size_x, beyond=False)
    _, corners = segments(WIDTHS, size_x, beside=False)
    own = [
        pltpu.with_memory_space_constraint(array, pltpu.HBM)
        for array in (density, labels, adjoint_start, adjoint_source, potential)
    ]
    x_bits = [("gx", 1 << k) for k in range(1, (lax.axis_size("gx") - 1).bit_length())]
    y_bits = [("gy", 1 << k) for k in range(1, (lax.axis_size("gy") - 1).bit_length())]

    shape = (size_x, size_y, size_z)
    odd, even, tile_even, tile_odd, *own = pl.pallas_call(
        pack_own,
        out_shape=(f32(planes, size_y, size_z),) * 2 + (f32(rows, size_z),) * 2
        + (f32(*shape), jax.ShapeDtypeStruct(shape, jnp.int32)) + (f32(*shape),) * 3,
        in_specs=[pl.BlockSpec(memory_space=pltpu.HBM)] * 5,
        scratch_shapes=[pltpu.SemaphoreType.DMA((5,))],
        compiler_params=pltpu.CompilerParams(vmem_limit_bytes=VMEM_LIMIT),
    )(*own)
    x_even = swap_even(even, "gx")
    x_odd = swap_odd(odd, "gx")
    y_even = swap_even(tile_even, "gy")
    y_odd = swap_odd(tile_odd, "gy")
    even, odd = call(functools.partial(pack_corners, size_x), (f32(corners, size_z),) * 2)(x_odd, x_even)
    corner_even = swap_even(even, "gy")
    corner_odd = swap_odd(odd, "gy")

    wide = size_y + 2 * RIM

    def room(extra):
        return pltpu.VMEM((size_x + extra, wide, size_z), jnp.float32)

    energy = call(energy_part, f32(8, size_z), [room(2)])(x_odd, x_even, y_odd, y_even, own[0], own[1], own[4])
    mine, other = doubling(energy, y_bits[1:])
    face = f32(FILTER_SWEEPS, size_y, size_z)
    raw = call(
        adjoint_part,
        f32(*shape),
        [room(6), room(6), room(4), room(2), room(5), room(4), room(4), room(4), room(4), room(2)],
        cost=10000000,
    )(x_odd, x_even, y_odd, y_even, corner_odd, corner_even, *own)

    x_odd = swap_odd(call(pack_raw_x_odd, face)(raw), "gx")
    even, energy = call(pack_raw_x_even, (face, f32(8, size_z)))(raw, mine, other)
    x_even = swap_even(even, "gx")
    mine, other = doubling(energy, x_bits)
    _, rows = segments((FILTER_SWEEPS,), size_x)
    even, odd, energy = call(pack_raw_y, (f32(rows + 8, size_z), f32(rows, size_z), f32(8, size_z)))(
        x_odd, x_even, raw, mine, other)
    y_even = swap_even(even, "gy")
    y_odd = swap_odd(odd, "gy")
    energy = energy + y_even[rows:rows + 8]
    mine, other = doubling(energy, y_bits[:1] + [("gx", 1)])
    padded = f32(size_x + 2 * FILTER_SWEEPS, wide, size_z)
    raw, filtered = call(
        filter_first,
        (padded, padded),
        [pltpu.VMEM(padded.shape, jnp.float32)],
        cost=10000000,
    )(x_odd, x_even, y_odd, y_even, raw)
    sensitivity, mean_energy = pl.pallas_call(
        filter_last,
        out_shape=(f32(*shape), f32(1, 1)),
        out_specs=(pl.BlockSpec(memory_space=pl.ANY), pl.BlockSpec(memory_space=pltpu.SMEM)),
        scratch_shapes=[pltpu.VMEM(shape, jnp.float32), pltpu.SemaphoreType.DMA((2,))],
        compiler_params=pltpu.CompilerParams(vmem_limit_bytes=VMEM_LIMIT),
    )(raw, filtered, own[1], mine, other)
    return (sensitivity, mean_energy[0, 0])


def solution(mesh):
    spec = P("gx", "gy", None)
    return jax.shard_map(
        shards, mesh=mesh, in_specs=(spec,) * 5, out_specs=(spec, P()), check_vma=False
    )
```

```python
import functools

import jax
import jax.numpy as jnp
from jax import lax
from jax.experimental import pallas as pl
from jax.experimental.pallas import tpu as pltpu
from jax.sharding import PartitionSpec as P

ADJ_SWEEPS = 2
FILTER_SWEEPS = 4

eps_void = 1.0
eps_solid = 12.0
eps_back = 4.0
eps_metal = 40.0
screen = 0.5
radius_sq = 2.0
epsilon_mean = 1e-06

WIDTHS = (ADJ_SWEEPS + 1, ADJ_SWEEPS + 1, ADJ_SWEEPS, 1)
RIM = 4
VMEM_LIMIT = 24 * 1024 * 1024


def segments(widths, size_x, beside=True, beyond=True):
    found, at = [], 0
    for field, width in enumerate(widths):
        for x in range(-width, size_x + width):
            rows = width - max(0, -x, x - size_x + 1)
            if rows > 0 and (beside if 0 <= x < size_x else beyond):
                found.append((field, x, rows, at))
                at += rows
    return found, -(-at // 8) * 8


def plane_starts(widths):
    starts, at = [], 0
    for width in widths:
        starts.append(at)
        at += width
    return starts, at


def material(density, labels):
    design = eps_void + density * density * density * (eps_solid - eps_void)
    return jnp.where(labels == 1, design, jnp.where(labels == 2, eps_metal, eps_back))


def call(body, outs, scratch=(), in_specs=None, cost=10000):
    kwargs = {} if in_specs is None else {"in_specs": in_specs, "grid": (1,)}
    return pl.pallas_call(
        body,
        out_shape=outs,
        scratch_shapes=list(scratch),
        compiler_params=pltpu.CompilerParams(vmem_limit_bytes=VMEM_LIMIT),
        cost_estimate=pl.CostEstimate(flops=cost, bytes_accessed=cost, transcendentals=0),
        **kwargs,
    )


def f32(*shape):
    return jax.ShapeDtypeStruct(shape, jnp.float32)


def odd_place(axis):
    return lax.rem(lax.axis_index(axis), 2) == 1


def pack_own(*refs):
    inputs, (x_odd_out, x_even_out, y_even_out, y_odd_out), held, sem = refs[:5], refs[5:9], refs[9:14], refs[14]
    density, labels, adjoint, source, potential = held
    size_x, size_y, _ = density.shape
    starts, _ = plane_starts(WIDTHS)
    copies = [pltpu.make_async_copy(a, b, sem.at[k]) for k, (a, b) in enumerate(zip(inputs, held))]
    for copy in copies:
        copy.start()
    copies[0].wait()
    low_first, y_swap = odd_place("gx"), odd_place("gy")
    found, _ = segments(WIDTHS, size_x, beyond=False)
    for field, width in enumerate(WIDTHS):
        copies[field + 1].wait()
        for out, low in ((x_even_out, low_first), (x_odd_out, jnp.logical_not(low_first))):
            span = pl.ds(jnp.where(low, 0, size_x - width), width)
            if field == 0:
                face = material(density[span], labels[span])
            else:
                face = (adjoint, source, potential)[field - 1][span]
            out[pl.ds(starts[field], width)] = face
        for _, x, rows, at in (part for part in found if part[0] == field):
            faces = []
            for rim in (slice(0, rows), slice(size_y - rows, size_y)):
                if field == 0:
                    faces.append(material(density[x, rim], labels[x, rim]))
                else:
                    faces.append((adjoint, source, potential)[field - 1][x, rim])
            low, high = faces
            y_even_out[at:at + rows] = jnp.where(y_swap, low, high)
            y_odd_out[at:at + rows] = jnp.where(y_swap, high, low)


def pack_corners(size_x, x_odd, x_even, even_out, odd_out):
    size_y = x_odd.shape[1]
    starts, _ = plane_starts(WIDTHS)
    x_swap, y_swap = odd_place("gx"), odd_place("gy")
    for field, x, rows, at in segments(WIDTHS, size_x, beside=False)[0]:
        faces = []
        for rim in (slice(0, rows), slice(size_y - rows, size_y)):
            if x < 0:
                plane = starts[field] + WIDTHS[field] + x
                face = jnp.where(x_swap, x_even[plane, rim], x_odd[plane, rim])
            else:
                plane = starts[field] + x - size_x
                face = jnp.where(x_swap, x_odd[plane, rim], x_even[plane, rim])
            faces.append(face)
        low, high = faces
        even_out[at:at + rows] = jnp.where(y_swap, low, high)
        odd_out[at:at + rows] = jnp.where(y_swap, high, low)


def shift(value, by, axis):
    return pltpu.roll(value, by % value.shape[axis], axis)


def planes_loop(low, high, block, step):
    count = high - low
    block = max(k for k in range(1, block + 1) if count % k == 0)

    def body(k, carry):
        step(low + k * block, block)
        return carry

    lax.fori_loop(0, count // block, body, 0)


def unpack_rows(fields, widths, found, even, odd, size_y):
    wide = size_y + 2 * RIM
    swap = odd_place("gy")
    for field, x, rows, at in found:
        if fields[field] is None:
            continue
        a, b = even[at:at + rows], odd[at:at + rows]
        fields[field][x + widths[field], wide - rows:wide] = jnp.where(swap, a, b)
        fields[field][x + widths[field], size_y:size_y + rows] = jnp.where(swap, b, a)


def unpack_planes(field, width, even, odd, size_x, size_y):
    swap = odd_place("gx")
    tile = pl.ds(0, size_y)
    field[pl.ds(0, width), tile] = jnp.where(swap, even, odd)
    field[pl.ds(width + size_x, width), tile] = jnp.where(swap, odd, even)


def energy_part(x_odd, x_even, y_odd, y_even, density, labels, potential, energy_out, poten):
    size_x, size_y, size_z = density.shape
    starts, planes = plane_starts(WIDTHS)
    planes_loop(0, size_x, 4, lambda x, n: poten.__setitem__((pl.ds(x + 1, n), pl.ds(0, size_y)), potential[pl.ds(x, n)]))
    span = pl.ds(starts[3], 1)
    unpack_planes(poten, 1, x_even[span], x_odd[span], size_x, size_y)
    found, _ = segments(WIDTHS, size_x, beyond=False)
    unpack_rows((None, None, None, poten), WIDTHS, found, y_even, y_odd, size_y)
    wide = size_y + 2 * RIM
    lane = lax.broadcasted_iota(jnp.int32, (1, wide, size_z), 2)
    is_first = lane == 0
    is_last = lane == size_z - 1
    energy_out[...] = jnp.zeros_like(energy_out)

    def step(x, n):
        span = pl.ds(x, n)
        v = poten[pl.ds(x + 1, n)]
        low, high = poten[pl.ds(x, n)] - v, poten[pl.ds(x + 2, n)] - v
        squares = low * low + high * high
        dv = shift(v, -1, 1) - v
        square = dv * dv
        squares = squares + square + shift(square, 1, 1)
        dv = jnp.where(is_last, 0.0, shift(v, -1, 2)) - v
        square = dv * dv
        squares = squares + square + jnp.where(is_first, v * v, shift(square, 1, 2))
        energy = material(density[span], labels[span]) * squares[:, :size_y]
        energy_out[...] += jnp.sum(energy.reshape(-1, 8, size_z), axis=0)

    planes_loop(0, size_x, 4, step)


def adjoint_part(x_odd, x_even, y_odd, y_even, corner_odd, corner_even, density, labels, adjoint_start, adjoint_source, potential,
                 raw_out,
                 permit, start, source, poten, face_x, face_y, face_z, inverse, first, second):
    size_x, size_y, size_z = density.shape
    starts, _ = plane_starts(WIDTHS)
    fields = (permit, start, source, poten)
    tile = pl.ds(0, size_y)

    def fill(x, n):
        span = pl.ds(x, n)
        permit[pl.ds(x + WIDTHS[0], n), tile] = material(density[span], labels[span])
        start[pl.ds(x + WIDTHS[1], n), tile] = adjoint_start[span]
        source[pl.ds(x + WIDTHS[2], n), tile] = adjoint_source[span]
        poten[pl.ds(x + WIDTHS[3], n), tile] = potential[span]

    planes_loop(0, size_x, 4, fill)
    for field, width in enumerate(WIDTHS):
        span = pl.ds(starts[field], width)
        unpack_planes(fields[field], width, x_even[span], x_odd[span], size_x, size_y)
    unpack_rows(fields, WIDTHS, segments(WIDTHS, size_x, beyond=False)[0], y_even, y_odd, size_y)
    unpack_rows(fields, WIDTHS, segments(WIDTHS, size_x, beside=False)[0], corner_even, corner_odd, size_y)

    wide = size_y + 2 * RIM
    lane = lax.broadcasted_iota(jnp.int32, (1, wide, size_z), 2)
    is_first = lane == 0
    is_last = lane == size_z - 1

    def inverted(d):
        first_guess = pl.reciprocal(d, approx=True)
        return first_guess * (2.0 - d * first_guess)

    def harmonic(a, b):
        return 2.0 * a * b * inverted(jnp.maximum(a + b, 0.25))

    def faces_x(x, n):
        face_x[pl.ds(x, n)] = harmonic(permit[pl.ds(x, n)], permit[pl.ds(x + 1, n)])

    planes_loop(0, size_x + 5, 7, faces_x)

    def weigh(x, n):
        span = pl.ds(x, n)
        p = permit[pl.ds(x + 1, n)]
        fy = harmonic(p, shift(p, -1, 1))
        fz = jnp.where(is_last, 0.0, harmonic(p, shift(p, -1, 2)))
        face_y[span] = fy
        face_z[span] = fz
        total = screen + face_x[span] + face_x[pl.ds(x + 1, n)] + fy + shift(fy, 1, 1) + fz + shift(fz, 1, 2)
        inverse[span] = jnp.where(p > 20.0, 0.0, inverted(total))

    planes_loop(0, size_x + 4, 10, weigh)

    def relax(x, n, a, a_low, a_high):
        span = pl.ds(x, n)
        fy, fz = face_y[span], face_z[span]
        total = source[span] + face_x[pl.ds(x + 1, n)] * a_high + face_x[span] * a_low
        total = total + fy * shift(a, -1, 1) + shift(fy * a, 1, 1)
        total = total + fz * shift(a, -1, 2) + shift(fz * a, 1, 2)
        return total * inverse[span]

    def sweep_one(x, n):
        first[pl.ds(x, n)] = relax(x, n, start[pl.ds(x + 1, n)], start[pl.ds(x, n)], start[pl.ds(x + 2, n)])

    planes_loop(0, size_x + 4, 10, sweep_one)

    def sweep_two(x, n):
        second[pl.ds(x, n)] = relax(x + 1, n, first[pl.ds(x + 1, n)], first[pl.ds(x, n)], first[pl.ds(x + 2, n)])

    planes_loop(0, size_x + 2, 9, sweep_two)

    def finish(x, n):
        span = pl.ds(x, n)
        v, a = poten[pl.ds(x + 1, n)], second[pl.ds(x + 1, n)]
        product = (poten[pl.ds(x, n)] - v) * (second[pl.ds(x, n)] - a)
        product = product + (poten[pl.ds(x + 2, n)] - v) * (second[pl.ds(x + 2, n)] - a)
        both = (shift(v, -1, 1) - v) * (shift(a, -1, 1) - a)
        product = product + both + shift(both, 1, 1)
        both = (jnp.where(is_last, 0.0, shift(v, -1, 2)) - v) * (jnp.where(is_last, 0.0, shift(a, -1, 2)) - a)
        product = product + both + jnp.where(is_first, v * a, shift(both, 1, 2))
        d = density[span]
        gain = jnp.where(labels[span] == 1, -1.5 * (eps_solid - eps_void) * d * d, 0.0)
        raw_out[span] = gain * product[:, :size_y]

    planes_loop(0, size_x, 8, finish)


def pack_raw_x(raw, out, low):
    out[...] = raw[pl.ds(jnp.where(low, 0, raw.shape[0] - FILTER_SWEEPS), FILTER_SWEEPS)]


def pack_raw_x_odd(raw, out):
    pack_raw_x(raw, out, jnp.logical_not(odd_place("gx")))


def pack_raw_x_even(raw, mine, other, out, energy_out):
    energy_out[...] = mine[...] + other[...]
    pack_raw_x(raw, out, odd_place("gx"))


def pack_raw_y(x_odd, x_even, raw, mine, other, even_out, odd_out, energy_out):
    size_x, size_y, _ = raw.shape
    width = FILTER_SWEEPS
    found, total = segments((width,), size_x)
    x_swap, y_swap = odd_place("gx"), odd_place("gy")
    energy = mine[...] + other[...]
    energy_out[...] = energy
    even_out[total:total + 8] = energy
    for _, x, rows, at in found:
        faces = []
        for rim in (slice(0, rows), slice(size_y - rows, size_y)):
            if x < 0:
                face = jnp.where(x_swap, x_even[width + x, rim], x_odd[width + x, rim])
            elif x >= size_x:
                face = jnp.where(x_swap, x_odd[x - size_x, rim], x_even[x - size_x, rim])
            else:
                face = raw[x, rim]
            faces.append(face)
        low, high = faces
        even_out[at:at + rows] = jnp.where(y_swap, low, high)
        odd_out[at:at + rows] = jnp.where(y_swap, high, low)


def relaxation(raw, size_x, size_y, size_z):
    width = FILTER_SWEEPS
    wide = size_y + 2 * RIM
    extent_x = lax.axis_size("gx") * size_x
    extent_y = lax.axis_size("gy") * size_y
    base_x = lax.axis_index("gx") * size_x - width
    lane = lax.broadcasted_iota(jnp.int32, (1, wide, size_z), 2)
    row = lax.broadcasted_iota(jnp.int32, (1, wide, size_z), 1)
    place = lax.axis_index("gy") * size_y + jnp.where(row < size_y + RIM, row, row - wide)
    is_first, is_last = lane == 0, lane == size_z - 1

    def edges(at, extent):
        return jnp.where(at > 0, 1.0, 0.0) + jnp.where(at < extent - 1, 1.0, 0.0)

    count = edges(place, extent_y) + edges(lane, size_z)
    inside = (place >= 0) & (place < extent_y)
    scale_two = jnp.where(inside, 1.0 / (1.0 + radius_sq * (count + 2.0)), 0.0)
    scale_one = jnp.where(inside, 1.0 / (1.0 + radius_sq * (count + 1.0)), 0.0)

    def relax(src, x, n):
        f = src[pl.ds(x, n)]
        near = src[pl.ds(x - 1, n)] + src[pl.ds(x + 1, n)] + shift(f, 1, 1) + shift(f, -1, 1)
        near = near + jnp.where(is_first, 0.0, shift(f, 1, 2)) + jnp.where(is_last, 0.0, shift(f, -1, 2))
        total = raw[pl.ds(x, n)] + radius_sq * near
        scaled = []
        for k in range(n):
            at = base_x + x + k
            outside = (at < 0) | (at >= extent_x)
            border = (at == 0) | (at == extent_x - 1)
            scale = jnp.where(outside, 0.0, jnp.where(border, scale_one, scale_two))
            scaled.append(total[k:k + 1] * scale)
        return jnp.concatenate(scaled, axis=0)

    return relax


def filter_part(x_odd, x_even, y_odd, y_even, raw_in, labels, out, raw, odd, even):
    size_x, size_y, size_z = raw_in.shape
    width = FILTER_SWEEPS
    tile = pl.ds(0, size_y)

    def fill(x, n):
        raw[pl.ds(x + width, n), tile] = raw_in[pl.ds(x, n)]

    planes_loop(0, size_x, 4, fill)
    unpack_planes(raw, width, x_even[...], x_odd[...], size_x, size_y)
    unpack_rows((raw,), (width,), segments((width,), size_x)[0], y_even, y_odd, size_y)
    relax = relaxation(raw, size_x, size_y, size_z)
    src = raw
    for sweep in range(FILTER_SWEEPS - 1):
        dst = (odd, even)[sweep % 2]

        def step(x, n, src=src, dst=dst):
            dst[pl.ds(x, n)] = relax(src, x, n)

        planes_loop(sweep + 1, size_x + 2 * width - sweep - 1, 11, step)
        src = dst

    def last(x, n):
        f = relax(src, x + width, n)[:, :size_y]
        out[pl.ds(x, n)] = jnp.where(labels[pl.ds(x, n)] == 1, f, 0.0)

    planes_loop(0, size_x, 8, last)


def rescale(filtered, mine, other, out, mean_out, held, sem):
    size_x, size_y, size_z = filtered.shape
    voxels = lax.axis_size("gx") * size_x * lax.axis_size("gy") * size_y * size_z
    mean = 0.5 * jnp.sum(mine[...] + other[...]) / voxels + epsilon_mean
    mean_out[0, 0] = mean
    inverse = 1.0 / jnp.full((1, 1, size_z), mean, jnp.float32)
    block = size_x // 4
    copies = []
    for k in range(4):
        span = pl.ds(k * block, block)
        held[span] = filtered[span] * inverse
        copies.append(pltpu.make_async_copy(held.at[span], out.at[span], sem.at[k]))
        copies[k].start()
    for copy in copies:
        copy.wait()


def swap_even(value, axis):
    return lax.ppermute(value, axis, [(i, i ^ 1) for i in range(lax.axis_size(axis))])


def swap_odd(value, axis):
    count = lax.axis_size(axis)
    up = [(i, i + 1) for i in range(1, count - 1, 2)]
    return lax.ppermute(value, axis, up + [(b, a) for a, b in up])


def partner(value, axis, bit):
    return lax.ppermute(value, axis, [(i, i ^ bit) for i in range(lax.axis_size(axis))])


def doubling(energy, stages):
    other = partner(energy, *stages[0])
    for stage in stages[1:]:
        energy = energy + other
        other = partner(energy, *stage)
    return energy, other


def shards(density, potential, adjoint_start, adjoint_source, labels):
    size_x, size_y, size_z = potential.shape
    _, planes = plane_starts(WIDTHS)
    _, rows = segments(WIDTHS, size_x, beyond=False)
    _, corners = segments(WIDTHS, size_x, beside=False)
    own = [
        pltpu.with_memory_space_constraint(array, pltpu.HBM)
        for array in (density, labels, adjoint_start, adjoint_source, potential)
    ]
    x_bits = [("gx", 1 << k) for k in range(1, (lax.axis_size("gx") - 1).bit_length())]
    y_bits = [("gy", 1 << k) for k in range(1, (lax.axis_size("gy") - 1).bit_length())]

    shape = (size_x, size_y, size_z)
    odd, even, tile_even, tile_odd, *own = pl.pallas_call(
        pack_own,
        out_shape=(f32(planes, size_y, size_z),) * 2 + (f32(rows, size_z),) * 2
        + (f32(*shape), jax.ShapeDtypeStruct(shape, jnp.int32)) + (f32(*shape),) * 3,
        in_specs=[pl.BlockSpec(memory_space=pltpu.HBM)] * 5,
        scratch_shapes=[pltpu.SemaphoreType.DMA((5,))],
        compiler_params=pltpu.CompilerParams(vmem_limit_bytes=VMEM_LIMIT),
    )(*own)
    x_even = swap_even(even, "gx")
    x_odd = swap_odd(odd, "gx")
    y_even = swap_even(tile_even, "gy")
    y_odd = swap_odd(tile_odd, "gy")
    even, odd = call(functools.partial(pack_corners, size_x), (f32(corners, size_z),) * 2)(x_odd, x_even)
    corner_even = swap_even(even, "gy")
    corner_odd = swap_odd(odd, "gy")

    wide = size_y + 2 * RIM

    def room(extra):
        return pltpu.VMEM((size_x + extra, wide, size_z), jnp.float32)

    energy = call(energy_part, f32(8, size_z), [room(2)])(x_odd, x_even, y_odd, y_even, own[0], own[1], own[4])
    mine, other = doubling(energy, y_bits[1:])
    face = f32(FILTER_SWEEPS, size_y, size_z)
    raw = call(
        adjoint_part,
        f32(*shape),
        [room(6), room(6), room(4), room(2), room(5), room(4), room(4), room(4), room(4), room(2)],
        cost=10000000,
    )(x_odd, x_even, y_odd, y_even, corner_odd, corner_even, *own)

    x_odd = swap_odd(call(pack_raw_x_odd, face)(raw), "gx")
    even, energy = call(pack_raw_x_even, (face, f32(8, size_z)))(raw, mine, other)
    x_even = swap_even(even, "gx")
    mine, other = doubling(energy, x_bits)
    _, rows = segments((FILTER_SWEEPS,), size_x)
    even, odd, energy = call(pack_raw_y, (f32(rows + 8, size_z), f32(rows, size_z), f32(8, size_z)))(
        x_odd, x_even, raw, mine, other)
    y_even = swap_even(even, "gy")
    y_odd = swap_odd(odd, "gy")
    energy = energy + y_even[rows:rows + 8]
    mine, other = doubling(energy, y_bits[:1] + [("gx", 1)])
    filtered = call(
        filter_part,
        f32(*shape),
        [room(2 * FILTER_SWEEPS)] * 3,
        cost=10000000,
    )(x_odd, x_even, y_odd, y_even, raw, own[1])
    sensitivity, mean_energy = pl.pallas_call(
        rescale,
        out_shape=(f32(*shape), f32(1, 1)),
        out_specs=(pl.BlockSpec(memory_space=pl.ANY), pl.BlockSpec(memory_space=pltpu.SMEM)),
        scratch_shapes=[pltpu.VMEM(shape, jnp.float32), pltpu.SemaphoreType.DMA((4,))],
        compiler_params=pltpu.CompilerParams(vmem_limit_bytes=VMEM_LIMIT),
    )(filtered, mine, other)
    return (sensitivity, mean_energy[0, 0])


def solution(mesh):
    spec = P("gx", "gy", None)
    return jax.shard_map(
        shards, mesh=mesh, in_specs=(spec,) * 5, out_specs=(spec, P()), check_vma=False
    )
```

```python
import functools

import jax
import jax.numpy as jnp
from jax import lax
from jax.experimental import pallas as pl
from jax.experimental.pallas import tpu as pltpu
from jax.sharding import PartitionSpec as P

ADJ_SWEEPS = 2
FILTER_SWEEPS = 4

eps_void = 1.0
eps_solid = 12.0
eps_back = 4.0
eps_metal = 40.0
screen = 0.5
radius_sq = 2.0
epsilon_mean = 1e-06

WIDTHS = (ADJ_SWEEPS + 1, ADJ_SWEEPS + 1, ADJ_SWEEPS, 1)
RIM = 4
VMEM_LIMIT = 24 * 1024 * 1024


def segments(widths, size_x, beside=True, beyond=True):
    found, at = [], 0
    for field, width in enumerate(widths):
        for x in range(-width, size_x + width):
            rows = width - max(0, -x, x - size_x + 1)
            if rows > 0 and (beside if 0 <= x < size_x else beyond):
                found.append((field, x, rows, at))
                at += rows
    return found, -(-at // 8) * 8


def plane_starts(widths):
    starts, at = [], 0
    for width in widths:
        starts.append(at)
        at += width
    return starts, at


def material(density, labels):
    design = eps_void + density * density * density * (eps_solid - eps_void)
    return jnp.where(labels == 1, design, jnp.where(labels == 2, eps_metal, eps_back))


def call(body, outs, scratch=(), in_specs=None, cost=10000):
    kwargs = {} if in_specs is None else {"in_specs": in_specs, "grid": (1,)}
    return pl.pallas_call(
        body,
        out_shape=outs,
        scratch_shapes=list(scratch),
        compiler_params=pltpu.CompilerParams(vmem_limit_bytes=VMEM_LIMIT),
        cost_estimate=pl.CostEstimate(flops=cost, bytes_accessed=cost, transcendentals=0),
        **kwargs,
    )


def f32(*shape):
    return jax.ShapeDtypeStruct(shape, jnp.float32)


def odd_place(axis):
    return lax.rem(lax.axis_index(axis), 2) == 1


def pack_own(*refs):
    inputs, (x_odd_out, x_even_out, y_even_out, y_odd_out), held, sem = refs[:5], refs[5:9], refs[9:14], refs[14]
    density, labels, adjoint, source, potential = held
    size_x, size_y, _ = density.shape
    starts, _ = plane_starts(WIDTHS)
    copies = [pltpu.make_async_copy(a, b, sem.at[k]) for k, (a, b) in enumerate(zip(inputs, held))]
    for copy in copies:
        copy.start()
    copies[0].wait()
    low_first, y_swap = odd_place("gx"), odd_place("gy")
    found, _ = segments(WIDTHS, size_x, beyond=False)
    for field, width in enumerate(WIDTHS):
        copies[field + 1].wait()
        for out, low in ((x_even_out, low_first), (x_odd_out, jnp.logical_not(low_first))):
            span = pl.ds(jnp.where(low, 0, size_x - width), width)
            if field == 0:
                face = material(density[span], labels[span])
            else:
                face = (adjoint, source, potential)[field - 1][span]
            out[pl.ds(starts[field], width)] = face
        for _, x, rows, at in (part for part in found if part[0] == field):
            faces = []
            for rim in (slice(0, rows), slice(size_y - rows, size_y)):
                if field == 0:
                    faces.append(material(density[x, rim], labels[x, rim]))
                else:
                    faces.append((adjoint, source, potential)[field - 1][x, rim])
            low, high = faces
            y_even_out[at:at + rows] = jnp.where(y_swap, low, high)
            y_odd_out[at:at + rows] = jnp.where(y_swap, high, low)


def pack_corners(size_x, x_odd, x_even, even_out, odd_out):
    size_y = x_odd.shape[1]
    starts, _ = plane_starts(WIDTHS)
    x_swap, y_swap = odd_place("gx"), odd_place("gy")
    for field, x, rows, at in segments(WIDTHS, size_x, beside=False)[0]:
        faces = []
        for rim in (slice(0, rows), slice(size_y - rows, size_y)):
            if x < 0:
                plane = starts[field] + WIDTHS[field] + x
                face = jnp.where(x_swap, x_even[plane, rim], x_odd[plane, rim])
            else:
                plane = starts[field] + x - size_x
                face = jnp.where(x_swap, x_odd[plane, rim], x_even[plane, rim])
            faces.append(face)
        low, high = faces
        even_out[at:at + rows] = jnp.where(y_swap, low, high)
        odd_out[at:at + rows] = jnp.where(y_swap, high, low)


def shift(value, by, axis):
    return pltpu.roll(value, by % value.shape[axis], axis)


def planes_loop(low, high, block, step):
    count = high - low
    block = max(k for k in range(1, block + 1) if count % k == 0)

    def body(k, carry):
        step(low + k * block, block)
        return carry

    lax.fori_loop(0, count // block, body, 0)


def unpack_rows(fields, widths, found, even, odd, size_y):
    wide = size_y + 2 * RIM
    swap = odd_place("gy")
    for field, x, rows, at in found:
        if fields[field] is None:
            continue
        a, b = even[at:at + rows], odd[at:at + rows]
        fields[field][x + widths[field], wide - rows:wide] = jnp.where(swap, a, b)
        fields[field][x + widths[field], size_y:size_y + rows] = jnp.where(swap, b, a)


def unpack_planes(field, width, even, odd, size_x, size_y):
    swap = odd_place("gx")
    tile = pl.ds(0, size_y)
    field[pl.ds(0, width), tile] = jnp.where(swap, even, odd)
    field[pl.ds(width + size_x, width), tile] = jnp.where(swap, odd, even)


def energy_part(x_odd, x_even, y_odd, y_even, density, labels, potential, energy_out, poten):
    size_x, size_y, size_z = density.shape
    starts, planes = plane_starts(WIDTHS)
    planes_loop(0, size_x, 4, lambda x, n: poten.__setitem__((pl.ds(x + 1, n), pl.ds(0, size_y)), potential[pl.ds(x, n)]))
    span = pl.ds(starts[3], 1)
    unpack_planes(poten, 1, x_even[span], x_odd[span], size_x, size_y)
    found, _ = segments(WIDTHS, size_x, beyond=False)
    unpack_rows((None, None, None, poten), WIDTHS, found, y_even, y_odd, size_y)
    wide = size_y + 2 * RIM
    lane = lax.broadcasted_iota(jnp.int32, (1, wide, size_z), 2)
    is_first = lane == 0
    is_last = lane == size_z - 1
    energy_out[...] = jnp.zeros_like(energy_out)

    def step(x, n):
        span = pl.ds(x, n)
        v = poten[pl.ds(x + 1, n)]
        low, high = poten[pl.ds(x, n)] - v, poten[pl.ds(x + 2, n)] - v
        squares = low * low + high * high
        dv = shift(v, -1, 1) - v
        square = dv * dv
        squares = squares + square + shift(square, 1, 1)
        dv = jnp.where(is_last, 0.0, shift(v, -1, 2)) - v
        square = dv * dv
        squares = squares + square + jnp.where(is_first, v * v, shift(square, 1, 2))
        energy = material(density[span], labels[span]) * squares[:, :size_y]
        energy_out[...] += jnp.sum(energy.reshape(-1, 8, size_z), axis=0)

    planes_loop(0, size_x, 4, step)


def adjoint_part(x_odd, x_even, y_odd, y_even, corner_odd, corner_even, density, labels, adjoint_start, adjoint_source, potential,
                 raw_out,
                 permit, start, source, poten, face_x, face_y, face_z, inverse, first, second):
    size_x, size_y, size_z = density.shape
    starts, _ = plane_starts(WIDTHS)
    fields = (permit, start, source, poten)
    tile = pl.ds(0, size_y)

    def fill(x, n):
        span = pl.ds(x, n)
        permit[pl.ds(x + WIDTHS[0], n), tile] = material(density[span], labels[span])
        start[pl.ds(x + WIDTHS[1], n), tile] = adjoint_start[span]
        source[pl.ds(x + WIDTHS[2], n), tile] = adjoint_source[span]
        poten[pl.ds(x + WIDTHS[3], n), tile] = potential[span]

    planes_loop(0, size_x, 4, fill)
    for field, width in enumerate(WIDTHS):
        span = pl.ds(starts[field], width)
        unpack_planes(fields[field], width, x_even[span], x_odd[span], size_x, size_y)
    unpack_rows(fields, WIDTHS, segments(WIDTHS, size_x, beyond=False)[0], y_even, y_odd, size_y)
    unpack_rows(fields, WIDTHS, segments(WIDTHS, size_x, beside=False)[0], corner_even, corner_odd, size_y)

    wide = size_y + 2 * RIM
    lane = lax.broadcasted_iota(jnp.int32, (1, wide, size_z), 2)
    is_first = lane == 0
    is_last = lane == size_z - 1

    def inverted(d):
        first_guess = pl.reciprocal(d, approx=True)
        return first_guess * (2.0 - d * first_guess)

    def harmonic(a, b):
        return 2.0 * a * b * inverted(jnp.maximum(a + b, 0.25))

    def faces_x(x, n):
        face_x[pl.ds(x, n)] = harmonic(permit[pl.ds(x, n)], permit[pl.ds(x + 1, n)])

    planes_loop(0, size_x + 5, 7, faces_x)

    def weigh(x, n):
        span = pl.ds(x, n)
        p = permit[pl.ds(x + 1, n)]
        fy = harmonic(p, shift(p, -1, 1))
        fz = jnp.where(is_last, 0.0, harmonic(p, shift(p, -1, 2)))
        face_y[span] = fy
        face_z[span] = fz
        total = screen + face_x[span] + face_x[pl.ds(x + 1, n)] + fy + shift(fy, 1, 1) + fz + shift(fz, 1, 2)
        inverse[span] = jnp.where(p > 20.0, 0.0, inverted(total))

    planes_loop(0, size_x + 4, 10, weigh)

    def relax(x, n, a, a_low, a_high):
        span = pl.ds(x, n)
        fy, fz = face_y[span], face_z[span]
        total = source[span] + face_x[pl.ds(x + 1, n)] * a_high + face_x[span] * a_low
        total = total + fy * shift(a, -1, 1) + shift(fy * a, 1, 1)
        total = total + fz * shift(a, -1, 2) + shift(fz * a, 1, 2)
        return total * inverse[span]

    def sweep_one(x, n):
        first[pl.ds(x, n)] = relax(x, n, start[pl.ds(x + 1, n)], start[pl.ds(x, n)], start[pl.ds(x + 2, n)])

    planes_loop(0, size_x + 4, 10, sweep_one)

    def sweep_two(x, n):
        second[pl.ds(x, n)] = relax(x + 1, n, first[pl.ds(x + 1, n)], first[pl.ds(x, n)], first[pl.ds(x + 2, n)])

    planes_loop(0, size_x + 2, 9, sweep_two)

    def finish(x, n):
        span = pl.ds(x, n)
        v, a = poten[pl.ds(x + 1, n)], second[pl.ds(x + 1, n)]
        product = (poten[pl.ds(x, n)] - v) * (second[pl.ds(x, n)] - a)
        product = product + (poten[pl.ds(x + 2, n)] - v) * (second[pl.ds(x + 2, n)] - a)
        both = (shift(v, -1, 1) - v) * (shift(a, -1, 1) - a)
        product = product + both + shift(both, 1, 1)
        both = (jnp.where(is_last, 0.0, shift(v, -1, 2)) - v) * (jnp.where(is_last, 0.0, shift(a, -1, 2)) - a)
        product = product + both + jnp.where(is_first, v * a, shift(both, 1, 2))
        d = density[span]
        gain = jnp.where(labels[span] == 1, -1.5 * (eps_solid - eps_void) * d * d, 0.0)
        raw_out[span] = gain * product[:, :size_y]

    planes_loop(0, size_x, 8, finish)


def pack_raw_x(raw, out, low):
    out[...] = raw[pl.ds(jnp.where(low, 0, raw.shape[0] - FILTER_SWEEPS), FILTER_SWEEPS)]


def pack_raw_x_odd(raw, out):
    pack_raw_x(raw, out, jnp.logical_not(odd_place("gx")))


def pack_raw_x_even(raw, mine, other, out, energy_out):
    energy_out[...] = mine[...] + other[...]
    pack_raw_x(raw, out, odd_place("gx"))


def pack_raw_y(x_odd, x_even, raw, mine, other, even_out, odd_out, energy_out):
    size_x, size_y, _ = raw.shape
    width = FILTER_SWEEPS
    found, total = segments((width,), size_x)
    x_swap, y_swap = odd_place("gx"), odd_place("gy")
    energy = mine[...] + other[...]
    energy_out[...] = energy
    even_out[total:total + 8] = energy
    for _, x, rows, at in found:
        faces = []
        for rim in (slice(0, rows), slice(size_y - rows, size_y)):
            if x < 0:
                face = jnp.where(x_swap, x_even[width + x, rim], x_odd[width + x, rim])
            elif x >= size_x:
                face = jnp.where(x_swap, x_odd[x - size_x, rim], x_even[x - size_x, rim])
            else:
                face = raw[x, rim]
            faces.append(face)
        low, high = faces
        even_out[at:at + rows] = jnp.where(y_swap, low, high)
        odd_out[at:at + rows] = jnp.where(y_swap, high, low)


def relaxation(raw, size_x, size_y, size_z):
    width = FILTER_SWEEPS
    wide = size_y + 2 * RIM
    extent_x = lax.axis_size("gx") * size_x
    extent_y = lax.axis_size("gy") * size_y
    base_x = lax.axis_index("gx") * size_x - width
    lane = lax.broadcasted_iota(jnp.int32, (1, wide, size_z), 2)
    row = lax.broadcasted_iota(jnp.int32, (1, wide, size_z), 1)
    place = lax.axis_index("gy") * size_y + jnp.where(row < size_y + RIM, row, row - wide)
    is_first, is_last = lane == 0, lane == size_z - 1

    def edges(at, extent):
        return jnp.where(at > 0, 1.0, 0.0) + jnp.where(at < extent - 1, 1.0, 0.0)

    count = edges(place, extent_y) + edges(lane, size_z)
    inside = (place >= 0) & (place < extent_y)
    scale_two = jnp.where(inside, 1.0 / (1.0 + radius_sq * (count + 2.0)), 0.0)
    scale_one = jnp.where(inside, 1.0 / (1.0 + radius_sq * (count + 1.0)), 0.0)

    def relax(src, x, n):
        f = src[pl.ds(x, n)]
        near = src[pl.ds(x - 1, n)] + src[pl.ds(x + 1, n)] + shift(f, 1, 1) + shift(f, -1, 1)
        near = near + jnp.where(is_first, 0.0, shift(f, 1, 2)) + jnp.where(is_last, 0.0, shift(f, -1, 2))
        total = raw[pl.ds(x, n)] + radius_sq * near
        scaled = []
        for k in range(n):
            at = base_x + x + k
            outside = (at < 0) | (at >= extent_x)
            border = (at == 0) | (at == extent_x - 1)
            scale = jnp.where(outside, 0.0, jnp.where(border, scale_one, scale_two))
            scaled.append(total[k:k + 1] * scale)
        return jnp.concatenate(scaled, axis=0)

    return relax


def filter_part(x_odd, x_even, y_odd, y_even, raw_in, labels, out, raw, odd, even):
    size_x, size_y, size_z = raw_in.shape
    width = FILTER_SWEEPS
    tile = pl.ds(0, size_y)

    def fill(x, n):
        raw[pl.ds(x + width, n), tile] = raw_in[pl.ds(x, n)]

    planes_loop(0, size_x, 4, fill)
    unpack_planes(raw, width, x_even[...], x_odd[...], size_x, size_y)
    unpack_rows((raw,), (width,), segments((width,), size_x)[0], y_even, y_odd, size_y)
    relax = relaxation(raw, size_x, size_y, size_z)
    src = raw
    for sweep in range(FILTER_SWEEPS - 1):
        dst = (odd, even)[sweep % 2]

        def step(x, n, src=src, dst=dst):
            dst[pl.ds(x, n)] = relax(src, x, n)

        planes_loop(sweep + 1, size_x + 2 * width - sweep - 1, 11, step)
        src = dst

    def last(x, n):
        f = relax(src, x + width, n)[:, :size_y]
        out[pl.ds(x, n)] = jnp.where(labels[pl.ds(x, n)] == 1, f, 0.0)

    planes_loop(0, size_x, 8, last)


def rescale(filtered, mine, other, out, mean_out):
    size_x, size_y, size_z = filtered.shape
    voxels = lax.axis_size("gx") * size_x * lax.axis_size("gy") * size_y * size_z
    mean = 0.5 * jnp.sum(mine[...] + other[...]) / voxels + epsilon_mean
    mean_out[0, 0] = mean
    out[...] = filtered[...] * (1.0 / jnp.full((1, 1, size_z), mean, jnp.float32))


def swap_even(value, axis):
    return lax.ppermute(value, axis, [(i, i ^ 1) for i in range(lax.axis_size(axis))])


def swap_odd(value, axis):
    count = lax.axis_size(axis)
    up = [(i, i + 1) for i in range(1, count - 1, 2)]
    return lax.ppermute(value, axis, up + [(b, a) for a, b in up])


def partner(value, axis, bit):
    return lax.ppermute(value, axis, [(i, i ^ bit) for i in range(lax.axis_size(axis))])


def doubling(energy, stages):
    other = partner(energy, *stages[0])
    for stage in stages[1:]:
        energy = energy + other
        other = partner(energy, *stage)
    return energy, other


def shards(density, potential, adjoint_start, adjoint_source, labels):
    size_x, size_y, size_z = potential.shape
    _, planes = plane_starts(WIDTHS)
    _, rows = segments(WIDTHS, size_x, beyond=False)
    _, corners = segments(WIDTHS, size_x, beside=False)
    own = [
        pltpu.with_memory_space_constraint(array, pltpu.HBM)
        for array in (density, labels, adjoint_start, adjoint_source, potential)
    ]
    x_bits = [("gx", 1 << k) for k in range(1, (lax.axis_size("gx") - 1).bit_length())]
    y_bits = [("gy", 1 << k) for k in range(1, (lax.axis_size("gy") - 1).bit_length())]

    shape = (size_x, size_y, size_z)
    odd, even, tile_even, tile_odd, *own = pl.pallas_call(
        pack_own,
        out_shape=(f32(planes, size_y, size_z),) * 2 + (f32(rows, size_z),) * 2
        + (f32(*shape), jax.ShapeDtypeStruct(shape, jnp.int32)) + (f32(*shape),) * 3,
        in_specs=[pl.BlockSpec(memory_space=pltpu.HBM)] * 5,
        scratch_shapes=[pltpu.SemaphoreType.DMA((5,))],
        compiler_params=pltpu.CompilerParams(vmem_limit_bytes=VMEM_LIMIT),
    )(*own)
    x_even = swap_even(even, "gx")
    x_odd = swap_odd(odd, "gx")
    y_even = swap_even(tile_even, "gy")
    y_odd = swap_odd(tile_odd, "gy")
    even, odd = call(functools.partial(pack_corners, size_x), (f32(corners, size_z),) * 2)(x_odd, x_even)
    corner_even = swap_even(even, "gy")
    corner_odd = swap_odd(odd, "gy")

    wide = size_y + 2 * RIM

    def room(extra):
        return pltpu.VMEM((size_x + extra, wide, size_z), jnp.float32)

    energy = call(energy_part, f32(8, size_z), [room(2)])(x_odd, x_even, y_odd, y_even, own[0], own[1], own[4])
    mine, other = doubling(energy, y_bits[1:])
    face = f32(FILTER_SWEEPS, size_y, size_z)
    raw = call(
        adjoint_part,
        f32(*shape),
        [room(6), room(6), room(4), room(2), room(5), room(4), room(4), room(4), room(4), room(2)],
        cost=10000000,
    )(x_odd, x_even, y_odd, y_even, corner_odd, corner_even, *own)

    x_odd = swap_odd(call(pack_raw_x_odd, face)(raw), "gx")
    even, energy = call(pack_raw_x_even, (face, f32(8, size_z)))(raw, mine, other)
    x_even = swap_even(even, "gx")
    mine, other = doubling(energy, x_bits)
    _, rows = segments((FILTER_SWEEPS,), size_x)
    even, odd, energy = call(pack_raw_y, (f32(rows + 8, size_z), f32(rows, size_z), f32(8, size_z)))(
        x_odd, x_even, raw, mine, other)
    y_even = swap_even(even, "gy")
    y_odd = swap_odd(odd, "gy")
    energy = energy + y_even[rows:rows + 8]
    mine, other = doubling(energy, y_bits[:1] + [("gx", 1)])
    filtered = call(
        filter_part,
        f32(*shape),
        [room(2 * FILTER_SWEEPS)] * 3,
        cost=10000000,
    )(x_odd, x_even, y_odd, y_even, raw, own[1])
    sensitivity, mean_energy = pl.pallas_call(
        rescale,
        out_shape=(f32(*shape), f32(1, 1)),
        out_specs=(pl.BlockSpec(memory_space=pltpu.VMEM), pl.BlockSpec(memory_space=pltpu.SMEM)),
        compiler_params=pltpu.CompilerParams(vmem_limit_bytes=VMEM_LIMIT),
    )(filtered, mine, other)
    return (sensitivity, mean_energy[0, 0])


def solution(mesh):
    spec = P("gx", "gy", None)
    return jax.shard_map(
        shards, mesh=mesh, in_specs=(spec,) * 5, out_specs=(spec, P()), check_vma=False
    )
```

```python
import functools

import jax
import jax.numpy as jnp
from jax import lax
from jax.experimental import pallas as pl
from jax.experimental.pallas import tpu as pltpu
from jax.sharding import PartitionSpec as P

ADJ_SWEEPS = 2
FILTER_SWEEPS = 4

eps_void = 1.0
eps_solid = 12.0
eps_back = 4.0
eps_metal = 40.0
screen = 0.5
radius_sq = 2.0
epsilon_mean = 1e-06

WIDTHS = (ADJ_SWEEPS + 1, ADJ_SWEEPS + 1, ADJ_SWEEPS, 1)
RIM = 4
VMEM_LIMIT = 24 * 1024 * 1024


def segments(widths, size_x, beside=True, beyond=True):
    found, at = [], 0
    for field, width in enumerate(widths):
        for x in range(-width, size_x + width):
            rows = width - max(0, -x, x - size_x + 1)
            if rows > 0 and (beside if 0 <= x < size_x else beyond):
                found.append((field, x, rows, at))
                at += rows
    return found, -(-at // 8) * 8


def plane_starts(widths):
    starts, at = [], 0
    for width in widths:
        starts.append(at)
        at += width
    return starts, at


def material(density, labels):
    design = eps_void + density * density * density * (eps_solid - eps_void)
    return jnp.where(labels == 1, design, jnp.where(labels == 2, eps_metal, eps_back))


def call(body, outs, scratch=(), in_specs=None, cost=10000):
    kwargs = {} if in_specs is None else {"in_specs": in_specs, "grid": (1,)}
    return pl.pallas_call(
        body,
        out_shape=outs,
        scratch_shapes=list(scratch),
        compiler_params=pltpu.CompilerParams(vmem_limit_bytes=VMEM_LIMIT),
        cost_estimate=pl.CostEstimate(flops=cost, bytes_accessed=cost, transcendentals=0),
        **kwargs,
    )


def f32(*shape):
    return jax.ShapeDtypeStruct(shape, jnp.float32)


def odd_place(axis):
    return lax.rem(lax.axis_index(axis), 2) == 1


def pack_own(*refs):
    inputs, (x_odd_out, x_even_out, y_even_out, y_odd_out), held, sem = refs[:5], refs[5:9], refs[9:14], refs[14]
    density, labels, adjoint, source, potential = held
    size_x, size_y, _ = density.shape
    starts, _ = plane_starts(WIDTHS)
    copies = [pltpu.make_async_copy(a, b, sem.at[k]) for k, (a, b) in enumerate(zip(inputs, held))]
    for copy in copies:
        copy.start()
    copies[0].wait()
    low_first, y_swap = odd_place("gx"), odd_place("gy")
    found, _ = segments(WIDTHS, size_x, beyond=False)
    for field, width in enumerate(WIDTHS):
        copies[field + 1].wait()
        for out, low in ((x_even_out, low_first), (x_odd_out, jnp.logical_not(low_first))):
            span = pl.ds(jnp.where(low, 0, size_x - width), width)
            if field == 0:
                face = material(density[span], labels[span])
            else:
                face = (adjoint, source, potential)[field - 1][span]
            out[pl.ds(starts[field], width)] = face
        for _, x, rows, at in (part for part in found if part[0] == field):
            faces = []
            for rim in (slice(0, rows), slice(size_y - rows, size_y)):
                if field == 0:
                    faces.append(material(density[x, rim], labels[x, rim]))
                else:
                    faces.append((adjoint, source, potential)[field - 1][x, rim])
            low, high = faces
            y_even_out[at:at + rows] = jnp.where(y_swap, low, high)
            y_odd_out[at:at + rows] = jnp.where(y_swap, high, low)


def pack_corners(size_x, x_odd, x_even, even_out, odd_out):
    size_y = x_odd.shape[1]
    starts, _ = plane_starts(WIDTHS)
    x_swap, y_swap = odd_place("gx"), odd_place("gy")
    for field, x, rows, at in segments(WIDTHS, size_x, beside=False)[0]:
        faces = []
        for rim in (slice(0, rows), slice(size_y - rows, size_y)):
            if x < 0:
                plane = starts[field] + WIDTHS[field] + x
                face = jnp.where(x_swap, x_even[plane, rim], x_odd[plane, rim])
            else:
                plane = starts[field] + x - size_x
                face = jnp.where(x_swap, x_odd[plane, rim], x_even[plane, rim])
            faces.append(face)
        low, high = faces
        even_out[at:at + rows] = jnp.where(y_swap, low, high)
        odd_out[at:at + rows] = jnp.where(y_swap, high, low)


def shift(value, by, axis):
    return pltpu.roll(value, by % value.shape[axis], axis)


def planes_loop(low, high, block, step):
    count = high - low
    block = max(k for k in range(1, block + 1) if count % k == 0)

    def body(k, carry):
        step(low + k * block, block)
        return carry

    lax.fori_loop(0, count // block, body, 0)


def unpack_rows(fields, widths, found, even, odd, size_y):
    wide = size_y + 2 * RIM
    swap = odd_place("gy")
    for field, x, rows, at in found:
        if fields[field] is None:
            continue
        a, b = even[at:at + rows], odd[at:at + rows]
        fields[field][x + widths[field], wide - rows:wide] = jnp.where(swap, a, b)
        fields[field][x + widths[field], size_y:size_y + rows] = jnp.where(swap, b, a)


def unpack_planes(field, width, even, odd, size_x, size_y):
    swap = odd_place("gx")
    tile = pl.ds(0, size_y)
    field[pl.ds(0, width), tile] = jnp.where(swap, even, odd)
    field[pl.ds(width + size_x, width), tile] = jnp.where(swap, odd, even)


def energy_part(x_odd, x_even, y_odd, y_even, density, labels, potential, energy_out, poten):
    size_x, size_y, size_z = density.shape
    starts, planes = plane_starts(WIDTHS)
    planes_loop(0, size_x, 4, lambda x, n: poten.__setitem__((pl.ds(x + 1, n), pl.ds(0, size_y)), potential[pl.ds(x, n)]))
    span = pl.ds(starts[3], 1)
    unpack_planes(poten, 1, x_even[span], x_odd[span], size_x, size_y)
    found, _ = segments(WIDTHS, size_x, beyond=False)
    unpack_rows((None, None, None, poten), WIDTHS, found, y_even, y_odd, size_y)
    wide = size_y + 2 * RIM
    lane = lax.broadcasted_iota(jnp.int32, (1, wide, size_z), 2)
    is_first = lane == 0
    is_last = lane == size_z - 1
    energy_out[...] = jnp.zeros_like(energy_out)

    def step(x, n):
        span = pl.ds(x, n)
        v = poten[pl.ds(x + 1, n)]
        low, high = poten[pl.ds(x, n)] - v, poten[pl.ds(x + 2, n)] - v
        squares = low * low + high * high
        dv = shift(v, -1, 1) - v
        square = dv * dv
        squares = squares + square + shift(square, 1, 1)
        dv = jnp.where(is_last, 0.0, shift(v, -1, 2)) - v
        square = dv * dv
        squares = squares + square + jnp.where(is_first, v * v, shift(square, 1, 2))
        energy = material(density[span], labels[span]) * squares[:, :size_y]
        energy_out[...] += jnp.sum(energy.reshape(-1, 8, size_z), axis=0)

    planes_loop(0, size_x, 4, step)


def inverted(d):
    first_guess = pl.reciprocal(d, approx=True)
    return first_guess * (2.0 - d * first_guess)


def harmonic(a, b):
    return 2.0 * a * b * inverted(jnp.maximum(a + b, 0.25))


def weigh(permit, face_x, face_y, face_z, inverse, x, k, n):
    p = permit[pl.ds(x, n)]
    span = pl.ds(k, n)
    is_last = lax.broadcasted_iota(jnp.int32, (1,) + p.shape[1:], 2) == p.shape[2] - 1
    fy = harmonic(p, shift(p, -1, 1))
    fz = jnp.where(is_last, 0.0, harmonic(p, shift(p, -1, 2)))
    face_y[span] = fy
    face_z[span] = fz
    total = screen + face_x[span] + face_x[pl.ds(k + 1, n)] + fy + shift(fy, 1, 1) + fz + shift(fz, 1, 2)
    inverse[span] = jnp.where(p > 20.0, 0.0, inverted(total))


def inner_weights(y_odd, y_even, density, labels, face_x, face_y, face_z, inverse, permit):
    size_x, size_y, _ = density.shape

    def fill(x, n):
        permit[pl.ds(x, n), pl.ds(0, size_y)] = material(density[pl.ds(x, n)], labels[pl.ds(x, n)])

    planes_loop(0, size_x, 8, fill)
    found = [part for part in segments(WIDTHS, size_x, beyond=False)[0] if part[0] == 0]
    unpack_rows((permit,), (0,), found, y_even, y_odd, size_y)

    def faces(x, n):
        face_x[pl.ds(x, n)] = harmonic(permit[pl.ds(x, n)], permit[pl.ds(x + 1, n)])

    planes_loop(0, size_x - 1, 5, faces)
    planes_loop(0, size_x - 2, 7, lambda k, n: weigh(permit, face_x, face_y, face_z, inverse, k + 1, k, n))


def adjoint_part(x_odd, x_even, y_odd, y_even, corner_odd, corner_even, density, labels, adjoint_start, adjoint_source, potential,
                 inner_x, inner_y, inner_z, inner_inverse, raw_out,
                 permit, start, source, poten, edge_x, edge_y, edge_z, edge_inverse, first, second):
    size_x, size_y, size_z = density.shape
    starts, _ = plane_starts(WIDTHS)
    fields = (permit, start, source, poten)
    tile = pl.ds(0, size_y)

    def fill(x, n):
        span = pl.ds(x, n)
        permit[pl.ds(x + WIDTHS[0], n), tile] = material(density[span], labels[span])
        start[pl.ds(x + WIDTHS[1], n), tile] = adjoint_start[span]
        source[pl.ds(x + WIDTHS[2], n), tile] = adjoint_source[span]
        poten[pl.ds(x + WIDTHS[3], n), tile] = potential[span]

    planes_loop(0, size_x, 4, fill)
    for field, width in enumerate(WIDTHS):
        span = pl.ds(starts[field], width)
        unpack_planes(fields[field], width, x_even[span], x_odd[span], size_x, size_y)
    unpack_rows(fields, WIDTHS, segments(WIDTHS, size_x, beyond=False)[0], y_even, y_odd, size_y)
    unpack_rows(fields, WIDTHS, segments(WIDTHS, size_x, beside=False)[0], corner_even, corner_odd, size_y)

    wide = size_y + 2 * RIM
    lane = lax.broadcasted_iota(jnp.int32, (1, wide, size_z), 2)
    is_first = lane == 0
    is_last = lane == size_z - 1

    top = size_x + 1
    for side, x in ((0, 0), (1, top)):
        edge_x[side] = harmonic(permit[pl.ds(x, 4)], permit[pl.ds(x + 1, 4)])
        weigh(permit, edge_x.at[side], edge_y.at[side], edge_z.at[side], edge_inverse.at[side], x + 1, 0, 3)
    inner = (inner_x, inner_y, inner_z, inner_inverse)
    low_edge, high_edge = (
        tuple(ref.at[side] for ref in (edge_x, edge_y, edge_z, edge_inverse)) for side in (0, 1)
    )

    def relax(x, n, field, at, weights, base):
        face_x, face_y, face_z, inverse = weights
        a = field[pl.ds(at, n)]
        k = x - base
        span = pl.ds(k, n)
        fy, fz = face_y[span], face_z[span]
        total = source[pl.ds(x, n)] + face_x[pl.ds(k + 1, n)] * field[pl.ds(at + 1, n)]
        total = total + face_x[span] * field[pl.ds(at - 1, n)]
        total = total + fy * shift(a, -1, 1) + shift(fy * a, 1, 1)
        total = total + fz * shift(a, -1, 2) + shift(fz * a, 1, 2)
        return total * inverse[span]

    def sweep(out, field, by, skip):
        def step(weights, base):
            def put(x, n):
                out[pl.ds(x - skip, n)] = relax(x, n, field, x + by, weights, base)

            return put

        step(low_edge, 0)(skip, 3 - skip)
        planes_loop(3, top, 7, step(inner, 3))
        step(high_edge, top)(top, 3 - skip)

    sweep(first, start, 1, 0)
    sweep(second, first, 0, 1)

    def finish(x, n):
        span = pl.ds(x, n)
        v, a = poten[pl.ds(x + 1, n)], second[pl.ds(x + 1, n)]
        product = (poten[pl.ds(x, n)] - v) * (second[pl.ds(x, n)] - a)
        product = product + (poten[pl.ds(x + 2, n)] - v) * (second[pl.ds(x + 2, n)] - a)
        both = (shift(v, -1, 1) - v) * (shift(a, -1, 1) - a)
        product = product + both + shift(both, 1, 1)
        both = (jnp.where(is_last, 0.0, shift(v, -1, 2)) - v) * (jnp.where(is_last, 0.0, shift(a, -1, 2)) - a)
        product = product + both + jnp.where(is_first, v * a, shift(both, 1, 2))
        d = density[span]
        gain = jnp.where(labels[span] == 1, -1.5 * (eps_solid - eps_void) * d * d, 0.0)
        raw_out[span] = gain * product[:, :size_y]

    planes_loop(0, size_x, 8, finish)


def pack_raw_x(raw, out, low):
    out[...] = raw[pl.ds(jnp.where(low, 0, raw.shape[0] - FILTER_SWEEPS), FILTER_SWEEPS)]


def pack_raw_x_odd(raw, out):
    pack_raw_x(raw, out, jnp.logical_not(odd_place("gx")))


def pack_raw_x_even(raw, mine, other, out, energy_out):
    energy_out[...] = mine[...] + other[...]
    pack_raw_x(raw, out, odd_place("gx"))


def pack_raw_y(x_odd, x_even, raw, mine, other, even_out, odd_out, energy_out):
    size_x, size_y, _ = raw.shape
    width = FILTER_SWEEPS
    found, total = segments((width,), size_x)
    x_swap, y_swap = odd_place("gx"), odd_place("gy")
    energy = mine[...] + other[...]
    energy_out[...] = energy
    even_out[total:total + 8] = energy
    for _, x, rows, at in found:
        faces = []
        for rim in (slice(0, rows), slice(size_y - rows, size_y)):
            if x < 0:
                face = jnp.where(x_swap, x_even[width + x, rim], x_odd[width + x, rim])
            elif x >= size_x:
                face = jnp.where(x_swap, x_odd[x - size_x, rim], x_even[x - size_x, rim])
            else:
                face = raw[x, rim]
            faces.append(face)
        low, high = faces
        even_out[at:at + rows] = jnp.where(y_swap, low, high)
        odd_out[at:at + rows] = jnp.where(y_swap, high, low)


def relaxation(raw, size_x, size_y, size_z):
    width = FILTER_SWEEPS
    wide = size_y + 2 * RIM
    extent_x = lax.axis_size("gx") * size_x
    extent_y = lax.axis_size("gy") * size_y
    base_x = lax.axis_index("gx") * size_x - width
    lane = lax.broadcasted_iota(jnp.int32, (1, wide, size_z), 2)
    row = lax.broadcasted_iota(jnp.int32, (1, wide, size_z), 1)
    place = lax.axis_index("gy") * size_y + jnp.where(row < size_y + RIM, row, row - wide)
    is_first, is_last = lane == 0, lane == size_z - 1

    def edges(at, extent):
        return jnp.where(at > 0, 1.0, 0.0) + jnp.where(at < extent - 1, 1.0, 0.0)

    count = edges(place, extent_y) + edges(lane, size_z)
    inside = (place >= 0) & (place < extent_y)
    scale_two = jnp.where(inside, 1.0 / (1.0 + radius_sq * (count + 2.0)), 0.0)
    scale_one = jnp.where(inside, 1.0 / (1.0 + radius_sq * (count + 1.0)), 0.0)

    def relax(src, x, n):
        f = src[pl.ds(x, n)]
        near = src[pl.ds(x - 1, n)] + src[pl.ds(x + 1, n)] + shift(f, 1, 1) + shift(f, -1, 1)
        near = near + jnp.where(is_first, 0.0, shift(f, 1, 2)) + jnp.where(is_last, 0.0, shift(f, -1, 2))
        total = raw[pl.ds(x, n)] + radius_sq * near
        scaled = []
        for k in range(n):
            at = base_x + x + k
            outside = (at < 0) | (at >= extent_x)
            border = (at == 0) | (at == extent_x - 1)
            scale = jnp.where(outside, 0.0, jnp.where(border, scale_one, scale_two))
            scaled.append(total[k:k + 1] * scale)
        return jnp.concatenate(scaled, axis=0)

    return relax


def filter_part(x_odd, x_even, y_odd, y_even, raw_in, labels, out, raw, odd, even):
    size_x, size_y, size_z = raw_in.shape
    width = FILTER_SWEEPS
    tile = pl.ds(0, size_y)

    def fill(x, n):
        raw[pl.ds(x + width, n), tile] = raw_in[pl.ds(x, n)]

    planes_loop(0, size_x, 4, fill)
    unpack_planes(raw, width, x_even[...], x_odd[...], size_x, size_y)
    unpack_rows((raw,), (width,), segments((width,), size_x)[0], y_even, y_odd, size_y)
    relax = relaxation(raw, size_x, size_y, size_z)
    src = raw
    for sweep in range(FILTER_SWEEPS - 1):
        dst = (odd, even)[sweep % 2]

        def step(x, n, src=src, dst=dst):
            dst[pl.ds(x, n)] = relax(src, x, n)

        planes_loop(sweep + 1, size_x + 2 * width - sweep - 1, 11, step)
        src = dst

    def last(x, n):
        f = relax(src, x + width, n)[:, :size_y]
        out[pl.ds(x, n)] = jnp.where(labels[pl.ds(x, n)] == 1, f, 0.0)

    planes_loop(0, size_x, 8, last)


def rescale(filtered, mine, other, out, mean_out):
    size_x, size_y, size_z = filtered.shape
    voxels = lax.axis_size("gx") * size_x * lax.axis_size("gy") * size_y * size_z
    mean = 0.5 * jnp.sum(mine[...] + other[...]) / voxels + epsilon_mean
    mean_out[0, 0] = mean
    out[...] = filtered[...] * (1.0 / jnp.full((1, 1, size_z), mean, jnp.float32))


def swap_even(value, axis):
    return lax.ppermute(value, axis, [(i, i ^ 1) for i in range(lax.axis_size(axis))])


def swap_odd(value, axis):
    count = lax.axis_size(axis)
    up = [(i, i + 1) for i in range(1, count - 1, 2)]
    return lax.ppermute(value, axis, up + [(b, a) for a, b in up])


def partner(value, axis, bit):
    return lax.ppermute(value, axis, [(i, i ^ bit) for i in range(lax.axis_size(axis))])


def doubling(energy, stages):
    other = partner(energy, *stages[0])
    for stage in stages[1:]:
        energy = energy + other
        other = partner(energy, *stage)
    return energy, other


def shards(density, potential, adjoint_start, adjoint_source, labels):
    size_x, size_y, size_z = potential.shape
    _, planes = plane_starts(WIDTHS)
    _, rows = segments(WIDTHS, size_x, beyond=False)
    _, corners = segments(WIDTHS, size_x, beside=False)
    own = [
        pltpu.with_memory_space_constraint(array, pltpu.HBM)
        for array in (density, labels, adjoint_start, adjoint_source, potential)
    ]
    x_bits = [("gx", 1 << k) for k in range(1, (lax.axis_size("gx") - 1).bit_length())]
    y_bits = [("gy", 1 << k) for k in range(1, (lax.axis_size("gy") - 1).bit_length())]

    shape = (size_x, size_y, size_z)
    odd, even, tile_even, tile_odd, *own = pl.pallas_call(
        pack_own,
        out_shape=(f32(planes, size_y, size_z),) * 2 + (f32(rows, size_z),) * 2
        + (f32(*shape), jax.ShapeDtypeStruct(shape, jnp.int32)) + (f32(*shape),) * 3,
        in_specs=[pl.BlockSpec(memory_space=pltpu.HBM)] * 5,
        scratch_shapes=[pltpu.SemaphoreType.DMA((5,))],
        compiler_params=pltpu.CompilerParams(vmem_limit_bytes=VMEM_LIMIT),
    )(*own)
    x_even = swap_even(even, "gx")
    x_odd = swap_odd(odd, "gx")
    y_even = swap_even(tile_even, "gy")
    y_odd = swap_odd(tile_odd, "gy")
    even, odd = call(functools.partial(pack_corners, size_x), (f32(corners, size_z),) * 2)(x_odd, x_even)
    corner_even = swap_even(even, "gy")
    corner_odd = swap_odd(odd, "gy")

    wide = size_y + 2 * RIM

    def room(extra):
        return pltpu.VMEM((size_x + extra, wide, size_z), jnp.float32)

    energy = call(energy_part, f32(8, size_z), [room(2)])(x_odd, x_even, y_odd, y_even, own[0], own[1], own[4])
    mine, other = doubling(energy, y_bits[1:])
    face = f32(FILTER_SWEEPS, size_y, size_z)
    inner = call(
        inner_weights,
        (f32(size_x - 1, wide, size_z),) + (f32(size_x - 2, wide, size_z),) * 3,
        [room(0)],
    )(y_odd, y_even, own[0], own[1])

    def edges(planes):
        return pltpu.VMEM((2, planes, wide, size_z), jnp.float32)

    raw = call(
        adjoint_part,
        f32(*shape),
        [room(6), room(6), room(4), room(2), edges(4), edges(3), edges(3), edges(3), room(4), room(2)],
        cost=10000000,
    )(x_odd, x_even, y_odd, y_even, corner_odd, corner_even, *own, *inner)

    x_odd = swap_odd(call(pack_raw_x_odd, face)(raw), "gx")
    even, energy = call(pack_raw_x_even, (face, f32(8, size_z)))(raw, mine, other)
    x_even = swap_even(even, "gx")
    mine, other = doubling(energy, x_bits)
    _, rows = segments((FILTER_SWEEPS,), size_x)
    even, odd, energy = call(pack_raw_y, (f32(rows + 8, size_z), f32(rows, size_z), f32(8, size_z)))(
        x_odd, x_even, raw, mine, other)
    y_even = swap_even(even, "gy")
    y_odd = swap_odd(odd, "gy")
    energy = energy + y_even[rows:rows + 8]
    mine, other = doubling(energy, y_bits[:1] + [("gx", 1)])
    filtered = call(
        filter_part,
        f32(*shape),
        [room(2 * FILTER_SWEEPS)] * 3,
        cost=10000000,
    )(x_odd, x_even, y_odd, y_even, raw, own[1])
    sensitivity, mean_energy = pl.pallas_call(
        rescale,
        out_shape=(f32(*shape), f32(1, 1)),
        out_specs=(pl.BlockSpec(memory_space=pltpu.VMEM), pl.BlockSpec(memory_space=pltpu.SMEM)),
        compiler_params=pltpu.CompilerParams(vmem_limit_bytes=VMEM_LIMIT),
    )(filtered, mine, other)
    return (sensitivity, mean_energy[0, 0])


def solution(mesh):
    spec = P("gx", "gy", None)
    return jax.shard_map(
        shards, mesh=mesh, in_specs=(spec,) * 5, out_specs=(spec, P()), check_vma=False
    )
```

```python
import functools

import jax
import jax.numpy as jnp
from jax import lax
from jax.experimental import pallas as pl
from jax.experimental.pallas import tpu as pltpu
from jax.sharding import PartitionSpec as P

ADJ_SWEEPS = 2
FILTER_SWEEPS = 4

eps_void = 1.0
eps_solid = 12.0
eps_back = 4.0
eps_metal = 40.0
screen = 0.5
radius_sq = 2.0
epsilon_mean = 1e-06

WIDTHS = (ADJ_SWEEPS + 1, ADJ_SWEEPS + 1, ADJ_SWEEPS, 1)
RIM = 4
VMEM_LIMIT = 24 * 1024 * 1024


def segments(widths, size_x, beside=True, beyond=True):
    found, at = [], 0
    for field, width in enumerate(widths):
        for x in range(-width, size_x + width):
            rows = width - max(0, -x, x - size_x + 1)
            if rows > 0 and (beside if 0 <= x < size_x else beyond):
                found.append((field, x, rows, at))
                at += rows
    return found, -(-at // 8) * 8


def plane_starts(widths):
    starts, at = [], 0
    for width in widths:
        starts.append(at)
        at += width
    return starts, at


def material(density, labels):
    design = eps_void + density * density * density * (eps_solid - eps_void)
    return jnp.where(labels == 1, design, jnp.where(labels == 2, eps_metal, eps_back))


def call(body, outs, scratch=(), in_specs=None, cost=10000):
    kwargs = {} if in_specs is None else {"in_specs": in_specs, "grid": (1,)}
    return pl.pallas_call(
        body,
        out_shape=outs,
        scratch_shapes=list(scratch),
        compiler_params=pltpu.CompilerParams(vmem_limit_bytes=VMEM_LIMIT),
        cost_estimate=pl.CostEstimate(flops=cost, bytes_accessed=cost, transcendentals=0),
        **kwargs,
    )


def f32(*shape):
    return jax.ShapeDtypeStruct(shape, jnp.float32)


def odd_place(axis):
    return lax.rem(lax.axis_index(axis), 2) == 1


def pack_own(*refs):
    inputs, (x_odd_out, x_even_out, y_even_out, y_odd_out), held, sem = refs[:5], refs[5:9], refs[9:14], refs[14]
    density, labels, adjoint, source, potential = held
    size_x, size_y, _ = density.shape
    starts, _ = plane_starts(WIDTHS)
    copies = [pltpu.make_async_copy(a, b, sem.at[k]) for k, (a, b) in enumerate(zip(inputs, held))]
    for copy in copies:
        copy.start()
    copies[0].wait()
    low_first, y_swap = odd_place("gx"), odd_place("gy")
    found, _ = segments(WIDTHS, size_x, beyond=False)
    for field, width in enumerate(WIDTHS):
        copies[field + 1].wait()
        for out, low in ((x_even_out, low_first), (x_odd_out, jnp.logical_not(low_first))):
            span = pl.ds(jnp.where(low, 0, size_x - width), width)
            if field == 0:
                face = material(density[span], labels[span])
            else:
                face = (adjoint, source, potential)[field - 1][span]
            out[pl.ds(starts[field], width)] = face
        for _, x, rows, at in (part for part in found if part[0] == field):
            faces = []
            for rim in (slice(0, rows), slice(size_y - rows, size_y)):
                if field == 0:
                    faces.append(material(density[x, rim], labels[x, rim]))
                else:
                    faces.append((adjoint, source, potential)[field - 1][x, rim])
            low, high = faces
            y_even_out[at:at + rows] = jnp.where(y_swap, low, high)
            y_odd_out[at:at + rows] = jnp.where(y_swap, high, low)


def pack_corners(size_x, x_odd, x_even, even_out, odd_out):
    size_y = x_odd.shape[1]
    starts, _ = plane_starts(WIDTHS)
    x_swap, y_swap = odd_place("gx"), odd_place("gy")
    for field, x, rows, at in segments(WIDTHS, size_x, beside=False)[0]:
        faces = []
        for rim in (slice(0, rows), slice(size_y - rows, size_y)):
            if x < 0:
                plane = starts[field] + WIDTHS[field] + x
                face = jnp.where(x_swap, x_even[plane, rim], x_odd[plane, rim])
            else:
                plane = starts[field] + x - size_x
                face = jnp.where(x_swap, x_odd[plane, rim], x_even[plane, rim])
            faces.append(face)
        low, high = faces
        even_out[at:at + rows] = jnp.where(y_swap, low, high)
        odd_out[at:at + rows] = jnp.where(y_swap, high, low)


def shift(value, by, axis):
    return pltpu.roll(value, by % value.shape[axis], axis)


def planes_loop(low, high, block, step):
    count = high - low
    block = max(k for k in range(1, block + 1) if count % k == 0)

    def body(k, carry):
        step(low + k * block, block)
        return carry

    lax.fori_loop(0, count // block, body, 0)


def unpack_rows(fields, widths, found, even, odd, size_y):
    wide = size_y + 2 * RIM
    swap = odd_place("gy")
    for field, x, rows, at in found:
        if fields[field] is None:
            continue
        a, b = even[at:at + rows], odd[at:at + rows]
        fields[field][x + widths[field], wide - rows:wide] = jnp.where(swap, a, b)
        fields[field][x + widths[field], size_y:size_y + rows] = jnp.where(swap, b, a)


def unpack_planes(field, width, even, odd, size_x, size_y):
    swap = odd_place("gx")
    tile = pl.ds(0, size_y)
    field[pl.ds(0, width), tile] = jnp.where(swap, even, odd)
    field[pl.ds(width + size_x, width), tile] = jnp.where(swap, odd, even)


def energy_part(x_odd, x_even, y_even, y_odd, density, labels, potential, energy_out, poten):
    size_x, size_y, size_z = density.shape
    starts, planes = plane_starts(WIDTHS)
    planes_loop(0, size_x, 4, lambda x, n: poten.__setitem__((pl.ds(x + 1, n), pl.ds(0, size_y)), potential[pl.ds(x, n)]))
    span = pl.ds(starts[3], 1)
    unpack_planes(poten, 1, x_even[span], x_odd[span], size_x, size_y)
    found, _ = segments(WIDTHS, size_x, beyond=False)
    unpack_rows((None, None, None, poten), WIDTHS, found, y_even, y_odd, size_y)
    wide = size_y + 2 * RIM
    lane = lax.broadcasted_iota(jnp.int32, (1, wide, size_z), 2)
    is_first = lane == 0
    is_last = lane == size_z - 1
    energy_out[...] = jnp.zeros_like(energy_out)

    def step(x, n):
        span = pl.ds(x, n)
        v = poten[pl.ds(x + 1, n)]
        low, high = poten[pl.ds(x, n)] - v, poten[pl.ds(x + 2, n)] - v
        squares = low * low + high * high
        dv = shift(v, -1, 1) - v
        square = dv * dv
        squares = squares + square + shift(square, 1, 1)
        dv = jnp.where(is_last, 0.0, shift(v, -1, 2)) - v
        square = dv * dv
        squares = squares + square + jnp.where(is_first, v * v, shift(square, 1, 2))
        energy = material(density[span], labels[span]) * squares[:, :size_y]
        energy_out[...] += jnp.sum(energy.reshape(-1, 8, size_z), axis=0)

    planes_loop(0, size_x, 4, step)


def adjoint_part(x_odd, x_even, y_even, y_odd, corner_odd, corner_even, density, labels, adjoint_start, adjoint_source, potential,
                 raw_out,
                 permit, start, source, poten, face_x, face_y, face_z, inverse, first, second):
    size_x, size_y, size_z = density.shape
    starts, _ = plane_starts(WIDTHS)
    fields = (permit, start, source, poten)
    tile = pl.ds(0, size_y)

    def fill(x, n):
        span = pl.ds(x, n)
        permit[pl.ds(x + WIDTHS[0], n), tile] = material(density[span], labels[span])
        start[pl.ds(x + WIDTHS[1], n), tile] = adjoint_start[span]
        source[pl.ds(x + WIDTHS[2], n), tile] = adjoint_source[span]
        poten[pl.ds(x + WIDTHS[3], n), tile] = potential[span]

    planes_loop(0, size_x, 4, fill)
    for field, width in enumerate(WIDTHS):
        span = pl.ds(starts[field], width)
        unpack_planes(fields[field], width, x_even[span], x_odd[span], size_x, size_y)
    unpack_rows(fields, WIDTHS, segments(WIDTHS, size_x, beyond=False)[0], y_even, y_odd, size_y)
    unpack_rows(fields, WIDTHS, segments(WIDTHS, size_x, beside=False)[0], corner_even, corner_odd, size_y)

    wide = size_y + 2 * RIM
    lane = lax.broadcasted_iota(jnp.int32, (1, wide, size_z), 2)
    is_first = lane == 0
    is_last = lane == size_z - 1

    def inverted(d):
        first_guess = pl.reciprocal(d, approx=True)
        return first_guess * (2.0 - d * first_guess)

    def harmonic(a, b):
        return 2.0 * a * b * inverted(jnp.maximum(a + b, 0.25))

    def faces_x(x, n):
        face_x[pl.ds(x, n)] = harmonic(permit[pl.ds(x, n)], permit[pl.ds(x + 1, n)])

    planes_loop(0, size_x + 5, 7, faces_x)

    def weigh(x, n):
        span = pl.ds(x, n)
        p = permit[pl.ds(x + 1, n)]
        fy = harmonic(p, shift(p, -1, 1))
        fz = jnp.where(is_last, 0.0, harmonic(p, shift(p, -1, 2)))
        face_y[span] = fy
        face_z[span] = fz
        total = screen + face_x[span] + face_x[pl.ds(x + 1, n)] + fy + shift(fy, 1, 1) + fz + shift(fz, 1, 2)
        inverse[span] = jnp.where(p > 20.0, 0.0, inverted(total))

    planes_loop(0, size_x + 4, 10, weigh)

    def relax(x, n, a, a_low, a_high):
        span = pl.ds(x, n)
        fy, fz = face_y[span], face_z[span]
        total = source[span] + face_x[pl.ds(x + 1, n)] * a_high + face_x[span] * a_low
        total = total + fy * shift(a, -1, 1) + shift(fy * a, 1, 1)
        total = total + fz * shift(a, -1, 2) + shift(fz * a, 1, 2)
        return total * inverse[span]

    def sweep_one(x, n):
        first[pl.ds(x, n)] = relax(x, n, start[pl.ds(x + 1, n)], start[pl.ds(x, n)], start[pl.ds(x + 2, n)])

    planes_loop(0, size_x + 4, 10, sweep_one)

    def sweep_two(x, n):
        second[pl.ds(x, n)] = relax(x + 1, n, first[pl.ds(x + 1, n)], first[pl.ds(x, n)], first[pl.ds(x + 2, n)])

    planes_loop(0, size_x + 2, 9, sweep_two)

    def finish(x, n):
        span = pl.ds(x, n)
        v, a = poten[pl.ds(x + 1, n)], second[pl.ds(x + 1, n)]
        product = (poten[pl.ds(x, n)] - v) * (second[pl.ds(x, n)] - a)
        product = product + (poten[pl.ds(x + 2, n)] - v) * (second[pl.ds(x + 2, n)] - a)
        both = (shift(v, -1, 1) - v) * (shift(a, -1, 1) - a)
        product = product + both + shift(both, 1, 1)
        both = (jnp.where(is_last, 0.0, shift(v, -1, 2)) - v) * (jnp.where(is_last, 0.0, shift(a, -1, 2)) - a)
        product = product + both + jnp.where(is_first, v * a, shift(both, 1, 2))
        d = density[span]
        gain = jnp.where(labels[span] == 1, -1.5 * (eps_solid - eps_void) * d * d, 0.0)
        raw_out[span] = gain * product[:, :size_y]

    planes_loop(0, size_x, 8, finish)


def pack_raw_x(raw, out, low):
    out[...] = raw[pl.ds(jnp.where(low, 0, raw.shape[0] - FILTER_SWEEPS), FILTER_SWEEPS)]


def pack_raw_x_odd(raw, out):
    pack_raw_x(raw, out, jnp.logical_not(odd_place("gx")))


def pack_raw_x_even(raw, mine, other, out, energy_out):
    energy_out[...] = mine[...] + other[...]
    pack_raw_x(raw, out, odd_place("gx"))


def pack_raw_y(x_odd, x_even, raw, mine, other, even_out, odd_out, energy_out):
    size_x, size_y, _ = raw.shape
    width = FILTER_SWEEPS
    found, total = segments((width,), size_x)
    x_swap, y_swap = odd_place("gx"), odd_place("gy")
    energy = mine[...] + other[...]
    energy_out[...] = energy
    even_out[total:total + 8] = energy
    for _, x, rows, at in found:
        faces = []
        for rim in (slice(0, rows), slice(size_y - rows, size_y)):
            if x < 0:
                face = jnp.where(x_swap, x_even[width + x, rim], x_odd[width + x, rim])
            elif x >= size_x:
                face = jnp.where(x_swap, x_odd[x - size_x, rim], x_even[x - size_x, rim])
            else:
                face = raw[x, rim]
            faces.append(face)
        low, high = faces
        even_out[at:at + rows] = jnp.where(y_swap, low, high)
        odd_out[at:at + rows] = jnp.where(y_swap, high, low)


def relaxation(raw, size_x, size_y, size_z):
    width = FILTER_SWEEPS
    wide = size_y + 2 * RIM
    extent_x = lax.axis_size("gx") * size_x
    extent_y = lax.axis_size("gy") * size_y
    base_x = lax.axis_index("gx") * size_x - width
    lane = lax.broadcasted_iota(jnp.int32, (1, wide, size_z), 2)
    row = lax.broadcasted_iota(jnp.int32, (1, wide, size_z), 1)
    place = lax.axis_index("gy") * size_y + jnp.where(row < size_y + RIM, row, row - wide)
    is_first, is_last = lane == 0, lane == size_z - 1

    def edges(at, extent):
        return jnp.where(at > 0, 1.0, 0.0) + jnp.where(at < extent - 1, 1.0, 0.0)

    count = edges(place, extent_y) + edges(lane, size_z)
    inside = (place >= 0) & (place < extent_y)
    scale_two = jnp.where(inside, 1.0 / (1.0 + radius_sq * (count + 2.0)), 0.0)
    scale_one = jnp.where(inside, 1.0 / (1.0 + radius_sq * (count + 1.0)), 0.0)

    def relax(src, x, n):
        f = src[pl.ds(x, n)]
        near = src[pl.ds(x - 1, n)] + src[pl.ds(x + 1, n)] + shift(f, 1, 1) + shift(f, -1, 1)
        near = near + jnp.where(is_first, 0.0, shift(f, 1, 2)) + jnp.where(is_last, 0.0, shift(f, -1, 2))
        total = raw[pl.ds(x, n)] + radius_sq * near
        scaled = []
        for k in range(n):
            at = base_x + x + k
            outside = (at < 0) | (at >= extent_x)
            border = (at == 0) | (at == extent_x - 1)
            scale = jnp.where(outside, 0.0, jnp.where(border, scale_one, scale_two))
            scaled.append(total[k:k + 1] * scale)
        return jnp.concatenate(scaled, axis=0)

    return relax


def filter_part(x_odd, x_even, y_odd, y_even, raw_in, labels, out, raw, odd, even):
    size_x, size_y, size_z = raw_in.shape
    width = FILTER_SWEEPS
    tile = pl.ds(0, size_y)

    def fill(x, n):
        raw[pl.ds(x + width, n), tile] = raw_in[pl.ds(x, n)]

    planes_loop(0, size_x, 4, fill)
    unpack_planes(raw, width, x_even[...], x_odd[...], size_x, size_y)
    unpack_rows((raw,), (width,), segments((width,), size_x)[0], y_even, y_odd, size_y)
    relax = relaxation(raw, size_x, size_y, size_z)
    src = raw
    for sweep in range(FILTER_SWEEPS - 1):
        dst = (odd, even)[sweep % 2]

        def step(x, n, src=src, dst=dst):
            dst[pl.ds(x, n)] = relax(src, x, n)

        planes_loop(sweep + 1, size_x + 2 * width - sweep - 1, 11, step)
        src = dst

    def last(x, n):
        f = relax(src, x + width, n)[:, :size_y]
        out[pl.ds(x, n)] = jnp.where(labels[pl.ds(x, n)] == 1, f, 0.0)

    planes_loop(0, size_x, 8, last)


def rescale(filtered, mine, other, out, mean_out):
    size_x, size_y, size_z = filtered.shape
    voxels = lax.axis_size("gx") * size_x * lax.axis_size("gy") * size_y * size_z
    mean = 0.5 * jnp.sum(mine[...] + other[...]) / voxels + epsilon_mean
    mean_out[0, 0] = mean
    out[...] = filtered[...] * (1.0 / jnp.full((1, 1, size_z), mean, jnp.float32))


def swap_even(value, axis):
    return lax.ppermute(value, axis, [(i, i ^ 1) for i in range(lax.axis_size(axis))])


def swap_odd(value, axis):
    count = lax.axis_size(axis)
    up = [(i, i + 1) for i in range(1, count - 1, 2)]
    return lax.ppermute(value, axis, up + [(b, a) for a, b in up])


def partner(value, axis, bit):
    return lax.ppermute(value, axis, [(i, i ^ bit) for i in range(lax.axis_size(axis))])


def doubling(energy, stages):
    other = partner(energy, *stages[0])
    for stage in stages[1:]:
        energy = energy + other
        other = partner(energy, *stage)
    return energy, other


def shards(density, potential, adjoint_start, adjoint_source, labels):
    size_x, size_y, size_z = potential.shape
    _, planes = plane_starts(WIDTHS)
    _, rows = segments(WIDTHS, size_x, beyond=False)
    _, corners = segments(WIDTHS, size_x, beside=False)
    own = [
        pltpu.with_memory_space_constraint(array, pltpu.HBM)
        for array in (density, labels, adjoint_start, adjoint_source, potential)
    ]
    x_bits = [("gx", 1 << k) for k in range(1, (lax.axis_size("gx") - 1).bit_length())]
    y_bits = [("gy", 1 << k) for k in range(1, (lax.axis_size("gy") - 1).bit_length())]

    shape = (size_x, size_y, size_z)
    odd, even, tile_even, tile_odd, *own = pl.pallas_call(
        pack_own,
        out_shape=(f32(planes, size_y, size_z),) * 2 + (f32(rows, size_z),) * 2
        + (f32(*shape), jax.ShapeDtypeStruct(shape, jnp.int32)) + (f32(*shape),) * 3,
        in_specs=[pl.BlockSpec(memory_space=pltpu.HBM)] * 5,
        scratch_shapes=[pltpu.SemaphoreType.DMA((5,))],
        compiler_params=pltpu.CompilerParams(vmem_limit_bytes=VMEM_LIMIT),
    )(*own)
    x_even = swap_even(even, "gx")
    x_odd = swap_odd(odd, "gx")
    y_even = swap_even(tile_even, "gy")
    y_odd = swap_odd(tile_odd, "gy")
    even, odd = call(functools.partial(pack_corners, size_x), (f32(corners, size_z),) * 2)(x_odd, x_even)
    corner_even = swap_even(even, "gy")
    corner_odd = swap_odd(odd, "gy")

    wide = size_y + 2 * RIM

    def room(extra):
        return pltpu.VMEM((size_x + extra, wide, size_z), jnp.float32)

    energy = call(energy_part, f32(8, size_z), [room(2)])(x_odd, x_even, y_even, y_odd, own[0], own[1], own[4])
    mine, other = doubling(energy, y_bits[1:])
    face = f32(FILTER_SWEEPS, size_y, size_z)
    raw = call(
        adjoint_part,
        f32(*shape),
        [room(6), room(6), room(4), room(2), room(5), room(4), room(4), room(4), room(4), room(2)],
        cost=10000000,
    )(x_odd, x_even, y_even, y_odd, corner_odd, corner_even, *own)

    x_odd = swap_odd(call(pack_raw_x_odd, face)(raw), "gx")
    even, energy = call(pack_raw_x_even, (face, f32(8, size_z)))(raw, mine, other)
    x_even = swap_even(even, "gx")
    mine, other = doubling(energy, x_bits)
    _, rows = segments((FILTER_SWEEPS,), size_x)
    even, odd, energy = call(pack_raw_y, (f32(rows + 8, size_z), f32(rows, size_z), f32(8, size_z)))(
        x_odd, x_even, raw, mine, other)
    y_even = swap_even(even, "gy")
    y_odd = swap_odd(odd, "gy")
    energy = energy + y_even[rows:rows + 8]
    mine, other = doubling(energy, y_bits[:1] + [("gx", 1)])
    filtered = call(
        filter_part,
        f32(*shape),
        [room(2 * FILTER_SWEEPS)] * 3,
        cost=10000000,
    )(x_odd, x_even, y_odd, y_even, raw, own[1])
    sensitivity, mean_energy = pl.pallas_call(
        rescale,
        out_shape=(f32(*shape), f32(1, 1)),
        out_specs=(pl.BlockSpec(memory_space=pltpu.VMEM), pl.BlockSpec(memory_space=pltpu.SMEM)),
        compiler_params=pltpu.CompilerParams(vmem_limit_bytes=VMEM_LIMIT),
    )(filtered, mine, other)
    return (sensitivity, mean_energy[0, 0])


def solution(mesh):
    spec = P("gx", "gy", None)
    return jax.shard_map(
        shards, mesh=mesh, in_specs=(spec,) * 5, out_specs=(spec, P()), check_vma=False
    )
```

```python
import functools

import jax
import jax.numpy as jnp
from jax import lax
from jax.experimental import pallas as pl
from jax.experimental.pallas import tpu as pltpu
from jax.sharding import PartitionSpec as P

ADJ_SWEEPS = 2
FILTER_SWEEPS = 4

eps_void = 1.0
eps_solid = 12.0
eps_back = 4.0
eps_metal = 40.0
screen = 0.5
radius_sq = 2.0
epsilon_mean = 1e-06

WIDTHS = (ADJ_SWEEPS + 1, ADJ_SWEEPS + 1, ADJ_SWEEPS, 1)
RIM = 4
VMEM_LIMIT = 24 * 1024 * 1024


def segments(widths, size_x, beside=True, beyond=True):
    found, at = [], 0
    for field, width in enumerate(widths):
        for x in range(-width, size_x + width):
            rows = width - max(0, -x, x - size_x + 1)
            if rows > 0 and (beside if 0 <= x < size_x else beyond):
                found.append((field, x, rows, at))
                at += rows
    return found, -(-at // 8) * 8


def plane_starts(widths):
    starts, at = [], 0
    for width in widths:
        starts.append(at)
        at += width
    return starts, at


def material(density, labels):
    design = eps_void + density * density * density * (eps_solid - eps_void)
    return jnp.where(labels == 1, design, jnp.where(labels == 2, eps_metal, eps_back))


def call(body, outs, scratch=(), in_specs=None, cost=10000):
    kwargs = {} if in_specs is None else {"in_specs": in_specs, "grid": (1,)}
    return pl.pallas_call(
        body,
        out_shape=outs,
        scratch_shapes=list(scratch),
        compiler_params=pltpu.CompilerParams(vmem_limit_bytes=VMEM_LIMIT),
        cost_estimate=pl.CostEstimate(flops=cost, bytes_accessed=cost, transcendentals=0),
        **kwargs,
    )


def f32(*shape):
    return jax.ShapeDtypeStruct(shape, jnp.float32)


def odd_place(axis):
    return lax.rem(lax.axis_index(axis), 2) == 1


def pack_own(*refs):
    inputs, (x_odd_out, x_even_out, y_even_out, y_odd_out), held, sem = refs[:5], refs[5:9], refs[9:14], refs[14]
    density, labels, adjoint, source, potential = held
    size_x, size_y, _ = density.shape
    starts, _ = plane_starts(WIDTHS)
    copies = [pltpu.make_async_copy(a, b, sem.at[k]) for k, (a, b) in enumerate(zip(inputs, held))]
    for copy in copies:
        copy.start()
    copies[0].wait()
    low_first, y_swap = odd_place("gx"), odd_place("gy")
    found, _ = segments(WIDTHS, size_x, beyond=False)
    for field, width in enumerate(WIDTHS):
        copies[field + 1].wait()
        for out, low in ((x_even_out, low_first), (x_odd_out, jnp.logical_not(low_first))):
            span = pl.ds(jnp.where(low, 0, size_x - width), width)
            if field == 0:
                face = material(density[span], labels[span])
            else:
                face = (adjoint, source, potential)[field - 1][span]
            out[pl.ds(starts[field], width)] = face
        for _, x, rows, at in (part for part in found if part[0] == field):
            faces = []
            for rim in (slice(0, rows), slice(size_y - rows, size_y)):
                if field == 0:
                    faces.append(material(density[x, rim], labels[x, rim]))
                else:
                    faces.append((adjoint, source, potential)[field - 1][x, rim])
            low, high = faces
            y_even_out[at:at + rows] = jnp.where(y_swap, low, high)
            y_odd_out[at:at + rows] = jnp.where(y_swap, high, low)


def pack_corners(size_x, x_odd, x_even, even_out, odd_out):
    size_y = x_odd.shape[1]
    starts, _ = plane_starts(WIDTHS)
    x_swap, y_swap = odd_place("gx"), odd_place("gy")
    for field, x, rows, at in segments(WIDTHS, size_x, beside=False)[0]:
        faces = []
        for rim in (slice(0, rows), slice(size_y - rows, size_y)):
            if x < 0:
                plane = starts[field] + WIDTHS[field] + x
                face = jnp.where(x_swap, x_even[plane, rim], x_odd[plane, rim])
            else:
                plane = starts[field] + x - size_x
                face = jnp.where(x_swap, x_odd[plane, rim], x_even[plane, rim])
            faces.append(face)
        low, high = faces
        even_out[at:at + rows] = jnp.where(y_swap, low, high)
        odd_out[at:at + rows] = jnp.where(y_swap, high, low)


def shift(value, by, axis):
    return pltpu.roll(value, by % value.shape[axis], axis)


def planes_loop(low, high, block, step):
    count = high - low
    block = max(k for k in range(1, block + 1) if count % k == 0)

    def body(k, carry):
        step(low + k * block, block)
        return carry

    lax.fori_loop(0, count // block, body, 0)


def unpack_rows(fields, widths, found, even, odd, size_y):
    wide = size_y + 2 * RIM
    swap = odd_place("gy")
    for field, x, rows, at in found:
        if fields[field] is None:
            continue
        a, b = even[at:at + rows], odd[at:at + rows]
        fields[field][x + widths[field], wide - rows:wide] = jnp.where(swap, a, b)
        fields[field][x + widths[field], size_y:size_y + rows] = jnp.where(swap, b, a)


def unpack_planes(field, width, even, odd, size_x, size_y):
    swap = odd_place("gx")
    tile = pl.ds(0, size_y)
    field[pl.ds(0, width), tile] = jnp.where(swap, even, odd)
    field[pl.ds(width + size_x, width), tile] = jnp.where(swap, odd, even)


def energy_part(x_odd, x_even, y_even, y_odd, density, labels, potential, energy_out, poten):
    size_x, size_y, size_z = density.shape
    starts, planes = plane_starts(WIDTHS)
    planes_loop(0, size_x, 4, lambda x, n: poten.__setitem__((pl.ds(x + 1, n), pl.ds(0, size_y)), potential[pl.ds(x, n)]))
    span = pl.ds(starts[3], 1)
    unpack_planes(poten, 1, x_even[span], x_odd[span], size_x, size_y)
    found, _ = segments(WIDTHS, size_x, beyond=False)
    unpack_rows((None, None, None, poten), WIDTHS, found, y_even, y_odd, size_y)
    wide = size_y + 2 * RIM
    lane = lax.broadcasted_iota(jnp.int32, (1, wide, size_z), 2)
    is_first = lane == 0
    is_last = lane == size_z - 1
    energy_out[...] = jnp.zeros_like(energy_out)

    def step(x, n):
        span = pl.ds(x, n)
        v = poten[pl.ds(x + 1, n)]
        low, high = poten[pl.ds(x, n)] - v, poten[pl.ds(x + 2, n)] - v
        squares = low * low + high * high
        dv = shift(v, -1, 1) - v
        square = dv * dv
        squares = squares + square + shift(square, 1, 1)
        dv = jnp.where(is_last, 0.0, shift(v, -1, 2)) - v
        square = dv * dv
        squares = squares + square + jnp.where(is_first, v * v, shift(square, 1, 2))
        energy = material(density[span], labels[span]) * squares[:, :size_y]
        energy_out[...] += jnp.sum(energy.reshape(-1, 8, size_z), axis=0)

    planes_loop(0, size_x, 4, step)


def inverted(d):
    first_guess = pl.reciprocal(d, approx=True)
    return first_guess * (2.0 - d * first_guess)


def harmonic(a, b):
    return 2.0 * a * b * inverted(jnp.maximum(a + b, 0.25))


def weigh(permit, face_x, face_y, face_z, inverse, x, k, n):
    p = permit[pl.ds(x, n)]
    span = pl.ds(k, n)
    is_last = lax.broadcasted_iota(jnp.int32, (1,) + p.shape[1:], 2) == p.shape[2] - 1
    fy = harmonic(p, shift(p, -1, 1))
    fz = jnp.where(is_last, 0.0, harmonic(p, shift(p, -1, 2)))
    face_y[span] = fy
    face_z[span] = fz
    total = screen + face_x[span] + face_x[pl.ds(k + 1, n)] + fy + shift(fy, 1, 1) + fz + shift(fz, 1, 2)
    inverse[span] = jnp.where(p > 20.0, 0.0, inverted(total))


def inner_weights(y_even, y_odd, density, labels, face_x, face_y, face_z, inverse, permit):
    size_x, size_y, _ = density.shape

    def fill(x, n):
        permit[pl.ds(x, n), pl.ds(0, size_y)] = material(density[pl.ds(x, n)], labels[pl.ds(x, n)])

    planes_loop(0, size_x, 8, fill)
    found = [part for part in segments(WIDTHS, size_x, beyond=False)[0] if part[0] == 0]
    unpack_rows((permit,), (0,), found, y_even, y_odd, size_y)

    def faces(x, n):
        face_x[pl.ds(x, n)] = harmonic(permit[pl.ds(x, n)], permit[pl.ds(x + 1, n)])

    planes_loop(0, size_x - 1, 5, faces)
    planes_loop(0, size_x - 2, 7, lambda k, n: weigh(permit, face_x, face_y, face_z, inverse, k + 1, k, n))


def adjoint_part(x_odd, x_even, y_even, y_odd, corner_odd, corner_even, density, labels, adjoint_start, adjoint_source, potential,
                 inner_x, inner_y, inner_z, inner_inverse, raw_out,
                 permit, start, source, poten, edge_x, edge_y, edge_z, edge_inverse, first, second):
    size_x, size_y, size_z = density.shape
    starts, _ = plane_starts(WIDTHS)
    fields = (permit, start, source, poten)
    tile = pl.ds(0, size_y)

    def fill(x, n):
        span = pl.ds(x, n)
        permit[pl.ds(x + WIDTHS[0], n), tile] = material(density[span], labels[span])
        start[pl.ds(x + WIDTHS[1], n), tile] = adjoint_start[span]
        source[pl.ds(x + WIDTHS[2], n), tile] = adjoint_source[span]
        poten[pl.ds(x + WIDTHS[3], n), tile] = potential[span]

    planes_loop(0, size_x, 4, fill)
    for field, width in enumerate(WIDTHS):
        span = pl.ds(starts[field], width)
        unpack_planes(fields[field], width, x_even[span], x_odd[span], size_x, size_y)
    unpack_rows(fields, WIDTHS, segments(WIDTHS, size_x, beyond=False)[0], y_even, y_odd, size_y)
    unpack_rows(fields, WIDTHS, segments(WIDTHS, size_x, beside=False)[0], corner_even, corner_odd, size_y)

    wide = size_y + 2 * RIM
    lane = lax.broadcasted_iota(jnp.int32, (1, wide, size_z), 2)
    is_first = lane == 0
    is_last = lane == size_z - 1

    top = size_x + 1
    for side, x in ((0, 0), (1, top)):
        edge_x[side] = harmonic(permit[pl.ds(x, 4)], permit[pl.ds(x + 1, 4)])
        weigh(permit, edge_x.at[side], edge_y.at[side], edge_z.at[side], edge_inverse.at[side], x + 1, 0, 3)
    inner = (inner_x, inner_y, inner_z, inner_inverse)
    low_edge, high_edge = (
        tuple(ref.at[side] for ref in (edge_x, edge_y, edge_z, edge_inverse)) for side in (0, 1)
    )

    def relax(x, n, field, at, weights, base):
        face_x, face_y, face_z, inverse = weights
        a = field[pl.ds(at, n)]
        k = x - base
        span = pl.ds(k, n)
        fy, fz = face_y[span], face_z[span]
        total = source[pl.ds(x, n)] + face_x[pl.ds(k + 1, n)] * field[pl.ds(at + 1, n)]
        total = total + face_x[span] * field[pl.ds(at - 1, n)]
        total = total + fy * shift(a, -1, 1) + shift(fy * a, 1, 1)
        total = total + fz * shift(a, -1, 2) + shift(fz * a, 1, 2)
        return total * inverse[span]

    def sweep(out, field, by, skip):
        def step(weights, base):
            def put(x, n):
                out[pl.ds(x - skip, n)] = relax(x, n, field, x + by, weights, base)

            return put

        step(low_edge, 0)(skip, 3 - skip)
        planes_loop(3, top, 7, step(inner, 3))
        step(high_edge, top)(top, 3 - skip)

    sweep(first, start, 1, 0)
    sweep(second, first, 0, 1)

    def finish(x, n):
        span = pl.ds(x, n)
        v, a = poten[pl.ds(x + 1, n)], second[pl.ds(x + 1, n)]
        product = (poten[pl.ds(x, n)] - v) * (second[pl.ds(x, n)] - a)
        product = product + (poten[pl.ds(x + 2, n)] - v) * (second[pl.ds(x + 2, n)] - a)
        both = (shift(v, -1, 1) - v) * (shift(a, -1, 1) - a)
        product = product + both + shift(both, 1, 1)
        both = (jnp.where(is_last, 0.0, shift(v, -1, 2)) - v) * (jnp.where(is_last, 0.0, shift(a, -1, 2)) - a)
        product = product + both + jnp.where(is_first, v * a, shift(both, 1, 2))
        d = density[span]
        gain = jnp.where(labels[span] == 1, -1.5 * (eps_solid - eps_void) * d * d, 0.0)
        raw_out[span] = gain * product[:, :size_y]

    planes_loop(0, size_x, 8, finish)


def pack_raw_x(raw, out, low):
    out[...] = raw[pl.ds(jnp.where(low, 0, raw.shape[0] - FILTER_SWEEPS), FILTER_SWEEPS)]


def pack_raw_x_odd(raw, out):
    pack_raw_x(raw, out, jnp.logical_not(odd_place("gx")))


def pack_raw_x_even(raw, mine, other, out, energy_out):
    energy_out[...] = mine[...] + other[...]
    pack_raw_x(raw, out, odd_place("gx"))


def pack_raw_y(x_odd, x_even, raw, mine, other, even_out, odd_out, energy_out):
    size_x, size_y, _ = raw.shape
    width = FILTER_SWEEPS
    found, total = segments((width,), size_x)
    x_swap, y_swap = odd_place("gx"), odd_place("gy")
    energy = mine[...] + other[...]
    energy_out[...] = energy
    even_out[total:total + 8] = energy
    for _, x, rows, at in found:
        faces = []
        for rim in (slice(0, rows), slice(size_y - rows, size_y)):
            if x < 0:
                face = jnp.where(x_swap, x_even[width + x, rim], x_odd[width + x, rim])
            elif x >= size_x:
                face = jnp.where(x_swap, x_odd[x - size_x, rim], x_even[x - size_x, rim])
            else:
                face = raw[x, rim]
            faces.append(face)
        low, high = faces
        even_out[at:at + rows] = jnp.where(y_swap, low, high)
        odd_out[at:at + rows] = jnp.where(y_swap, high, low)


def relaxation(raw, size_x, size_y, size_z):
    width = FILTER_SWEEPS
    wide = size_y + 2 * RIM
    extent_x = lax.axis_size("gx") * size_x
    extent_y = lax.axis_size("gy") * size_y
    base_x = lax.axis_index("gx") * size_x - width
    lane = lax.broadcasted_iota(jnp.int32, (1, wide, size_z), 2)
    row = lax.broadcasted_iota(jnp.int32, (1, wide, size_z), 1)
    place = lax.axis_index("gy") * size_y + jnp.where(row < size_y + RIM, row, row - wide)
    is_first, is_last = lane == 0, lane == size_z - 1

    def edges(at, extent):
        return jnp.where(at > 0, 1.0, 0.0) + jnp.where(at < extent - 1, 1.0, 0.0)

    count = edges(place, extent_y) + edges(lane, size_z)
    inside = (place >= 0) & (place < extent_y)
    scale_two = jnp.where(inside, 1.0 / (1.0 + radius_sq * (count + 2.0)), 0.0)
    scale_one = jnp.where(inside, 1.0 / (1.0 + radius_sq * (count + 1.0)), 0.0)

    def relax(src, x, n):
        f = src[pl.ds(x, n)]
        near = src[pl.ds(x - 1, n)] + src[pl.ds(x + 1, n)] + shift(f, 1, 1) + shift(f, -1, 1)
        near = near + jnp.where(is_first, 0.0, shift(f, 1, 2)) + jnp.where(is_last, 0.0, shift(f, -1, 2))
        total = raw[pl.ds(x, n)] + radius_sq * near
        scaled = []
        for k in range(n):
            at = base_x + x + k
            outside = (at < 0) | (at >= extent_x)
            border = (at == 0) | (at == extent_x - 1)
            scale = jnp.where(outside, 0.0, jnp.where(border, scale_one, scale_two))
            scaled.append(total[k:k + 1] * scale)
        return jnp.concatenate(scaled, axis=0)

    return relax


def filter_part(x_odd, x_even, y_odd, y_even, raw_in, labels, out, raw, odd, even):
    size_x, size_y, size_z = raw_in.shape
    width = FILTER_SWEEPS
    tile = pl.ds(0, size_y)

    def fill(x, n):
        raw[pl.ds(x + width, n), tile] = raw_in[pl.ds(x, n)]

    planes_loop(0, size_x, 4, fill)
    unpack_planes(raw, width, x_even[...], x_odd[...], size_x, size_y)
    unpack_rows((raw,), (width,), segments((width,), size_x)[0], y_even, y_odd, size_y)
    relax = relaxation(raw, size_x, size_y, size_z)
    src = raw
    for sweep in range(FILTER_SWEEPS - 1):
        dst = (odd, even)[sweep % 2]

        def step(x, n, src=src, dst=dst):
            dst[pl.ds(x, n)] = relax(src, x, n)

        planes_loop(sweep + 1, size_x + 2 * width - sweep - 1, 11, step)
        src = dst

    def last(x, n):
        f = relax(src, x + width, n)[:, :size_y]
        out[pl.ds(x, n)] = jnp.where(labels[pl.ds(x, n)] == 1, f, 0.0)

    planes_loop(0, size_x, 8, last)


def rescale(filtered, mine, other, out, mean_out):
    size_x, size_y, size_z = filtered.shape
    voxels = lax.axis_size("gx") * size_x * lax.axis_size("gy") * size_y * size_z
    mean = 0.5 * jnp.sum(mine[...] + other[...]) / voxels + epsilon_mean
    mean_out[0, 0] = mean
    out[...] = filtered[...] * (1.0 / jnp.full((1, 1, size_z), mean, jnp.float32))


def swap_even(value, axis):
    return lax.ppermute(value, axis, [(i, i ^ 1) for i in range(lax.axis_size(axis))])


def swap_odd(value, axis):
    count = lax.axis_size(axis)
    up = [(i, i + 1) for i in range(1, count - 1, 2)]
    return lax.ppermute(value, axis, up + [(b, a) for a, b in up])


def partner(value, axis, bit):
    return lax.ppermute(value, axis, [(i, i ^ bit) for i in range(lax.axis_size(axis))])


def doubling(energy, stages):
    other = partner(energy, *stages[0])
    for stage in stages[1:]:
        energy = energy + other
        other = partner(energy, *stage)
    return energy, other


def shards(density, potential, adjoint_start, adjoint_source, labels):
    size_x, size_y, size_z = potential.shape
    _, planes = plane_starts(WIDTHS)
    _, rows = segments(WIDTHS, size_x, beyond=False)
    _, corners = segments(WIDTHS, size_x, beside=False)
    own = [
        pltpu.with_memory_space_constraint(array, pltpu.HBM)
        for array in (density, labels, adjoint_start, adjoint_source, potential)
    ]
    x_bits = [("gx", 1 << k) for k in range(1, (lax.axis_size("gx") - 1).bit_length())]
    y_bits = [("gy", 1 << k) for k in range(1, (lax.axis_size("gy") - 1).bit_length())]

    shape = (size_x, size_y, size_z)
    odd, even, tile_even, tile_odd, *own = pl.pallas_call(
        pack_own,
        out_shape=(f32(planes, size_y, size_z),) * 2 + (f32(rows, size_z),) * 2
        + (f32(*shape), jax.ShapeDtypeStruct(shape, jnp.int32)) + (f32(*shape),) * 3,
        in_specs=[pl.BlockSpec(memory_space=pltpu.HBM)] * 5,
        scratch_shapes=[pltpu.SemaphoreType.DMA((5,))],
        compiler_params=pltpu.CompilerParams(vmem_limit_bytes=VMEM_LIMIT),
    )(*own)
    x_even = swap_even(even, "gx")
    x_odd = swap_odd(odd, "gx")
    y_even = swap_even(tile_even, "gy")
    y_odd = swap_odd(tile_odd, "gy")
    even, odd = call(functools.partial(pack_corners, size_x), (f32(corners, size_z),) * 2)(x_odd, x_even)
    corner_even = swap_even(even, "gy")
    corner_odd = swap_odd(odd, "gy")

    wide = size_y + 2 * RIM

    def room(extra):
        return pltpu.VMEM((size_x + extra, wide, size_z), jnp.float32)

    energy = call(energy_part, f32(8, size_z), [room(2)])(x_odd, x_even, y_even, y_odd, own[0], own[1], own[4])
    mine, other = doubling(energy, y_bits[1:])
    face = f32(FILTER_SWEEPS, size_y, size_z)
    inner = call(
        inner_weights,
        (f32(size_x - 1, wide, size_z),) + (f32(size_x - 2, wide, size_z),) * 3,
        [room(0)],
    )(y_even, y_odd, own[0], own[1])

    def edges(planes):
        return pltpu.VMEM((2, planes, wide, size_z), jnp.float32)

    raw = call(
        adjoint_part,
        f32(*shape),
        [room(6), room(6), room(4), room(2), edges(4), edges(3), edges(3), edges(3), room(4), room(2)],
        cost=10000000,
    )(x_odd, x_even, y_even, y_odd, corner_odd, corner_even, *own, *inner)

    x_odd = swap_odd(call(pack_raw_x_odd, face)(raw), "gx")
    even, energy = call(pack_raw_x_even, (face, f32(8, size_z)))(raw, mine, other)
    x_even = swap_even(even, "gx")
    mine, other = doubling(energy, x_bits)
    _, rows = segments((FILTER_SWEEPS,), size_x)
    even, odd, energy = call(pack_raw_y, (f32(rows + 8, size_z), f32(rows, size_z), f32(8, size_z)))(
        x_odd, x_even, raw, mine, other)
    y_even = swap_even(even, "gy")
    y_odd = swap_odd(odd, "gy")
    energy = energy + y_even[rows:rows + 8]
    mine, other = doubling(energy, y_bits[:1] + [("gx", 1)])
    filtered = call(
        filter_part,
        f32(*shape),
        [room(2 * FILTER_SWEEPS)] * 3,
        cost=10000000,
    )(x_odd, x_even, y_odd, y_even, raw, own[1])
    sensitivity, mean_energy = pl.pallas_call(
        rescale,
        out_shape=(f32(*shape), f32(1, 1)),
        out_specs=(pl.BlockSpec(memory_space=pltpu.VMEM), pl.BlockSpec(memory_space=pltpu.SMEM)),
        compiler_params=pltpu.CompilerParams(vmem_limit_bytes=VMEM_LIMIT),
    )(filtered, mine, other)
    return (sensitivity, mean_energy[0, 0])


def solution(mesh):
    spec = P("gx", "gy", None)
    return jax.shard_map(
        shards, mesh=mesh, in_specs=(spec,) * 5, out_specs=(spec, P()), check_vma=False
    )
```

```python
import functools

import jax
import jax.numpy as jnp
from jax import lax
from jax.experimental import pallas as pl
from jax.experimental.pallas import tpu as pltpu
from jax.sharding import PartitionSpec as P

ADJ_SWEEPS = 2
FILTER_SWEEPS = 4

eps_void = 1.0
eps_solid = 12.0
eps_back = 4.0
eps_metal = 40.0
screen = 0.5
radius_sq = 2.0
epsilon_mean = 1e-06

WIDTHS = (ADJ_SWEEPS + 1, ADJ_SWEEPS + 1, ADJ_SWEEPS, 1)
RIM = 4
VMEM_LIMIT = 24 * 1024 * 1024


def segments(widths, size_x, beside=True, beyond=True):
    found, at = [], 0
    for field, width in enumerate(widths):
        for x in range(-width, size_x + width):
            rows = width - max(0, -x, x - size_x + 1)
            if rows > 0 and (beside if 0 <= x < size_x else beyond):
                found.append((field, x, rows, at))
                at += rows
    return found, -(-at // 8) * 8


def plane_starts(widths):
    starts, at = [], 0
    for width in widths:
        starts.append(at)
        at += width
    return starts, at


def material(density, labels):
    design = eps_void + density * density * density * (eps_solid - eps_void)
    return jnp.where(labels == 1, design, jnp.where(labels == 2, eps_metal, eps_back))


def call(body, outs, scratch=(), in_specs=None, cost=10000):
    kwargs = {} if in_specs is None else {"in_specs": in_specs, "grid": (1,)}
    return pl.pallas_call(
        body,
        out_shape=outs,
        scratch_shapes=list(scratch),
        compiler_params=pltpu.CompilerParams(vmem_limit_bytes=VMEM_LIMIT),
        cost_estimate=pl.CostEstimate(flops=cost, bytes_accessed=cost, transcendentals=0),
        **kwargs,
    )


def f32(*shape):
    return jax.ShapeDtypeStruct(shape, jnp.float32)


def odd_place(axis):
    return lax.rem(lax.axis_index(axis), 2) == 1


def pack_own(*refs):
    inputs, (x_odd_out, x_even_out, y_even_out, y_odd_out), held, sem = refs[:5], refs[5:9], refs[9:14], refs[14]
    density, labels, adjoint, source, potential = held
    size_x, size_y, _ = density.shape
    starts, _ = plane_starts(WIDTHS)
    copies = [pltpu.make_async_copy(a, b, sem.at[k]) for k, (a, b) in enumerate(zip(inputs, held))]
    for copy in copies:
        copy.start()
    copies[0].wait()
    low_first, y_swap = odd_place("gx"), odd_place("gy")
    found, _ = segments(WIDTHS, size_x, beyond=False)
    for field, width in enumerate(WIDTHS):
        copies[field + 1].wait()
        for out, low in ((x_even_out, low_first), (x_odd_out, jnp.logical_not(low_first))):
            span = pl.ds(jnp.where(low, 0, size_x - width), width)
            if field == 0:
                face = material(density[span], labels[span])
            else:
                face = (adjoint, source, potential)[field - 1][span]
            out[pl.ds(starts[field], width)] = face
        for _, x, rows, at in (part for part in found if part[0] == field):
            faces = []
            for rim in (slice(0, rows), slice(size_y - rows, size_y)):
                if field == 0:
                    faces.append(material(density[x, rim], labels[x, rim]))
                else:
                    faces.append((adjoint, source, potential)[field - 1][x, rim])
            low, high = faces
            y_even_out[at:at + rows] = jnp.where(y_swap, low, high)
            y_odd_out[at:at + rows] = jnp.where(y_swap, high, low)


def pack_corners(size_x, x_odd, x_even, even_out, odd_out):
    size_y = x_odd.shape[1]
    starts, _ = plane_starts(WIDTHS)
    x_swap, y_swap = odd_place("gx"), odd_place("gy")
    for field, x, rows, at in segments(WIDTHS, size_x, beside=False)[0]:
        faces = []
        for rim in (slice(0, rows), slice(size_y - rows, size_y)):
            if x < 0:
                plane = starts[field] + WIDTHS[field] + x
                face = jnp.where(x_swap, x_even[plane, rim], x_odd[plane, rim])
            else:
                plane = starts[field] + x - size_x
                face = jnp.where(x_swap, x_odd[plane, rim], x_even[plane, rim])
            faces.append(face)
        low, high = faces
        even_out[at:at + rows] = jnp.where(y_swap, low, high)
        odd_out[at:at + rows] = jnp.where(y_swap, high, low)


def shift(value, by, axis):
    return pltpu.roll(value, by % value.shape[axis], axis)


def planes_loop(low, high, block, step):
    count = high - low
    block = max(k for k in range(1, block + 1) if count % k == 0)

    def body(k, carry):
        step(low + k * block, block)
        return carry

    lax.fori_loop(0, count // block, body, 0)


def unpack_rows(fields, widths, found, even, odd, size_y):
    wide = size_y + 2 * RIM
    swap = odd_place("gy")
    for field, x, rows, at in found:
        if fields[field] is None:
            continue
        a, b = even[at:at + rows], odd[at:at + rows]
        fields[field][x + widths[field], wide - rows:wide] = jnp.where(swap, a, b)
        fields[field][x + widths[field], size_y:size_y + rows] = jnp.where(swap, b, a)


def unpack_planes(field, width, even, odd, size_x, size_y):
    swap = odd_place("gx")
    tile = pl.ds(0, size_y)
    field[pl.ds(0, width), tile] = jnp.where(swap, even, odd)
    field[pl.ds(width + size_x, width), tile] = jnp.where(swap, odd, even)


def energy_part(x_odd, x_even, y_odd, y_even, density, labels, potential, energy_out, poten):
    size_x, size_y, size_z = density.shape
    starts, planes = plane_starts(WIDTHS)
    planes_loop(0, size_x, 4, lambda x, n: poten.__setitem__((pl.ds(x + 1, n), pl.ds(0, size_y)), potential[pl.ds(x, n)]))
    span = pl.ds(starts[3], 1)
    unpack_planes(poten, 1, x_even[span], x_odd[span], size_x, size_y)
    found, _ = segments(WIDTHS, size_x, beyond=False)
    unpack_rows((None, None, None, poten), WIDTHS, found, y_even, y_odd, size_y)
    wide = size_y + 2 * RIM
    lane = lax.broadcasted_iota(jnp.int32, (1, wide, size_z), 2)
    is_first = lane == 0
    is_last = lane == size_z - 1
    energy_out[...] = jnp.zeros_like(energy_out)

    def step(x, n):
        span = pl.ds(x, n)
        v = poten[pl.ds(x + 1, n)]
        low, high = poten[pl.ds(x, n)] - v, poten[pl.ds(x + 2, n)] - v
        squares = low * low + high * high
        dv = shift(v, -1, 1) - v
        square = dv * dv
        squares = squares + square + shift(square, 1, 1)
        dv = jnp.where(is_last, 0.0, shift(v, -1, 2)) - v
        square = dv * dv
        squares = squares + square + jnp.where(is_first, v * v, shift(square, 1, 2))
        energy = material(density[span], labels[span]) * squares[:, :size_y]
        energy_out[...] += jnp.sum(energy.reshape(-1, 8, size_z), axis=0)

    planes_loop(0, size_x, 4, step)


def adjoint_part(x_odd, x_even, y_odd, y_even, corner_odd, corner_even, density, labels, adjoint_start, adjoint_source, potential,
                 raw_out,
                 permit, start, source, poten, face_x, face_y, face_z, inverse, first, second):
    size_x, size_y, size_z = density.shape
    starts, _ = plane_starts(WIDTHS)
    fields = (permit, start, source, poten)
    tile = pl.ds(0, size_y)

    def fill(x, n):
        span = pl.ds(x, n)
        permit[pl.ds(x + WIDTHS[0], n), tile] = material(density[span], labels[span])
        start[pl.ds(x + WIDTHS[1], n), tile] = adjoint_start[span]
        source[pl.ds(x + WIDTHS[2], n), tile] = adjoint_source[span]
        poten[pl.ds(x + WIDTHS[3], n), tile] = potential[span]

    planes_loop(0, size_x, 4, fill)
    for field, width in enumerate(WIDTHS):
        span = pl.ds(starts[field], width)
        unpack_planes(fields[field], width, x_even[span], x_odd[span], size_x, size_y)
    unpack_rows(fields, WIDTHS, segments(WIDTHS, size_x, beyond=False)[0], y_even, y_odd, size_y)
    unpack_rows(fields, WIDTHS, segments(WIDTHS, size_x, beside=False)[0], corner_even, corner_odd, size_y)

    wide = size_y + 2 * RIM
    lane = lax.broadcasted_iota(jnp.int32, (1, wide, size_z), 2)
    is_first = lane == 0
    is_last = lane == size_z - 1

    def inverted(d):
        first_guess = pl.reciprocal(d, approx=True)
        return first_guess * (2.0 - d * first_guess)

    def harmonic(a, b):
        return 2.0 * a * b * inverted(jnp.maximum(a + b, 0.25))

    def faces_x(x, n):
        face_x[pl.ds(x, n)] = harmonic(permit[pl.ds(x, n)], permit[pl.ds(x + 1, n)])

    planes_loop(0, size_x + 5, 7, faces_x)

    def weigh(x, n):
        span = pl.ds(x, n)
        p = permit[pl.ds(x + 1, n)]
        fy = harmonic(p, shift(p, -1, 1))
        fz = jnp.where(is_last, 0.0, harmonic(p, shift(p, -1, 2)))
        face_y[span] = fy
        face_z[span] = fz
        total = screen + face_x[span] + face_x[pl.ds(x + 1, n)] + fy + shift(fy, 1, 1) + fz + shift(fz, 1, 2)
        inverse[span] = jnp.where(p > 20.0, 0.0, inverted(total))

    planes_loop(0, size_x + 4, 10, weigh)

    def relax(x, n, a, a_low, a_high):
        span = pl.ds(x, n)
        fy, fz = face_y[span], face_z[span]
        total = source[span] + face_x[pl.ds(x + 1, n)] * a_high + face_x[span] * a_low
        total = total + fy * shift(a, -1, 1) + shift(fy * a, 1, 1)
        total = total + fz * shift(a, -1, 2) + shift(fz * a, 1, 2)
        return total * inverse[span]

    def sweep_one(x, n):
        first[pl.ds(x, n)] = relax(x, n, start[pl.ds(x + 1, n)], start[pl.ds(x, n)], start[pl.ds(x + 2, n)])

    planes_loop(0, size_x + 4, 10, sweep_one)

    def sweep_two(x, n):
        second[pl.ds(x, n)] = relax(x + 1, n, first[pl.ds(x + 1, n)], first[pl.ds(x, n)], first[pl.ds(x + 2, n)])

    planes_loop(0, size_x + 2, 9, sweep_two)

    def finish(x, n):
        span = pl.ds(x, n)
        v, a = poten[pl.ds(x + 1, n)], second[pl.ds(x + 1, n)]
        product = (poten[pl.ds(x, n)] - v) * (second[pl.ds(x, n)] - a)
        product = product + (poten[pl.ds(x + 2, n)] - v) * (second[pl.ds(x + 2, n)] - a)
        both = (shift(v, -1, 1) - v) * (shift(a, -1, 1) - a)
        product = product + both + shift(both, 1, 1)
        both = (jnp.where(is_last, 0.0, shift(v, -1, 2)) - v) * (jnp.where(is_last, 0.0, shift(a, -1, 2)) - a)
        product = product + both + jnp.where(is_first, v * a, shift(both, 1, 2))
        d = density[span]
        gain = jnp.where(labels[span] == 1, -1.5 * (eps_solid - eps_void) * d * d, 0.0)
        raw_out[span] = gain * product[:, :size_y]

    planes_loop(0, size_x, 8, finish)


def pack_raw_x(raw, out, low):
    out[...] = raw[pl.ds(jnp.where(low, 0, raw.shape[0] - FILTER_SWEEPS), FILTER_SWEEPS)]


def pack_raw_x_odd(raw, out):
    pack_raw_x(raw, out, jnp.logical_not(odd_place("gx")))


def pack_raw_x_even(raw, mine, other, out, energy_out):
    energy_out[...] = mine[...] + other[...]
    pack_raw_x(raw, out, odd_place("gx"))


def pack_raw_y(x_odd, x_even, raw, mine, other, even_out, odd_out, energy_out):
    size_x, size_y, _ = raw.shape
    width = FILTER_SWEEPS
    found, total = segments((width,), size_x)
    x_swap, y_swap = odd_place("gx"), odd_place("gy")
    energy = mine[...] + other[...]
    energy_out[...] = energy
    even_out[total:total + 8] = energy
    for _, x, rows, at in found:
        faces = []
        for rim in (slice(0, rows), slice(size_y - rows, size_y)):
            if x < 0:
                face = jnp.where(x_swap, x_even[width + x, rim], x_odd[width + x, rim])
            elif x >= size_x:
                face = jnp.where(x_swap, x_odd[x - size_x, rim], x_even[x - size_x, rim])
            else:
                face = raw[x, rim]
            faces.append(face)
        low, high = faces
        even_out[at:at + rows] = jnp.where(y_swap, low, high)
        odd_out[at:at + rows] = jnp.where(y_swap, high, low)


def relaxation(raw, scales, size_x, size_y, size_z):
    width = FILTER_SWEEPS
    wide = size_y + 2 * RIM
    extent_x = lax.axis_size("gx") * size_x
    extent_y = lax.axis_size("gy") * size_y
    base_x = lax.axis_index("gx") * size_x - width
    lane = lax.broadcasted_iota(jnp.int32, (1, wide, size_z), 2)
    row = lax.broadcasted_iota(jnp.int32, (1, wide, size_z), 1)
    place = lax.axis_index("gy") * size_y + jnp.where(row < size_y + RIM, row, row - wide)
    is_first, is_last = lane == 0, lane == size_z - 1

    def edges(at, extent):
        return jnp.where(at > 0, 1.0, 0.0) + jnp.where(at < extent - 1, 1.0, 0.0)

    count = edges(place, extent_y) + edges(lane, size_z)
    inside = (place >= 0) & (place < extent_y)
    scales[pl.ds(0, 1)] = jnp.zeros((1, wide, size_z), jnp.float32)
    scales[pl.ds(1, 1)] = jnp.where(inside, 1.0 / (1.0 + radius_sq * (count + 1.0)), 0.0)
    scales[pl.ds(2, 1)] = jnp.where(inside, 1.0 / (1.0 + radius_sq * (count + 2.0)), 0.0)

    def relax(src, x, n):
        f = src[pl.ds(x, n)]
        near = src[pl.ds(x - 1, n)] + src[pl.ds(x + 1, n)] + shift(f, 1, 1) + shift(f, -1, 1)
        near = near + jnp.where(is_first, 0.0, shift(f, 1, 2)) + jnp.where(is_last, 0.0, shift(f, -1, 2))
        total = raw[pl.ds(x, n)] + radius_sq * near
        scaled = []
        for k in range(n):
            at = base_x + x + k
            outside = (at < 0) | (at >= extent_x)
            border = (at == 0) | (at == extent_x - 1)
            which = jnp.where(outside, 0, jnp.where(border, 1, 2))
            scaled.append(total[k:k + 1] * scales[pl.ds(which, 1)])
        return jnp.concatenate(scaled, axis=0)

    return relax


def filter_part(x_odd, x_even, y_odd, y_even, raw_in, labels, out, raw, odd, even, scales):
    size_x, size_y, size_z = raw_in.shape
    width = FILTER_SWEEPS
    tile = pl.ds(0, size_y)

    def fill(x, n):
        raw[pl.ds(x + width, n), tile] = raw_in[pl.ds(x, n)]

    planes_loop(0, size_x, 4, fill)
    unpack_planes(raw, width, x_even[...], x_odd[...], size_x, size_y)
    unpack_rows((raw,), (width,), segments((width,), size_x)[0], y_even, y_odd, size_y)
    relax = relaxation(raw, scales, size_x, size_y, size_z)
    src = raw
    for sweep in range(FILTER_SWEEPS - 1):
        dst = (odd, even)[sweep % 2]

        def step(x, n, src=src, dst=dst):
            dst[pl.ds(x, n)] = relax(src, x, n)

        planes_loop(sweep + 1, size_x + 2 * width - sweep - 1, 11, step)
        src = dst

    def last(x, n):
        f = relax(src, x + width, n)[:, :size_y]
        out[pl.ds(x, n)] = jnp.where(labels[pl.ds(x, n)] == 1, f, 0.0)

    planes_loop(0, size_x, 8, last)


def rescale(filtered, mine, other, out, mean_out):
    size_x, size_y, size_z = filtered.shape
    voxels = lax.axis_size("gx") * size_x * lax.axis_size("gy") * size_y * size_z
    mean = 0.5 * jnp.sum(mine[...] + other[...]) / voxels + epsilon_mean
    mean_out[0, 0] = mean
    out[...] = filtered[...] * (1.0 / jnp.full((1, 1, size_z), mean, jnp.float32))


def swap_even(value, axis):
    return lax.ppermute(value, axis, [(i, i ^ 1) for i in range(lax.axis_size(axis))])


def swap_odd(value, axis):
    count = lax.axis_size(axis)
    up = [(i, i + 1) for i in range(1, count - 1, 2)]
    return lax.ppermute(value, axis, up + [(b, a) for a, b in up])


def partner(value, axis, bit):
    return lax.ppermute(value, axis, [(i, i ^ bit) for i in range(lax.axis_size(axis))])


def doubling(energy, stages):
    other = partner(energy, *stages[0])
    for stage in stages[1:]:
        energy = energy + other
        other = partner(energy, *stage)
    return energy, other


def shards(density, potential, adjoint_start, adjoint_source, labels):
    size_x, size_y, size_z = potential.shape
    _, planes = plane_starts(WIDTHS)
    _, rows = segments(WIDTHS, size_x, beyond=False)
    _, corners = segments(WIDTHS, size_x, beside=False)
    own = [
        pltpu.with_memory_space_constraint(array, pltpu.HBM)
        for array in (density, labels, adjoint_start, adjoint_source, potential)
    ]
    x_bits = [("gx", 1 << k) for k in range(1, (lax.axis_size("gx") - 1).bit_length())]
    y_bits = [("gy", 1 << k) for k in range(1, (lax.axis_size("gy") - 1).bit_length())]

    shape = (size_x, size_y, size_z)
    odd, even, tile_even, tile_odd, *own = pl.pallas_call(
        pack_own,
        out_shape=(f32(planes, size_y, size_z),) * 2 + (f32(rows, size_z),) * 2
        + (f32(*shape), jax.ShapeDtypeStruct(shape, jnp.int32)) + (f32(*shape),) * 3,
        in_specs=[pl.BlockSpec(memory_space=pltpu.HBM)] * 5,
        scratch_shapes=[pltpu.SemaphoreType.DMA((5,))],
        compiler_params=pltpu.CompilerParams(vmem_limit_bytes=VMEM_LIMIT),
    )(*own)
    x_even = swap_even(even, "gx")
    x_odd = swap_odd(odd, "gx")
    y_even = swap_even(tile_even, "gy")
    y_odd = swap_odd(tile_odd, "gy")
    even, odd = call(functools.partial(pack_corners, size_x), (f32(corners, size_z),) * 2)(x_odd, x_even)
    corner_even = swap_even(even, "gy")
    corner_odd = swap_odd(odd, "gy")

    wide = size_y + 2 * RIM

    def room(extra):
        return pltpu.VMEM((size_x + extra, wide, size_z), jnp.float32)

    energy = call(energy_part, f32(8, size_z), [room(2)])(x_odd, x_even, y_odd, y_even, own[0], own[1], own[4])
    mine, other = doubling(energy, y_bits[1:])
    face = f32(FILTER_SWEEPS, size_y, size_z)
    raw = call(
        adjoint_part,
        f32(*shape),
        [room(6), room(6), room(4), room(2), room(5), room(4), room(4), room(4), room(4), room(2)],
        cost=10000000,
    )(x_odd, x_even, y_odd, y_even, corner_odd, corner_even, *own)

    x_odd = swap_odd(call(pack_raw_x_odd, face)(raw), "gx")
    even, energy = call(pack_raw_x_even, (face, f32(8, size_z)))(raw, mine, other)
    x_even = swap_even(even, "gx")
    mine, other = doubling(energy, x_bits)
    _, rows = segments((FILTER_SWEEPS,), size_x)
    even, odd, energy = call(pack_raw_y, (f32(rows + 8, size_z), f32(rows, size_z), f32(8, size_z)))(
        x_odd, x_even, raw, mine, other)
    y_even = swap_even(even, "gy")
    y_odd = swap_odd(odd, "gy")
    energy = energy + y_even[rows:rows + 8]
    mine, other = doubling(energy, y_bits[:1] + [("gx", 1)])
    filtered = call(
        filter_part,
        f32(*shape),
        [room(2 * FILTER_SWEEPS)] * 3 + [pltpu.VMEM((3, wide, size_z), jnp.float32)],
        cost=10000000,
    )(x_odd, x_even, y_odd, y_even, raw, own[1])
    sensitivity, mean_energy = pl.pallas_call(
        rescale,
        out_shape=(f32(*shape), f32(1, 1)),
        out_specs=(pl.BlockSpec(memory_space=pltpu.VMEM), pl.BlockSpec(memory_space=pltpu.SMEM)),
        compiler_params=pltpu.CompilerParams(vmem_limit_bytes=VMEM_LIMIT),
    )(filtered, mine, other)
    return (sensitivity, mean_energy[0, 0])


def solution(mesh):
    spec = P("gx", "gy", None)
    return jax.shard_map(
        shards, mesh=mesh, in_specs=(spec,) * 5, out_specs=(spec, P()), check_vma=False
    )
```

```python
import functools

import jax
import jax.numpy as jnp
from jax import lax
from jax.experimental import pallas as pl
from jax.experimental.pallas import tpu as pltpu
from jax.sharding import PartitionSpec as P

ADJ_SWEEPS = 2
FILTER_SWEEPS = 4

eps_void = 1.0
eps_solid = 12.0
eps_back = 4.0
eps_metal = 40.0
screen = 0.5
radius_sq = 2.0
epsilon_mean = 1e-06

WIDTHS = (ADJ_SWEEPS + 1, ADJ_SWEEPS + 1, ADJ_SWEEPS, 1)
RIM = 4
VMEM_LIMIT = 24 * 1024 * 1024


def segments(widths, size_x, beside=True, beyond=True):
    found, at = [], 0
    for field, width in enumerate(widths):
        for x in range(-width, size_x + width):
            rows = width - max(0, -x, x - size_x + 1)
            if rows > 0 and (beside if 0 <= x < size_x else beyond):
                found.append((field, x, rows, at))
                at += rows
    return found, -(-at // 8) * 8


def plane_starts(widths):
    starts, at = [], 0
    for width in widths:
        starts.append(at)
        at += width
    return starts, at


def material(density, labels):
    design = eps_void + density * density * density * (eps_solid - eps_void)
    return jnp.where(labels == 1, design, jnp.where(labels == 2, eps_metal, eps_back))


def call(body, outs, scratch=(), in_specs=None, cost=10000):
    kwargs = {} if in_specs is None else {"in_specs": in_specs, "grid": (1,)}
    return pl.pallas_call(
        body,
        out_shape=outs,
        scratch_shapes=list(scratch),
        compiler_params=pltpu.CompilerParams(vmem_limit_bytes=VMEM_LIMIT),
        cost_estimate=pl.CostEstimate(flops=cost, bytes_accessed=cost, transcendentals=0),
        **kwargs,
    )


def f32(*shape):
    return jax.ShapeDtypeStruct(shape, jnp.float32)


def odd_place(axis):
    return lax.rem(lax.axis_index(axis), 2) == 1


def pack_own(*refs):
    inputs, (x_odd_out, x_even_out, y_even_out, y_odd_out), held, sem = refs[:5], refs[5:9], refs[9:14], refs[14]
    density, labels, adjoint, source, potential = held
    size_x, size_y, _ = density.shape
    starts, _ = plane_starts(WIDTHS)
    copies = [pltpu.make_async_copy(a, b, sem.at[k]) for k, (a, b) in enumerate(zip(inputs, held))]
    for copy in copies:
        copy.start()
    copies[0].wait()
    low_first, y_swap = odd_place("gx"), odd_place("gy")
    found, _ = segments(WIDTHS, size_x, beyond=False)
    for field, width in enumerate(WIDTHS):
        copies[field + 1].wait()
        for out, low in ((x_even_out, low_first), (x_odd_out, jnp.logical_not(low_first))):
            span = pl.ds(jnp.where(low, 0, size_x - width), width)
            if field == 0:
                face = material(density[span], labels[span])
            else:
                face = (adjoint, source, potential)[field - 1][span]
            out[pl.ds(starts[field], width)] = face
        for _, x, rows, at in (part for part in found if part[0] == field):
            faces = []
            for rim in (slice(0, rows), slice(size_y - rows, size_y)):
                if field == 0:
                    faces.append(material(density[x, rim], labels[x, rim]))
                else:
                    faces.append((adjoint, source, potential)[field - 1][x, rim])
            low, high = faces
            y_even_out[at:at + rows] = jnp.where(y_swap, low, high)
            y_odd_out[at:at + rows] = jnp.where(y_swap, high, low)


def pack_corners(size_x, x_odd, x_even, even_out, odd_out):
    size_y = x_odd.shape[1]
    starts, _ = plane_starts(WIDTHS)
    x_swap, y_swap = odd_place("gx"), odd_place("gy")
    for field, x, rows, at in segments(WIDTHS, size_x, beside=False)[0]:
        faces = []
        for rim in (slice(0, rows), slice(size_y - rows, size_y)):
            if x < 0:
                plane = starts[field] + WIDTHS[field] + x
                face = jnp.where(x_swap, x_even[plane, rim], x_odd[plane, rim])
            else:
                plane = starts[field] + x - size_x
                face = jnp.where(x_swap, x_odd[plane, rim], x_even[plane, rim])
            faces.append(face)
        low, high = faces
        even_out[at:at + rows] = jnp.where(y_swap, low, high)
        odd_out[at:at + rows] = jnp.where(y_swap, high, low)


def shift(value, by, axis):
    return pltpu.roll(value, by % value.shape[axis], axis)


def planes_loop(low, high, block, step):
    count = high - low
    block = max(k for k in range(1, block + 1) if count % k == 0)

    def body(k, carry):
        step(low + k * block, block)
        return carry

    lax.fori_loop(0, count // block, body, 0)


def unpack_rows(fields, widths, found, even, odd, size_y):
    wide = size_y + 2 * RIM
    swap = odd_place("gy")
    for field, x, rows, at in found:
        if fields[field] is None:
            continue
        a, b = even[at:at + rows], odd[at:at + rows]
        fields[field][x + widths[field], wide - rows:wide] = jnp.where(swap, a, b)
        fields[field][x + widths[field], size_y:size_y + rows] = jnp.where(swap, b, a)


def unpack_planes(field, width, even, odd, size_x, size_y):
    swap = odd_place("gx")
    tile = pl.ds(0, size_y)
    field[pl.ds(0, width), tile] = jnp.where(swap, even, odd)
    field[pl.ds(width + size_x, width), tile] = jnp.where(swap, odd, even)


def energy_part(x_odd, x_even, y_odd, y_even, density, labels, potential, energy_out, poten):
    size_x, size_y, size_z = density.shape
    starts, planes = plane_starts(WIDTHS)
    planes_loop(0, size_x, 4, lambda x, n: poten.__setitem__((pl.ds(x + 1, n), pl.ds(0, size_y)), potential[pl.ds(x, n)]))
    span = pl.ds(starts[3], 1)
    unpack_planes(poten, 1, x_even[span], x_odd[span], size_x, size_y)
    found, _ = segments(WIDTHS, size_x, beyond=False)
    unpack_rows((None, None, None, poten), WIDTHS, found, y_even, y_odd, size_y)
    wide = size_y + 2 * RIM
    lane = lax.broadcasted_iota(jnp.int32, (1, wide, size_z), 2)
    is_first = lane == 0
    is_last = lane == size_z - 1
    energy_out[...] = jnp.zeros_like(energy_out)

    def step(x, n):
        span = pl.ds(x, n)
        v = poten[pl.ds(x + 1, n)]
        low, high = poten[pl.ds(x, n)] - v, poten[pl.ds(x + 2, n)] - v
        squares = low * low + high * high
        dv = shift(v, -1, 1) - v
        square = dv * dv
        squares = squares + square + shift(square, 1, 1)
        dv = jnp.where(is_last, 0.0, shift(v, -1, 2)) - v
        square = dv * dv
        squares = squares + square + jnp.where(is_first, v * v, shift(square, 1, 2))
        energy = material(density[span], labels[span]) * squares[:, :size_y]
        energy_out[...] += jnp.sum(energy.reshape(-1, 8, size_z), axis=0)

    planes_loop(0, size_x, 4, step)


def adjoint_part(x_odd, x_even, y_odd, y_even, corner_odd, corner_even, density, labels, adjoint_start, adjoint_source, potential,
                 raw_out,
                 permit, start, source, poten, face_x, face_y, face_z, inverse, first, second):
    size_x, size_y, size_z = density.shape
    starts, _ = plane_starts(WIDTHS)
    fields = (permit, start, source, poten)
    tile = pl.ds(0, size_y)

    def fill(x, n):
        span = pl.ds(x, n)
        permit[pl.ds(x + WIDTHS[0], n), tile] = material(density[span], labels[span])
        start[pl.ds(x + WIDTHS[1], n), tile] = adjoint_start[span]
        source[pl.ds(x + WIDTHS[2], n), tile] = adjoint_source[span]
        poten[pl.ds(x + WIDTHS[3], n), tile] = potential[span]

    planes_loop(0, size_x, 4, fill)
    for field, width in enumerate(WIDTHS):
        span = pl.ds(starts[field], width)
        unpack_planes(fields[field], width, x_even[span], x_odd[span], size_x, size_y)
    unpack_rows(fields, WIDTHS, segments(WIDTHS, size_x, beyond=False)[0], y_even, y_odd, size_y)
    unpack_rows(fields, WIDTHS, segments(WIDTHS, size_x, beside=False)[0], corner_even, corner_odd, size_y)

    wide = size_y + 2 * RIM
    lane = lax.broadcasted_iota(jnp.int32, (1, wide, size_z), 2)
    is_first = lane == 0
    is_last = lane == size_z - 1

    def inverted(d):
        first_guess = pl.reciprocal(d, approx=True)
        return first_guess * (2.0 - d * first_guess)

    def harmonic(a, b):
        return 2.0 * a * b * inverted(jnp.maximum(a + b, 0.25))

    def faces_x(x, n):
        face_x[pl.ds(x, n)] = harmonic(permit[pl.ds(x, n)], permit[pl.ds(x + 1, n)])

    planes_loop(0, size_x + 5, 21, faces_x)

    def weigh(x, n):
        span = pl.ds(x, n)
        p = permit[pl.ds(x + 1, n)]
        fy = harmonic(p, shift(p, -1, 1))
        fz = jnp.where(is_last, 0.0, harmonic(p, shift(p, -1, 2)))
        face_y[span] = fy
        face_z[span] = fz
        total = screen + face_x[span] + face_x[pl.ds(x + 1, n)] + fy + shift(fy, 1, 1) + fz + shift(fz, 1, 2)
        inverse[span] = jnp.where(p > 20.0, 0.0, inverted(total))

    planes_loop(0, size_x + 4, 20, weigh)

    def relax(x, n, a, a_low, a_high):
        span = pl.ds(x, n)
        fy, fz = face_y[span], face_z[span]
        total = source[span] + face_x[pl.ds(x + 1, n)] * a_high + face_x[span] * a_low
        total = total + fy * shift(a, -1, 1) + shift(fy * a, 1, 1)
        total = total + fz * shift(a, -1, 2) + shift(fz * a, 1, 2)
        return total * inverse[span]

    def sweep_one(x, n):
        first[pl.ds(x, n)] = relax(x, n, start[pl.ds(x + 1, n)], start[pl.ds(x, n)], start[pl.ds(x + 2, n)])

    planes_loop(0, size_x + 4, 20, sweep_one)

    def sweep_two(x, n):
        second[pl.ds(x, n)] = relax(x + 1, n, first[pl.ds(x + 1, n)], first[pl.ds(x, n)], first[pl.ds(x + 2, n)])

    planes_loop(0, size_x + 2, 18, sweep_two)

    def finish(x, n):
        span = pl.ds(x, n)
        v, a = poten[pl.ds(x + 1, n)], second[pl.ds(x + 1, n)]
        product = (poten[pl.ds(x, n)] - v) * (second[pl.ds(x, n)] - a)
        product = product + (poten[pl.ds(x + 2, n)] - v) * (second[pl.ds(x + 2, n)] - a)
        both = (shift(v, -1, 1) - v) * (shift(a, -1, 1) - a)
        product = product + both + shift(both, 1, 1)
        both = (jnp.where(is_last, 0.0, shift(v, -1, 2)) - v) * (jnp.where(is_last, 0.0, shift(a, -1, 2)) - a)
        product = product + both + jnp.where(is_first, v * a, shift(both, 1, 2))
        d = density[span]
        gain = jnp.where(labels[span] == 1, -1.5 * (eps_solid - eps_void) * d * d, 0.0)
        raw_out[span] = gain * product[:, :size_y]

    planes_loop(0, size_x, 16, finish)


def pack_raw_x(raw, out, low):
    out[...] = raw[pl.ds(jnp.where(low, 0, raw.shape[0] - FILTER_SWEEPS), FILTER_SWEEPS)]


def pack_raw_x_odd(raw, out):
    pack_raw_x(raw, out, jnp.logical_not(odd_place("gx")))


def pack_raw_x_even(raw, mine, other, out, energy_out):
    energy_out[...] = mine[...] + other[...]
    pack_raw_x(raw, out, odd_place("gx"))


def pack_raw_y(x_odd, x_even, raw, mine, other, even_out, odd_out, energy_out):
    size_x, size_y, _ = raw.shape
    width = FILTER_SWEEPS
    found, total = segments((width,), size_x)
    x_swap, y_swap = odd_place("gx"), odd_place("gy")
    energy = mine[...] + other[...]
    energy_out[...] = energy
    even_out[total:total + 8] = energy
    for _, x, rows, at in found:
        faces = []
        for rim in (slice(0, rows), slice(size_y - rows, size_y)):
            if x < 0:
                face = jnp.where(x_swap, x_even[width + x, rim], x_odd[width + x, rim])
            elif x >= size_x:
                face = jnp.where(x_swap, x_odd[x - size_x, rim], x_even[x - size_x, rim])
            else:
                face = raw[x, rim]
            faces.append(face)
        low, high = faces
        even_out[at:at + rows] = jnp.where(y_swap, low, high)
        odd_out[at:at + rows] = jnp.where(y_swap, high, low)


def relaxation(raw, size_x, size_y, size_z):
    width = FILTER_SWEEPS
    wide = size_y + 2 * RIM
    extent_x = lax.axis_size("gx") * size_x
    extent_y = lax.axis_size("gy") * size_y
    base_x = lax.axis_index("gx") * size_x - width
    lane = lax.broadcasted_iota(jnp.int32, (1, wide, size_z), 2)
    row = lax.broadcasted_iota(jnp.int32, (1, wide, size_z), 1)
    place = lax.axis_index("gy") * size_y + jnp.where(row < size_y + RIM, row, row - wide)
    is_first, is_last = lane == 0, lane == size_z - 1

    def edges(at, extent):
        return jnp.where(at > 0, 1.0, 0.0) + jnp.where(at < extent - 1, 1.0, 0.0)

    count = edges(place, extent_y) + edges(lane, size_z)
    inside = (place >= 0) & (place < extent_y)
    scale_two = jnp.where(inside, 1.0 / (1.0 + radius_sq * (count + 2.0)), 0.0)
    scale_one = jnp.where(inside, 1.0 / (1.0 + radius_sq * (count + 1.0)), 0.0)

    def relax(src, x, n):
        f = src[pl.ds(x, n)]
        near = src[pl.ds(x - 1, n)] + src[pl.ds(x + 1, n)] + shift(f, 1, 1) + shift(f, -1, 1)
        near = near + jnp.where(is_first, 0.0, shift(f, 1, 2)) + jnp.where(is_last, 0.0, shift(f, -1, 2))
        total = raw[pl.ds(x, n)] + radius_sq * near
        scaled = []
        for k in range(n):
            at = base_x + x + k
            outside = (at < 0) | (at >= extent_x)
            border = (at == 0) | (at == extent_x - 1)
            scale = jnp.where(outside, 0.0, jnp.where(border, scale_one, scale_two))
            scaled.append(total[k:k + 1] * scale)
        return jnp.concatenate(scaled, axis=0)

    return relax


def filter_part(x_odd, x_even, y_odd, y_even, raw_in, labels, out, raw, odd, even):
    size_x, size_y, size_z = raw_in.shape
    width = FILTER_SWEEPS
    tile = pl.ds(0, size_y)

    def fill(x, n):
        raw[pl.ds(x + width, n), tile] = raw_in[pl.ds(x, n)]

    planes_loop(0, size_x, 4, fill)
    unpack_planes(raw, width, x_even[...], x_odd[...], size_x, size_y)
    unpack_rows((raw,), (width,), segments((width,), size_x)[0], y_even, y_odd, size_y)
    relax = relaxation(raw, size_x, size_y, size_z)
    src = raw
    for sweep in range(FILTER_SWEEPS - 1):
        dst = (odd, even)[sweep % 2]

        def step(x, n, src=src, dst=dst):
            dst[pl.ds(x, n)] = relax(src, x, n)

        planes_loop(sweep + 1, size_x + 2 * width - sweep - 1, 22, step)
        src = dst

    def last(x, n):
        f = relax(src, x + width, n)[:, :size_y]
        out[pl.ds(x, n)] = jnp.where(labels[pl.ds(x, n)] == 1, f, 0.0)

    planes_loop(0, size_x, 16, last)


def rescale(filtered, mine, other, out, mean_out):
    size_x, size_y, size_z = filtered.shape
    voxels = lax.axis_size("gx") * size_x * lax.axis_size("gy") * size_y * size_z
    mean = 0.5 * jnp.sum(mine[...] + other[...]) / voxels + epsilon_mean
    mean_out[0, 0] = mean
    out[...] = filtered[...] * (1.0 / jnp.full((1, 1, size_z), mean, jnp.float32))


def swap_even(value, axis):
    return lax.ppermute(value, axis, [(i, i ^ 1) for i in range(lax.axis_size(axis))])


def swap_odd(value, axis):
    count = lax.axis_size(axis)
    up = [(i, i + 1) for i in range(1, count - 1, 2)]
    return lax.ppermute(value, axis, up + [(b, a) for a, b in up])


def partner(value, axis, bit):
    return lax.ppermute(value, axis, [(i, i ^ bit) for i in range(lax.axis_size(axis))])


def doubling(energy, stages):
    other = partner(energy, *stages[0])
    for stage in stages[1:]:
        energy = energy + other
        other = partner(energy, *stage)
    return energy, other


def shards(density, potential, adjoint_start, adjoint_source, labels):
    size_x, size_y, size_z = potential.shape
    _, planes = plane_starts(WIDTHS)
    _, rows = segments(WIDTHS, size_x, beyond=False)
    _, corners = segments(WIDTHS, size_x, beside=False)
    own = [
        pltpu.with_memory_space_constraint(array, pltpu.HBM)
        for array in (density, labels, adjoint_start, adjoint_source, potential)
    ]
    x_bits = [("gx", 1 << k) for k in range(1, (lax.axis_size("gx") - 1).bit_length())]
    y_bits = [("gy", 1 << k) for k in range(1, (lax.axis_size("gy") - 1).bit_length())]

    shape = (size_x, size_y, size_z)
    odd, even, tile_even, tile_odd, *own = pl.pallas_call(
        pack_own,
        out_shape=(f32(planes, size_y, size_z),) * 2 + (f32(rows, size_z),) * 2
        + (f32(*shape), jax.ShapeDtypeStruct(shape, jnp.int32)) + (f32(*shape),) * 3,
        in_specs=[pl.BlockSpec(memory_space=pltpu.HBM)] * 5,
        scratch_shapes=[pltpu.SemaphoreType.DMA((5,))],
        compiler_params=pltpu.CompilerParams(vmem_limit_bytes=VMEM_LIMIT),
    )(*own)
    x_even = swap_even(even, "gx")
    x_odd = swap_odd(odd, "gx")
    y_even = swap_even(tile_even, "gy")
    y_odd = swap_odd(tile_odd, "gy")
    even, odd = call(functools.partial(pack_corners, size_x), (f32(corners, size_z),) * 2)(x_odd, x_even)
    corner_even = swap_even(even, "gy")
    corner_odd = swap_odd(odd, "gy")

    wide = size_y + 2 * RIM

    def room(extra):
        return pltpu.VMEM((size_x + extra, wide, size_z), jnp.float32)

    energy = call(energy_part, f32(8, size_z), [room(2)])(x_odd, x_even, y_odd, y_even, own[0], own[1], own[4])
    mine, other = doubling(energy, y_bits[1:])
    face = f32(FILTER_SWEEPS, size_y, size_z)
    raw = call(
        adjoint_part,
        f32(*shape),
        [room(6), room(6), room(4), room(2), room(5), room(4), room(4), room(4), room(4), room(2)],
        cost=10000000,
    )(x_odd, x_even, y_odd, y_even, corner_odd, corner_even, *own)

    x_odd = swap_odd(call(pack_raw_x_odd, face)(raw), "gx")
    even, energy = call(pack_raw_x_even, (face, f32(8, size_z)))(raw, mine, other)
    x_even = swap_even(even, "gx")
    mine, other = doubling(energy, x_bits)
    _, rows = segments((FILTER_SWEEPS,), size_x)
    even, odd, energy = call(pack_raw_y, (f32(rows + 8, size_z), f32(rows, size_z), f32(8, size_z)))(
        x_odd, x_even, raw, mine, other)
    y_even = swap_even(even, "gy")
    y_odd = swap_odd(odd, "gy")
    energy = energy + y_even[rows:rows + 8]
    mine, other = doubling(energy, y_bits[:1] + [("gx", 1)])
    filtered = call(
        filter_part,
        f32(*shape),
        [room(2 * FILTER_SWEEPS)] * 3,
        cost=10000000,
    )(x_odd, x_even, y_odd, y_even, raw, own[1])
    sensitivity, mean_energy = pl.pallas_call(
        rescale,
        out_shape=(f32(*shape), f32(1, 1)),
        out_specs=(pl.BlockSpec(memory_space=pltpu.VMEM), pl.BlockSpec(memory_space=pltpu.SMEM)),
        compiler_params=pltpu.CompilerParams(vmem_limit_bytes=VMEM_LIMIT),
    )(filtered, mine, other)
    return (sensitivity, mean_energy[0, 0])


def solution(mesh):
    spec = P("gx", "gy", None)
    return jax.shard_map(
        shards, mesh=mesh, in_specs=(spec,) * 5, out_specs=(spec, P()), check_vma=False
    )
```

```python
import functools

import jax
import jax.numpy as jnp
from jax import lax
from jax.experimental import pallas as pl
from jax.experimental.pallas import tpu as pltpu
from jax.sharding import PartitionSpec as P

ADJ_SWEEPS = 2
FILTER_SWEEPS = 4

eps_void = 1.0
eps_solid = 12.0
eps_back = 4.0
eps_metal = 40.0
screen = 0.5
radius_sq = 2.0
epsilon_mean = 1e-06

WIDTHS = (ADJ_SWEEPS + 1, ADJ_SWEEPS + 1, ADJ_SWEEPS, 1)
RIM = 4
VMEM_LIMIT = 24 * 1024 * 1024


def segments(widths, size_x, beside=True, beyond=True):
    found, at = [], 0
    for field, width in enumerate(widths):
        for x in range(-width, size_x + width):
            rows = width - max(0, -x, x - size_x + 1)
            if rows > 0 and (beside if 0 <= x < size_x else beyond):
                found.append((field, x, rows, at))
                at += rows
    return found, -(-at // 8) * 8


def plane_starts(widths):
    starts, at = [], 0
    for width in widths:
        starts.append(at)
        at += width
    return starts, at


def material(density, labels):
    design = eps_void + density * density * density * (eps_solid - eps_void)
    return jnp.where(labels == 1, design, jnp.where(labels == 2, eps_metal, eps_back))


def call(body, outs, scratch=(), in_specs=None, cost=10000):
    kwargs = {} if in_specs is None else {"in_specs": in_specs, "grid": (1,)}
    return pl.pallas_call(
        body,
        out_shape=outs,
        scratch_shapes=list(scratch),
        compiler_params=pltpu.CompilerParams(vmem_limit_bytes=VMEM_LIMIT),
        cost_estimate=pl.CostEstimate(flops=cost, bytes_accessed=cost, transcendentals=0),
        **kwargs,
    )


def f32(*shape):
    return jax.ShapeDtypeStruct(shape, jnp.float32)


def odd_place(axis):
    return lax.rem(lax.axis_index(axis), 2) == 1


def pack_own(*refs):
    inputs, (x_odd_out, x_even_out, y_even_out, y_odd_out), held, sem = refs[:5], refs[5:9], refs[9:14], refs[14]
    density, labels, adjoint, source, potential = held
    size_x, size_y, _ = density.shape
    starts, _ = plane_starts(WIDTHS)
    copies = [pltpu.make_async_copy(a, b, sem.at[k]) for k, (a, b) in enumerate(zip(inputs, held))]
    for copy in copies:
        copy.start()
    copies[0].wait()
    low_first, y_swap = odd_place("gx"), odd_place("gy")
    found, _ = segments(WIDTHS, size_x, beyond=False)
    for field, width in enumerate(WIDTHS):
        copies[field + 1].wait()
        for out, low in ((x_even_out, low_first), (x_odd_out, jnp.logical_not(low_first))):
            span = pl.ds(jnp.where(low, 0, size_x - width), width)
            if field == 0:
                face = material(density[span], labels[span])
            else:
                face = (adjoint, source, potential)[field - 1][span]
            out[pl.ds(starts[field], width)] = face
        for _, x, rows, at in (part for part in found if part[0] == field):
            faces = []
            for rim in (slice(0, rows), slice(size_y - rows, size_y)):
                if field == 0:
                    faces.append(material(density[x, rim], labels[x, rim]))
                else:
                    faces.append((adjoint, source, potential)[field - 1][x, rim])
            low, high = faces
            y_even_out[at:at + rows] = jnp.where(y_swap, low, high)
            y_odd_out[at:at + rows] = jnp.where(y_swap, high, low)


def pack_corners(size_x, x_odd, x_even, even_out, odd_out):
    size_y = x_odd.shape[1]
    starts, _ = plane_starts(WIDTHS)
    x_swap, y_swap = odd_place("gx"), odd_place("gy")
    for field, x, rows, at in segments(WIDTHS, size_x, beside=False)[0]:
        faces = []
        for rim in (slice(0, rows), slice(size_y - rows, size_y)):
            if x < 0:
                plane = starts[field] + WIDTHS[field] + x
                face = jnp.where(x_swap, x_even[plane, rim], x_odd[plane, rim])
            else:
                plane = starts[field] + x - size_x
                face = jnp.where(x_swap, x_odd[plane, rim], x_even[plane, rim])
            faces.append(face)
        low, high = faces
        even_out[at:at + rows] = jnp.where(y_swap, low, high)
        odd_out[at:at + rows] = jnp.where(y_swap, high, low)


def shift(value, by, axis):
    return pltpu.roll(value, by % value.shape[axis], axis)


def planes_loop(low, high, block, step):
    count = high - low
    block = max(k for k in range(1, block + 1) if count % k == 0)

    def body(k, carry):
        step(low + k * block, block)
        return carry

    lax.fori_loop(0, count // block, body, 0)


def unpack_rows(fields, widths, found, even, odd, size_y):
    wide = size_y + 2 * RIM
    swap = odd_place("gy")
    for field, x, rows, at in found:
        if fields[field] is None:
            continue
        a, b = even[at:at + rows], odd[at:at + rows]
        fields[field][x + widths[field], wide - rows:wide] = jnp.where(swap, a, b)
        fields[field][x + widths[field], size_y:size_y + rows] = jnp.where(swap, b, a)


def unpack_planes(field, width, even, odd, size_x, size_y):
    swap = odd_place("gx")
    tile = pl.ds(0, size_y)
    field[pl.ds(0, width), tile] = jnp.where(swap, even, odd)
    field[pl.ds(width + size_x, width), tile] = jnp.where(swap, odd, even)


def energy_part(x_odd, x_even, y_odd, y_even, density, labels, potential, energy_out, poten):
    size_x, size_y, size_z = density.shape
    starts, planes = plane_starts(WIDTHS)
    planes_loop(0, size_x, 16, lambda x, n: poten.__setitem__((pl.ds(x + 1, n), pl.ds(0, size_y)), potential[pl.ds(x, n)]))
    span = pl.ds(starts[3], 1)
    unpack_planes(poten, 1, x_even[span], x_odd[span], size_x, size_y)
    found, _ = segments(WIDTHS, size_x, beyond=False)
    unpack_rows((None, None, None, poten), WIDTHS, found, y_even, y_odd, size_y)
    wide = size_y + 2 * RIM
    lane = lax.broadcasted_iota(jnp.int32, (1, wide, size_z), 2)
    is_first = lane == 0
    is_last = lane == size_z - 1
    energy_out[...] = jnp.zeros_like(energy_out)

    def step(x, n):
        span = pl.ds(x, n)
        v = poten[pl.ds(x + 1, n)]
        low, high = poten[pl.ds(x, n)] - v, poten[pl.ds(x + 2, n)] - v
        squares = low * low + high * high
        dv = shift(v, -1, 1) - v
        square = dv * dv
        squares = squares + square + shift(square, 1, 1)
        dv = jnp.where(is_last, 0.0, shift(v, -1, 2)) - v
        square = dv * dv
        squares = squares + square + jnp.where(is_first, v * v, shift(square, 1, 2))
        energy = material(density[span], labels[span]) * squares[:, :size_y]
        energy_out[...] += jnp.sum(energy.reshape(-1, 8, size_z), axis=0)

    planes_loop(0, size_x, 16, step)


def adjoint_part(x_odd, x_even, y_odd, y_even, corner_odd, corner_even, density, labels, adjoint_start, adjoint_source, potential,
                 raw_out,
                 permit, start, source, poten, face_x, face_y, face_z, inverse, first, second):
    size_x, size_y, size_z = density.shape
    starts, _ = plane_starts(WIDTHS)
    fields = (permit, start, source, poten)
    tile = pl.ds(0, size_y)

    def fill(x, n):
        span = pl.ds(x, n)
        permit[pl.ds(x + WIDTHS[0], n), tile] = material(density[span], labels[span])
        start[pl.ds(x + WIDTHS[1], n), tile] = adjoint_start[span]
        source[pl.ds(x + WIDTHS[2], n), tile] = adjoint_source[span]
        poten[pl.ds(x + WIDTHS[3], n), tile] = potential[span]

    planes_loop(0, size_x, 16, fill)
    for field, width in enumerate(WIDTHS):
        span = pl.ds(starts[field], width)
        unpack_planes(fields[field], width, x_even[span], x_odd[span], size_x, size_y)
    unpack_rows(fields, WIDTHS, segments(WIDTHS, size_x, beyond=False)[0], y_even, y_odd, size_y)
    unpack_rows(fields, WIDTHS, segments(WIDTHS, size_x, beside=False)[0], corner_even, corner_odd, size_y)

    wide = size_y + 2 * RIM
    lane = lax.broadcasted_iota(jnp.int32, (1, wide, size_z), 2)
    is_first = lane == 0
    is_last = lane == size_z - 1

    def inverted(d):
        first_guess = pl.reciprocal(d, approx=True)
        return first_guess * (2.0 - d * first_guess)

    def harmonic(a, b):
        return 2.0 * a * b * inverted(jnp.maximum(a + b, 0.25))

    def faces_x(x, n):
        face_x[pl.ds(x, n)] = harmonic(permit[pl.ds(x, n)], permit[pl.ds(x + 1, n)])

    planes_loop(0, size_x + 5, 21, faces_x)

    def weigh(x, n):
        span = pl.ds(x, n)
        p = permit[pl.ds(x + 1, n)]
        fy = harmonic(p, shift(p, -1, 1))
        fz = jnp.where(is_last, 0.0, harmonic(p, shift(p, -1, 2)))
        face_y[span] = fy
        face_z[span] = fz
        total = screen + face_x[span] + face_x[pl.ds(x + 1, n)] + fy + shift(fy, 1, 1) + fz + shift(fz, 1, 2)
        inverse[span] = jnp.where(p > 20.0, 0.0, inverted(total))

    planes_loop(0, size_x + 4, 20, weigh)

    def relax(x, n, a, a_low, a_high):
        span = pl.ds(x, n)
        fy, fz = face_y[span], face_z[span]
        total = source[span] + face_x[pl.ds(x + 1, n)] * a_high + face_x[span] * a_low
        total = total + fy * shift(a, -1, 1) + shift(fy * a, 1, 1)
        total = total + fz * shift(a, -1, 2) + shift(fz * a, 1, 2)
        return total * inverse[span]

    def sweep_one(x, n):
        first[pl.ds(x, n)] = relax(x, n, start[pl.ds(x + 1, n)], start[pl.ds(x, n)], start[pl.ds(x + 2, n)])

    planes_loop(0, size_x + 4, 20, sweep_one)

    def sweep_two(x, n):
        second[pl.ds(x, n)] = relax(x + 1, n, first[pl.ds(x + 1, n)], first[pl.ds(x, n)], first[pl.ds(x + 2, n)])

    planes_loop(0, size_x + 2, 18, sweep_two)

    def finish(x, n):
        span = pl.ds(x, n)
        v, a = poten[pl.ds(x + 1, n)], second[pl.ds(x + 1, n)]
        product = (poten[pl.ds(x, n)] - v) * (second[pl.ds(x, n)] - a)
        product = product + (poten[pl.ds(x + 2, n)] - v) * (second[pl.ds(x + 2, n)] - a)
        both = (shift(v, -1, 1) - v) * (shift(a, -1, 1) - a)
        product = product + both + shift(both, 1, 1)
        both = (jnp.where(is_last, 0.0, shift(v, -1, 2)) - v) * (jnp.where(is_last, 0.0, shift(a, -1, 2)) - a)
        product = product + both + jnp.where(is_first, v * a, shift(both, 1, 2))
        d = density[span]
        gain = jnp.where(labels[span] == 1, -1.5 * (eps_solid - eps_void) * d * d, 0.0)
        raw_out[span] = gain * product[:, :size_y]

    planes_loop(0, size_x, 16, finish)


def pack_raw_x(raw, out, low):
    out[...] = raw[pl.ds(jnp.where(low, 0, raw.shape[0] - FILTER_SWEEPS), FILTER_SWEEPS)]


def pack_raw_x_odd(raw, out):
    pack_raw_x(raw, out, jnp.logical_not(odd_place("gx")))


def pack_raw_x_even(raw, mine, other, out, energy_out):
    energy_out[...] = mine[...] + other[...]
    pack_raw_x(raw, out, odd_place("gx"))


def pack_raw_y(x_odd, x_even, raw, mine, other, even_out, odd_out, energy_out):
    size_x, size_y, _ = raw.shape
    width = FILTER_SWEEPS
    found, total = segments((width,), size_x)
    x_swap, y_swap = odd_place("gx"), odd_place("gy")
    energy = mine[...] + other[...]
    energy_out[...] = energy
    even_out[total:total + 8] = energy
    for _, x, rows, at in found:
        faces = []
        for rim in (slice(0, rows), slice(size_y - rows, size_y)):
            if x < 0:
                face = jnp.where(x_swap, x_even[width + x, rim], x_odd[width + x, rim])
            elif x >= size_x:
                face = jnp.where(x_swap, x_odd[x - size_x, rim], x_even[x - size_x, rim])
            else:
                face = raw[x, rim]
            faces.append(face)
        low, high = faces
        even_out[at:at + rows] = jnp.where(y_swap, low, high)
        odd_out[at:at + rows] = jnp.where(y_swap, high, low)


def relaxation(raw, size_x, size_y, size_z):
    width = FILTER_SWEEPS
    wide = size_y + 2 * RIM
    extent_x = lax.axis_size("gx") * size_x
    extent_y = lax.axis_size("gy") * size_y
    base_x = lax.axis_index("gx") * size_x - width
    lane = lax.broadcasted_iota(jnp.int32, (1, wide, size_z), 2)
    row = lax.broadcasted_iota(jnp.int32, (1, wide, size_z), 1)
    place = lax.axis_index("gy") * size_y + jnp.where(row < size_y + RIM, row, row - wide)
    is_first, is_last = lane == 0, lane == size_z - 1

    def edges(at, extent):
        return jnp.where(at > 0, 1.0, 0.0) + jnp.where(at < extent - 1, 1.0, 0.0)

    count = edges(place, extent_y) + edges(lane, size_z)
    inside = (place >= 0) & (place < extent_y)
    scale_two = jnp.where(inside, 1.0 / (1.0 + radius_sq * (count + 2.0)), 0.0)
    scale_one = jnp.where(inside, 1.0 / (1.0 + radius_sq * (count + 1.0)), 0.0)

    def relax(src, x, n):
        f = src[pl.ds(x, n)]
        near = src[pl.ds(x - 1, n)] + src[pl.ds(x + 1, n)] + shift(f, 1, 1) + shift(f, -1, 1)
        near = near + jnp.where(is_first, 0.0, shift(f, 1, 2)) + jnp.where(is_last, 0.0, shift(f, -1, 2))
        total = raw[pl.ds(x, n)] + radius_sq * near
        scaled = []
        for k in range(n):
            at = base_x + x + k
            outside = (at < 0) | (at >= extent_x)
            border = (at == 0) | (at == extent_x - 1)
            scale = jnp.where(outside, 0.0, jnp.where(border, scale_one, scale_two))
            scaled.append(total[k:k + 1] * scale)
        return jnp.concatenate(scaled, axis=0)

    return relax


def filter_part(x_odd, x_even, y_odd, y_even, raw_in, labels, out, raw, odd, even):
    size_x, size_y, size_z = raw_in.shape
    width = FILTER_SWEEPS
    tile = pl.ds(0, size_y)

    def fill(x, n):
        raw[pl.ds(x + width, n), tile] = raw_in[pl.ds(x, n)]

    planes_loop(0, size_x, 16, fill)
    unpack_planes(raw, width, x_even[...], x_odd[...], size_x, size_y)
    unpack_rows((raw,), (width,), segments((width,), size_x)[0], y_even, y_odd, size_y)
    relax = relaxation(raw, size_x, size_y, size_z)
    src = raw
    for sweep in range(FILTER_SWEEPS - 1):
        dst = (odd, even)[sweep % 2]

        def step(x, n, src=src, dst=dst):
            dst[pl.ds(x, n)] = relax(src, x, n)

        planes_loop(sweep + 1, size_x + 2 * width - sweep - 1, 22, step)
        src = dst

    def last(x, n):
        f = relax(src, x + width, n)[:, :size_y]
        out[pl.ds(x, n)] = jnp.where(labels[pl.ds(x, n)] == 1, f, 0.0)

    planes_loop(0, size_x, 16, last)


def rescale(filtered, mine, other, out, mean_out):
    size_x, size_y, size_z = filtered.shape
    voxels = lax.axis_size("gx") * size_x * lax.axis_size("gy") * size_y * size_z
    mean = 0.5 * jnp.sum(mine[...] + other[...]) / voxels + epsilon_mean
    mean_out[0, 0] = mean
    out[...] = filtered[...] * (1.0 / jnp.full((1, 1, size_z), mean, jnp.float32))


def swap_even(value, axis):
    return lax.ppermute(value, axis, [(i, i ^ 1) for i in range(lax.axis_size(axis))])


def swap_odd(value, axis):
    count = lax.axis_size(axis)
    up = [(i, i + 1) for i in range(1, count - 1, 2)]
    return lax.ppermute(value, axis, up + [(b, a) for a, b in up])


def partner(value, axis, bit):
    return lax.ppermute(value, axis, [(i, i ^ bit) for i in range(lax.axis_size(axis))])


def doubling(energy, stages):
    other = partner(energy, *stages[0])
    for stage in stages[1:]:
        energy = energy + other
        other = partner(energy, *stage)
    return energy, other


def shards(density, potential, adjoint_start, adjoint_source, labels):
    size_x, size_y, size_z = potential.shape
    _, planes = plane_starts(WIDTHS)
    _, rows = segments(WIDTHS, size_x, beyond=False)
    _, corners = segments(WIDTHS, size_x, beside=False)
    own = [
        pltpu.with_memory_space_constraint(array, pltpu.HBM)
        for array in (density, labels, adjoint_start, adjoint_source, potential)
    ]
    x_bits = [("gx", 1 << k) for k in range(1, (lax.axis_size("gx") - 1).bit_length())]
    y_bits = [("gy", 1 << k) for k in range(1, (lax.axis_size("gy") - 1).bit_length())]

    shape = (size_x, size_y, size_z)
    odd, even, tile_even, tile_odd, *own = pl.pallas_call(
        pack_own,
        out_shape=(f32(planes, size_y, size_z),) * 2 + (f32(rows, size_z),) * 2
        + (f32(*shape), jax.ShapeDtypeStruct(shape, jnp.int32)) + (f32(*shape),) * 3,
        in_specs=[pl.BlockSpec(memory_space=pltpu.HBM)] * 5,
        scratch_shapes=[pltpu.SemaphoreType.DMA((5,))],
        compiler_params=pltpu.CompilerParams(vmem_limit_bytes=VMEM_LIMIT),
    )(*own)
    x_even = swap_even(even, "gx")
    x_odd = swap_odd(odd, "gx")
    y_even = swap_even(tile_even, "gy")
    y_odd = swap_odd(tile_odd, "gy")
    even, odd = call(functools.partial(pack_corners, size_x), (f32(corners, size_z),) * 2)(x_odd, x_even)
    corner_even = swap_even(even, "gy")
    corner_odd = swap_odd(odd, "gy")

    wide = size_y + 2 * RIM

    def room(extra):
        return pltpu.VMEM((size_x + extra, wide, size_z), jnp.float32)

    energy = call(energy_part, f32(8, size_z), [room(2)])(x_odd, x_even, y_odd, y_even, own[0], own[1], own[4])
    mine, other = doubling(energy, y_bits[1:])
    face = f32(FILTER_SWEEPS, size_y, size_z)
    raw = call(
        adjoint_part,
        f32(*shape),
        [room(6), room(6), room(4), room(2), room(5), room(4), room(4), room(4), room(4), room(2)],
        cost=10000000,
    )(x_odd, x_even, y_odd, y_even, corner_odd, corner_even, *own)

    x_odd = swap_odd(call(pack_raw_x_odd, face)(raw), "gx")
    even, energy = call(pack_raw_x_even, (face, f32(8, size_z)))(raw, mine, other)
    x_even = swap_even(even, "gx")
    mine, other = doubling(energy, x_bits)
    _, rows = segments((FILTER_SWEEPS,), size_x)
    even, odd, energy = call(pack_raw_y, (f32(rows + 8, size_z), f32(rows, size_z), f32(8, size_z)))(
        x_odd, x_even, raw, mine, other)
    y_even = swap_even(even, "gy")
    y_odd = swap_odd(odd, "gy")
    energy = energy + y_even[rows:rows + 8]
    mine, other = doubling(energy, y_bits[:1] + [("gx", 1)])
    filtered = call(
        filter_part,
        f32(*shape),
        [room(2 * FILTER_SWEEPS)] * 3,
        cost=10000000,
    )(x_odd, x_even, y_odd, y_even, raw, own[1])
    sensitivity, mean_energy = pl.pallas_call(
        rescale,
        out_shape=(f32(*shape), f32(1, 1)),
        out_specs=(pl.BlockSpec(memory_space=pltpu.VMEM), pl.BlockSpec(memory_space=pltpu.SMEM)),
        compiler_params=pltpu.CompilerParams(vmem_limit_bytes=VMEM_LIMIT),
    )(filtered, mine, other)
    return (sensitivity, mean_energy[0, 0])


def solution(mesh):
    spec = P("gx", "gy", None)
    return jax.shard_map(
        shards, mesh=mesh, in_specs=(spec,) * 5, out_specs=(spec, P()), check_vma=False
    )
```
